512 devices in a mesh: py: 16 (over x_hi, z), pz: 32 (over y, x_lo, core).
Axes of the slice: x: 4 (x_hi: 2, x_lo: 2; x = x_hi * 2 + x_lo), y: 8, z: 8, core: 2. Of those that a mesh axis runs over, the one named last changes fastest.
Arguments:
- features: bfloat16 [32, 256, 256, 256], P(None, 'py', 'pz'), may hold values from -6 to 6
- spectral_weight: bfloat16 [2, 64, 32, 48, 1024], P(None, 'py', 'pz'), may hold values from -4 to 4
- bypass_weight: bfloat16 [32, 32], replicated, may hold values from -1 to 1
- bias_vector: float32 [32], replicated, may hold values from -3 to 3
Outputs:
- layer_output: bfloat16 [32, 256, 256, 256], P(None, 'py', 'pz')
The draws below stay inside these ranges and needn't reach their ends.
All inputs are finite; a program needn't handle non-finite values.
Results may differ from the reference program's by a relative error of at most 0.001.
Values sent between devices are 32-bit elements; how exact they have to be, the bound alone decides.
A program may use at most 128 MiB of HBM per device.

```python
import math
import jax
import jax.numpy as jnp
from jax import lax

C = 32
NX = 256
NY = 256
NZ = 256
MX = 64
MY = 32
MZ = 48


def level_of(rng, extent, cuts, smallest, largest):
    def one(dim, blocks):
        draws = jax.random.uniform(jax.random.fold_in(jax.random.fold_in(rng, 6), dim), (blocks,), jnp.float32, smallest / len(cuts), largest / len(cuts))
        return jnp.repeat(jnp.exp(draws), extent[dim] // blocks).reshape((-1,) + (1,) * (len(extent) - dim - 1))

    loudness = one(*cuts[0])
    for cut in cuts[1:]:
        loudness = loudness * one(*cut)
    return loudness


def normal_values(stream_key, shape, deviation, most, shards=(), held_as=jnp.bfloat16):
    entries = jax.random.normal(stream_key, shape, jnp.float32) * deviation
    if len(shards) > 0:
        entries = level_of(stream_key, shape, shards, -0.22, 0.18) * entries
    return jnp.clip(entries, min=-most, max=most).astype(held_as)


def setup_inputs(seed: int = 0) -> dict:
    keys = jax.random.split(jax.random.key(seed), 5)
    return {
        "features": normal_values(keys[0], (C, NY, NZ, NX), 1.0, 6.0, ((1, 16), (2, 32))),
        "spectral_weight": normal_values(keys[1], (2, MX, MY, MZ, C * C), (C // 16) ** -0.5, 4.0, ((1, 16), (2, 32))),
        "bypass_weight": normal_values(keys[2], (C, C), C ** -0.5, 1.0),
        "bias_vector": normal_values(keys[3], (C,), 0.5, 3.0, (), jnp.float32),
    }


def centred(mode_count):
    index_list = jnp.arange(mode_count, dtype=jnp.int32)
    return jnp.where(index_list < mode_count // 2, index_list, index_list - mode_count).astype(jnp.int32)

def phases(frequencies, positions, period):
    product = positions[:, None] * frequencies[None, :] % period
    return product.astype(jnp.float32) * jnp.float32(2.0 * math.pi / period)

def forward_pair(frequencies, positions, period):
    angles = phases(frequencies, positions, period)
    cosines = jnp.cos(angles)
    sinewaves = jnp.sin(angles)
    return jnp.stack([jnp.stack([cosines, -sinewaves]), jnp.stack([sinewaves, cosines])])

def inverse_pair(frequencies, positions, period):
    angles = phases(frequencies, positions, period).T
    cosines = jnp.cos(angles)
    sinewaves = jnp.sin(angles)
    return jnp.stack([jnp.stack([cosines, sinewaves]), jnp.stack([-sinewaves, cosines])])

def x_forward_table(mode_count, length, norming):
    angles = phases(jnp.arange(mode_count, dtype=jnp.int32), jnp.arange(length, dtype=jnp.int32), length)
    table = jnp.stack([jnp.cos(angles) * norming, -jnp.sin(angles) * norming], axis=2)
    return table.reshape(length, 2 * mode_count)

def x_inverse_table(mode_count, length, norming):
    angles = phases(jnp.arange(mode_count, dtype=jnp.int32), jnp.arange(length, dtype=jnp.int32), length).T
    factor = jnp.where(jnp.arange(mode_count) == 0, 1.0, 2.0).astype(jnp.float32)[:, None] * norming
    return jnp.stack([jnp.cos(angles) * factor, -jnp.sin(angles) * factor], axis=1)

def reference(features, spectral_weight, bypass_weight, bias_vector):
    highest = lax.Precision.HIGHEST
    norming = jnp.float32(1.0 / math.sqrt(NX * NY * NZ))
    x_table = x_forward_table(MX, NX, norming)
    y_table = forward_pair(centred(MY), jnp.arange(NY, dtype=jnp.int32), NY)
    z_table = forward_pair(centred(MZ), jnp.arange(NZ, dtype=jnp.int32), NZ)

    def forward_one(channel_plane):
        spectrum = jnp.einsum('yzx,xa->yza', channel_plane.astype(jnp.float32), x_table, precision=highest)
        spectrum = spectrum.reshape(NY, NZ, MX, 2)
        along_y = jnp.einsum('yzkp,pqyj->jzkq', spectrum, y_table, precision=highest)
        return jnp.einsum('jzkp,pqzm->jmkq', along_y, z_table, precision=highest)
    spectrum = lax.map(forward_one, features)
    weights = spectral_weight.astype(jnp.float32).reshape(2, MX, MY, MZ, C, C)
    real_in = spectrum[..., 0]
    imag_in = spectrum[..., 1]

    def contract(values, matrix):
        return jnp.einsum('ijmk,kjmio->ojmk', values, matrix, precision=highest)
    real_out = contract(real_in, weights[0]) - contract(imag_in, weights[1])
    imag_out = contract(imag_in, weights[0]) + contract(real_in, weights[1])
    mixed_modes = jnp.stack([real_out, imag_out], axis=-1)
    z_back = inverse_pair(centred(MZ), jnp.arange(NZ, dtype=jnp.int32), NZ)
    y_back = inverse_pair(centred(MY), jnp.arange(NY, dtype=jnp.int32), NY)
    x_back_table = x_inverse_table(MX, NX, norming).reshape(2 * MX, NX)
    flat_field = features.reshape(C, NY * NZ * NX)

    def inverse_one(packed):
        mode_block, column, offset = packed
        along_z = jnp.einsum('jmkq,qrmz->jzkr', mode_block, z_back, precision=highest)
        along_y = jnp.einsum('jzkq,qrjy->yzkr', along_z, y_back, precision=highest).reshape(NY * NZ, 2 * MX)
        spatial = jnp.dot(along_y, x_back_table, precision=highest, preferred_element_type=jnp.float32)
        bypass = jnp.dot(column, flat_field, preferred_element_type=jnp.float32).reshape(NY * NZ, NX)
        return jax.nn.gelu(spatial + bypass + offset).astype(jnp.bfloat16)
    result = lax.map(inverse_one, (mixed_modes, bypass_weight.T, bias_vector))
    return result.reshape(C, NY, NZ, NX)
```

```python
import functools
import math

import jax
import jax.numpy as jnp
import ml_dtypes
import numpy as np
from jax import lax
from jax.experimental import pallas as pl
from jax.experimental.pallas import tpu as pltpu
from jax.sharding import PartitionSpec as P

MESH = pl.DeviceIdType.MESH
BF = jnp.bfloat16
F32 = jnp.float32
MIB = 1 << 20


def centred(count):
    index = np.arange(count)
    return np.where(index < count // 2, index, index - count)


def split(table):
    high = table.astype(ml_dtypes.bfloat16)
    low = (table - high.astype(np.float64)).astype(ml_dtypes.bfloat16)
    return high, low


def pair(frequencies, positions, period, sign):
    angle = 2.0 * np.pi * ((positions[:, None] * frequencies[None, :]) % period) / period
    c, s = np.cos(angle), np.sin(angle)
    return np.stack([np.stack([c, sign * s]), np.stack([-sign * s, c])])


def make_tables(nx, ny, nz, mx, my, mz, py, pz):
    k = mx // py
    zl = nz // pz
    yl = ny // py
    norm = 1.0 / math.sqrt(nx * ny * nz)
    angle = 2.0 * np.pi * ((np.arange(mx)[:, None] * np.arange(nx)[None, :]) % nx) / nx
    eye = np.eye(k)
    xf = np.stack([np.cos(angle) * norm, -np.sin(angle) * norm], 1).reshape(2 * mx, nx)
    weight = np.where(np.arange(mx) == 0, 1.0, 2.0)[:, None] * norm
    xi = np.stack([np.cos(angle) * weight, -np.sin(angle) * weight], 1).reshape(2 * mx, nx)
    yf = pair(centred(my), np.arange(ny), ny, -1.0)
    yf = np.einsum("pqyj,kl->jkqylp", yf, eye).reshape(my * k * 2, ny * k * 2)
    yi = pair(centred(my), np.arange(ny), ny, 1.0)
    yi = np.einsum("qryj,kl->ykrjlq", yi, eye).reshape(ny * k * 2, my * k * 2)
    zf = pair(centred(mz), np.arange(nz), nz, -1.0).reshape(2, 2, pz, zl, mz)
    zf = np.einsum("pqszm,kl->zqkmslp", zf, eye).reshape(zl, 2 * k * mz, pz * k * 2)
    zi = pair(centred(mz), np.arange(nz), nz, 1.0).reshape(2, 2, pz, zl, mz)
    zi = np.einsum("qrszm,kl->zskrqlm", zi, eye).reshape(zl, pz * k * 2, 2 * k * mz)
    return xf, xi, yf, yi, zf, zi


def halves(value):
    high = value.astype(BF)
    return high, (value - high.astype(F32)).astype(BF)


def dot(a, b, dims=((1,), (0,))):
    return lax.dot_general(a, b, (dims, ((), ())), preferred_element_type=F32)


def dot3(ah, al, bh, bl):
    return dot(ah, bh) + dot(al, bh) + dot(ah, bl)


def exchange_kernel(axis, n, src, dst, send_sem, recv_sem, own_sem):
    me = lax.axis_index(axis)
    barrier = pltpu.get_barrier_semaphore()

    def greet(step, carry):
        pl.semaphore_signal(
            barrier, inc=1, device_id={axis: lax.rem(me + step, n)}, device_id_type=MESH
        )
        return carry

    lax.fori_loop(1, n, greet, 0)
    pl.semaphore_wait(barrier, n - 1)

    def copy(step):
        peer = lax.rem(me + step, n)
        return pltpu.make_async_remote_copy(
            src_ref=src.at[peer],
            dst_ref=dst.at[me],
            send_sem=send_sem.at[step],
            recv_sem=recv_sem.at[step],
            device_id={axis: peer},
            device_id_type=MESH,
        )

    def start(step, carry):
        copy(step).start()
        return carry

    def finish(step, carry):
        copy(step).wait()
        return carry

    lax.fori_loop(1, n, start, 0)
    own = pltpu.make_async_copy(src.at[me], dst.at[me], own_sem)
    own.start()
    own.wait()
    lax.fori_loop(1, n, finish, 0)


def exchange(blocks, axis, n, ident):
    return pl.pallas_call(
        functools.partial(exchange_kernel, axis, n),
        out_shape=jax.ShapeDtypeStruct(blocks.shape, blocks.dtype),
        in_specs=[pl.BlockSpec(memory_space=pl.ANY)],
        out_specs=pl.BlockSpec(memory_space=pl.ANY),
        scratch_shapes=[
            pltpu.SemaphoreType.DMA((n,)),
            pltpu.SemaphoreType.DMA((n,)),
            pltpu.SemaphoreType.DMA,
        ],
        compiler_params=pltpu.CompilerParams(collective_id=ident, has_side_effects=True),
        name="exchange_" + axis + str(ident),
    )(blocks)


def x_forward_kernel(zl, f_ref, t_ref, o_ref):
    block = f_ref[...].astype(F32)
    channels, rows, length = block.shape
    for y in range(rows // zl):
        field = block[:, y * zl : (y + 1) * zl, :].reshape(channels * zl, length).astype(BF)
        both = dot(t_ref[...], field, ((1,), (1,)))
        half = both.shape[0] // 2
        o_ref[:, y] = (both[:half] + both[half:]).reshape(o_ref.shape[0], o_ref.shape[2], -1)


def y_forward_kernel(x_ref, th_ref, tl_ref, o_ref):
    @pl.when(pl.program_id(0) == 0)
    def _():
        o_ref[...] = jnp.zeros_like(o_ref)

    xh, xl = halves(x_ref[...])
    o_ref[...] += dot3(th_ref[...], tl_ref[...], xh, xl)


def y_inverse_kernel(x_ref, th_ref, tl_ref, o_ref):
    xh, xl = halves(x_ref[...])
    o_ref[...] = dot3(th_ref[...], tl_ref[...], xh, xl)


def middle_kernel(zl, x_ref, w_ref, fh_ref, fl_ref, ih_ref, il_ref, o_ref):
    xh, xl = halves(x_ref[...])
    lanes = x_ref.shape[1]
    channels = lanes // zl
    inner = lax.broadcasted_iota(jnp.int32, (1, lanes), 1) % zl
    modes = jnp.zeros((fh_ref.shape[1], lanes), F32)
    for z in range(zl):
        modes += jnp.where(inner == z, dot3(fh_ref[z], fl_ref[z], xh, xl), 0.0)
    pairs = w_ref.shape[2]
    lane = lax.broadcasted_iota(jnp.int32, (lanes, pairs), 0) // zl
    both = lax.broadcasted_iota(jnp.int32, (lanes, pairs), 1)
    spread = jnp.where(lane == both // channels, 1.0, 0.0).astype(BF)
    mh, ml = halves(modes)
    wide = dot(mh, spread) + dot(ml, spread)
    half = wide.shape[0] // 2
    re, im = wide[:half], wide[half:]
    wr, wi = w_ref[0].astype(F32), w_ref[1].astype(F32)
    mixed = jnp.concatenate([wr * re - wi * im, wr * im + wi * re], axis=0)
    both = lax.broadcasted_iota(jnp.int32, (pairs, lanes), 0)
    lane = lax.broadcasted_iota(jnp.int32, (pairs, lanes), 1) // zl
    gather = jnp.where(both % channels == lane, 1.0, 0.0).astype(BF)
    ph, plo = halves(mixed)
    summed = dot(ph, gather) + dot(plo, gather)
    sh, sl = halves(summed)
    total = jnp.zeros(o_ref.shape, F32)
    for z in range(zl):
        total += jnp.where(inner == z, dot3(ih_ref[z], il_ref[z], sh, sl), 0.0)
    o_ref[...] = total


def x_inverse_kernel(zl, r_ref, f_ref, w_ref, b_ref, th_ref, tl_ref, o_ref, mix_ref, bias_ref):
    channels, rows, length = f_ref.shape
    lanes = channels * zl

    @pl.when(pl.program_id(0) == 0)
    def _():
        row = lax.broadcasted_iota(jnp.int32, (lanes, channels), 0) // zl
        column = lax.broadcasted_iota(jnp.int32, (lanes, channels), 1)
        pick = row == column
        ones = jnp.where(pick, 1.0, 0.0).astype(BF)
        left = dot(ones, w_ref[...], ((1,), (1,))).astype(BF)
        full = dot(left, ones, ((1,), (1,)))
        a = lax.broadcasted_iota(jnp.int32, (lanes, lanes), 0) % zl
        b = lax.broadcasted_iota(jnp.int32, (lanes, lanes), 1) % zl
        mix_ref[...] = jnp.where(a == b, full, 0.0).astype(BF)
        column = jnp.sum(jnp.where(pick, b_ref[...], 0.0), axis=1, keepdims=True)
        bias_ref[...] = jnp.broadcast_to(column, bias_ref.shape)

    block = f_ref[...].astype(F32)
    th, tl, mix, bias = th_ref[...], tl_ref[...], mix_ref[...], bias_ref[...]
    for y in range(rows // zl):
        spectrum = r_ref[:, y].reshape(-1, lanes)
        sh, sl = halves(spectrum)
        field = block[:, y * zl : (y + 1) * zl, :].reshape(lanes, length).astype(BF)
        first = ((0,), (0,))
        value = dot(sh, th, first) + dot(sl, th, first) + dot(sh, tl, first)
        value = value + dot(mix, field) + bias
        out = jax.nn.gelu(value).reshape(channels, zl, length)
        o_ref[:, y * zl : (y + 1) * zl, :] = out.astype(o_ref.dtype)


def params(mib):
    return pltpu.CompilerParams(vmem_limit_bytes=mib * MIB)


def whole(shape):
    return pl.BlockSpec(shape, lambda i: (0,) * len(shape))


def per_device(tables, n_y, n_z, features, spectral_weight, bypass_weight, bias_vector):
    xf, xi, yf, yi, zf, zi = tables
    c, yl, zl, nx = features.shape
    _, kl, _, mz, pairs = spectral_weight.shape
    lanes = c * zl
    part = 2 * kl
    flat = features.reshape(c, yl * zl, nx)
    step = 2
    steps = yl // step

    xh, xl = split(xf)
    x_rows = jnp.asarray(np.concatenate([xh, xl], 0))
    field_spec = pl.BlockSpec((c, step * zl, nx), lambda i: (0, i, 0))
    row_spec = pl.BlockSpec((n_y, step, part, lanes), lambda i: (0, i, 0, 0))
    a = pl.pallas_call(
        functools.partial(x_forward_kernel, zl),
        grid=(steps,),
        in_specs=[field_spec, whole(x_rows.shape)],
        out_specs=row_spec,
        out_shape=jax.ShapeDtypeStruct((n_y, yl, part, lanes), F32),
        compiler_params=params(32),
        name="x_forward",
    )(flat, x_rows)

    a = exchange(a, "py", n_y, 0).reshape(n_y * yl * part, lanes)

    yh, ylo = map(jnp.asarray, split(yf))
    my_rows = yh.shape[0]
    tile = 256
    b = pl.pallas_call(
        y_forward_kernel,
        grid=(a.shape[0] // tile,),
        in_specs=[
            pl.BlockSpec((tile, lanes), lambda i: (i, 0)),
            pl.BlockSpec((my_rows, tile), lambda i: (0, i)),
            pl.BlockSpec((my_rows, tile), lambda i: (0, i)),
        ],
        out_specs=whole((my_rows, lanes)),
        out_shape=jax.ShapeDtypeStruct((my_rows, lanes), F32),
        compiler_params=params(32),
        name="y_forward",
    )(a, yh, ylo)

    b = exchange(b.reshape(n_z, part, lanes), "pz", n_z, 1).reshape(n_z * part, lanes)

    fh, fl = map(jnp.asarray, split(zf))
    ih, il = map(jnp.asarray, split(zi))
    p = pl.pallas_call(
        functools.partial(middle_kernel, zl),
        out_shape=jax.ShapeDtypeStruct((n_z * part, lanes), F32),
        compiler_params=params(48),
        name="middle",
    )(b, spectral_weight.reshape(2, kl * mz, pairs), fh, fl, ih, il)

    p = exchange(p.reshape(n_z, part, lanes), "pz", n_z, 2).reshape(n_z * part, lanes)

    gh, gl = map(jnp.asarray, split(yi))
    q = pl.pallas_call(
        y_inverse_kernel,
        grid=(gh.shape[0] // tile,),
        in_specs=[
            whole(p.shape),
            pl.BlockSpec((tile, gh.shape[1]), lambda i: (i, 0)),
            pl.BlockSpec((tile, gh.shape[1]), lambda i: (i, 0)),
        ],
        out_specs=pl.BlockSpec((tile, lanes), lambda i: (i, 0)),
        out_shape=jax.ShapeDtypeStruct((gh.shape[0], lanes), F32),
        compiler_params=params(32),
        name="y_inverse",
    )(p, gh, gl)

    q = exchange(q.reshape(n_y, yl, part, lanes), "py", n_y, 3)

    th, tl = map(jnp.asarray, split(xi))
    out = pl.pallas_call(
        functools.partial(x_inverse_kernel, zl),
        grid=(steps,),
        in_specs=[
            row_spec,
            field_spec,
            whole(bypass_weight.shape),
            whole((1, c)),
            whole(th.shape),
            whole(tl.shape),
        ],
        out_specs=field_spec,
        out_shape=jax.ShapeDtypeStruct(flat.shape, BF),
        scratch_shapes=[pltpu.VMEM((lanes, lanes), BF), pltpu.VMEM((lanes, nx), F32)],
        compiler_params=params(32),
        name="x_inverse",
    )(q, flat, bypass_weight, bias_vector.reshape(1, c), th, tl)
    return out.reshape(features.shape)


def solution(mesh):
    n_y, n_z = mesh.shape["py"], mesh.shape["pz"]

    def run(features, spectral_weight, bypass_weight, bias_vector):
        _, ny, nz, nx = features.shape
        _, mx, my, mz, _ = spectral_weight.shape
        tables = make_tables(nx, ny, nz, mx, my, mz, n_y, n_z)
        return jax.shard_map(
            functools.partial(per_device, tables, n_y, n_z),
            mesh=mesh,
            in_specs=(P(None, "py", "pz", None), P(None, "py", "pz", None, None), P(), P()),
            out_specs=P(None, "py", "pz", None),
            check_vma=False,
        )(features, spectral_weight, bypass_weight, bias_vector)

    return run
```

```python
import functools
import math

import jax
import jax.numpy as jnp
import ml_dtypes
import numpy as np
from jax import lax
from jax.experimental import pallas as pl
from jax.experimental.pallas import tpu as pltpu
from jax.sharding import PartitionSpec as P

MESH = pl.DeviceIdType.MESH
BF = jnp.bfloat16
F32 = jnp.float32
MIB = 1 << 20
GROUP = 4


def centred(count):
    index = np.arange(count)
    return np.where(index < count // 2, index, index - count)


def split(table, axis=0):
    high = table.astype(ml_dtypes.bfloat16)
    low = (table - high.astype(np.float64)).astype(ml_dtypes.bfloat16)
    return np.stack([high, low], axis)


def pair(frequencies, positions, period, sign):
    angle = 2.0 * np.pi * ((positions[:, None] * frequencies[None, :]) % period) / period
    c, s = np.cos(angle), np.sin(angle)
    return np.stack([np.stack([c, sign * s]), np.stack([-sign * s, c])])


def make_tables(nx, ny, nz, mx, my, mz, py, pz):
    k = mx // py
    zl = nz // pz
    yl = ny // py
    norm = 1.0 / math.sqrt(nx * ny * nz)
    angle = 2.0 * np.pi * ((np.arange(mx)[:, None] * np.arange(nx)[None, :]) % nx) / nx
    eye = np.eye(k)
    xf = np.stack([np.cos(angle) * norm, -np.sin(angle) * norm], 1).reshape(2 * mx, nx)
    weight = np.where(np.arange(mx) == 0, 1.0, 2.0)[:, None] * norm
    xi = np.stack([np.cos(angle) * weight, -np.sin(angle) * weight], 1).reshape(2 * mx, nx)
    order = np.arange(my).reshape(pz // GROUP, GROUP).T.reshape(-1)
    yf = pair(centred(my), np.arange(ny), ny, -1.0)[..., order].reshape(2, 2, py, yl, my)
    yf = np.einsum("pqdyj,kl->djkqylp", yf, eye).reshape(py, my * k * 2, yl * k * 2)
    yi = pair(centred(my), np.arange(ny), ny, 1.0)[..., order].reshape(2, 2, py, yl, my)
    yi = np.einsum("qrdyj,kl->dykrjlq", yi, eye).reshape(py, yl * k * 2, my * k * 2)
    zf = pair(centred(mz), np.arange(nz), nz, -1.0).reshape(2, 2, pz, zl, mz)
    zf = np.einsum("pqszm,kl->zqkmslp", zf, eye).reshape(zl, 2 * k * mz, pz * k * 2)
    zi = pair(centred(mz), np.arange(nz), nz, 1.0).reshape(2, 2, pz, zl, mz)
    zi = np.einsum("qrszm,kl->zskrqlm", zi, eye).reshape(zl, pz * k * 2, 2 * k * mz)
    return xf, xi, yf, yi, zf, zi


def halves(value):
    high = value.astype(BF)
    return high, (value - high.astype(F32)).astype(BF)


def dot(a, b, dims=((1,), (0,))):
    return lax.dot_general(a, b, (dims, ((), ())), preferred_element_type=F32)


def dot3(ah, al, bh, bl):
    return dot(ah, bh) + dot(al, bh) + dot(ah, bl)


def x_forward(zl, field, table, out, first, last):
    def step(i, carry):
        block = field[:, pl.ds(pl.multiple_of(i * 2 * zl, 2 * zl), 2 * zl), :].astype(F32)
        channels, _, length = block.shape
        for y in range(2):
            plane = block[:, y * zl : (y + 1) * zl, :].reshape(channels * zl, length).astype(BF)
            both = dot(table[...], plane, ((1,), (1,)))
            half = both.shape[0] // 2
            rows = out.shape[1] // (field.shape[1] // zl)
            start = pl.multiple_of((i * 2 + y) * rows, rows)
            out[:, pl.ds(start, rows), :] = (both[:half] + both[half:]).reshape(
                out.shape[0], rows, out.shape[2]
            )
        return carry

    lax.fori_loop(first, last, step, 0)


def middle(zl, x, w, forward, inverse):
    xh, xl = halves(x)
    lanes = x.shape[1]
    channels = lanes // zl
    inner = lax.broadcasted_iota(jnp.int32, (1, lanes), 1) % zl
    modes = jnp.zeros((forward.shape[2], lanes), F32)
    for z in range(zl):
        modes += jnp.where(inner == z, dot3(forward[z, 0], forward[z, 1], xh, xl), 0.0)
    pairs = w.shape[2]
    lane = lax.broadcasted_iota(jnp.int32, (lanes, pairs), 0) // zl
    both = lax.broadcasted_iota(jnp.int32, (lanes, pairs), 1)
    spread = jnp.where(lane == both // channels, 1.0, 0.0).astype(BF)
    mh, ml = halves(modes)
    wide = dot(mh, spread) + dot(ml, spread)
    half = wide.shape[0] // 2
    re, im = wide[:half], wide[half:]
    wr, wi = w[0].astype(F32), w[1].astype(F32)
    mixed = jnp.concatenate([wr * re - wi * im, wr * im + wi * re], axis=0)
    both = lax.broadcasted_iota(jnp.int32, (pairs, lanes), 0)
    lane = lax.broadcasted_iota(jnp.int32, (pairs, lanes), 1) // zl
    gather = jnp.where(both % channels == lane, 1.0, 0.0).astype(BF)
    ph, plo = halves(mixed)
    summed = dot(ph, gather) + dot(plo, gather)
    sh, sl = halves(summed)
    total = jnp.zeros(x.shape, F32)
    for z in range(zl):
        total += jnp.where(inner == z, dot3(inverse[z, 0], inverse[z, 1], sh, sl), 0.0)
    return total


def spectrum_kernel(n_y, n_z, zl, *refs):
    (
        f_hbm, xt_hbm, yt_hbm, yi_hbm, zf_hbm, zi_hbm, w_hbm, r_hbm,
        f, xt, yt, yi, zf, zi, w, a, theirs, summing, arrived, total, seen, mixed, back, ring, planes,
        load_sem, swap_s, swap_r, sum_s, sum_r, out_s, out_r, in_s, in_r, ring_s, ring_r,
        turn_s, turn_r, keep_s,
    ) = refs
    here, column = lax.axis_index("py"), lax.axis_index("pz")
    n_ring = n_y // 2
    side, z = here // n_ring, here % n_ring
    other = 1 - side
    half_py = lambda s, at: s * n_ring + at % n_ring
    partner = {"py": half_py(other, z)}
    neighbours = ({"py": half_py(side, z + 1)}, {"py": half_py(side, z + n_ring - 1)})

    loads = []

    def load(source, target):
        copy = pltpu.make_async_copy(source, target, load_sem.at[len(loads)])
        copy.start()
        loads.append(copy)
        return copy

    pieces = 4
    rows = f.shape[1] // pieces
    table_x = load(xt_hbm, xt)
    fields = [
        load(f_hbm.at[:, pl.ds(i * rows, rows), :], f.at[:, pl.ds(i * rows, rows), :])
        for i in range(pieces)
    ]
    depth = yt_hbm.shape[3]
    table_y = [
        load(yt_hbm.at[half_py(s, z)], yt.at[:, :, pl.ds(i * depth, depth)])
        for i, s in enumerate((side, other))
    ]
    table_z = [load(zf_hbm, zf), load(w_hbm, w), load(zi_hbm, zi)]
    table_i = [load(yi_hbm.at[half_py(s, z)], yi.at[i]) for i, s in enumerate((side, other))]

    barrier = pltpu.get_barrier_semaphore()
    for peer in (partner,) + neighbours:
        pl.semaphore_signal(barrier, inc=1, device_id=peer, device_id_type=MESH)

    def greet(step, carry):
        pl.semaphore_signal(
            barrier, inc=1, device_id={"pz": (column + step) % n_z}, device_id_type=MESH
        )
        return carry

    lax.fori_loop(1, n_z, greet, 0)

    table_x.wait()
    turns = f.shape[1] // (2 * zl) // pieces
    for i in range(pieces):
        fields[i].wait()
        x_forward(zl, f, xt, a, i * turns, (i + 1) * turns)
    pl.semaphore_wait(barrier, n_z + 2)

    reach = n_ring // 2
    offsets = [reach] + [o * s for o in range(reach - 1, 0, -1) for s in (1, -1)] + [0]

    def swap(i):
        at = (z + offsets[i] + n_ring) % n_ring
        return pltpu.make_async_remote_copy(
            src_ref=a.at[half_py(other, at)],
            dst_ref=theirs.at[at],
            send_sem=swap_s.at[i],
            recv_sem=swap_r.at[i],
            device_id=partner,
            device_id_type=MESH,
        )

    for i in range(n_ring):
        swap(i).start()
    for copy in table_y:
        copy.wait()

    def partial(i):
        at = (z + offsets[i] + n_ring) % n_ring
        swap(i).wait_recv()
        block = jnp.concatenate([a[half_py(side, at)], theirs[at]], axis=0)
        high, low = halves(block)
        return dot3(yt[0], yt[1], high, low)

    part = total.shape[0] * total.shape[1] // GROUP
    span = lambda g: pl.ds(g * part, part)
    carries = lambda way, step, g: step > 0 or (g < GROUP // 2) == (way == 0)

    def hop(way, step, g):
        index = (way * reach + step) * GROUP + g
        return pltpu.make_async_remote_copy(
            src_ref=summing.at[way, step, span(g)],
            dst_ref=arrived.at[way, step, span(g)],
            send_sem=sum_s.at[index],
            recv_sem=sum_r.at[index],
            device_id=neighbours[way],
            device_id_type=MESH,
        )

    block = partial(0)
    for g in range(GROUP):
        way = 0 if g < GROUP // 2 else 1
        summing[way, 0, g * part : (g + 1) * part] = block[g * part : (g + 1) * part]
        hop(way, 0, g).start()
    for step in range(1, reach):
        for way in range(2):
            summing[way, step] = partial(2 * step - 1 + way)
        for g in range(GROUP):
            for way in range(2):
                if carries(way, step - 1, g):
                    hop(way, step - 1, g).wait_recv()
                    summing[way, step, span(g)] += arrived[way, step - 1, span(g)]
                hop(way, step, g).start()

    per = n_z // GROUP
    y_chip, place = column // GROUP, column % GROUP
    slot = place * per + y_chip
    last = partial(n_ring - 1)

    def to_owner(source, owner):
        return pltpu.make_async_remote_copy(
            src_ref=total.at[source],
            dst_ref=seen.at[column],
            send_sem=out_s.at[owner],
            recv_sem=out_r.at[column],
            device_id={"pz": owner},
            device_id_type=MESH,
        )

    def from_owner(owner):
        return pltpu.make_async_remote_copy(
            src_ref=total.at[0],
            dst_ref=seen.at[owner],
            send_sem=out_s.at[owner],
            recv_sem=out_r.at[owner],
            device_id={"pz": owner},
            device_id_type=MESH,
        )

    for g in range(GROUP):
        for way in range(2):
            hop(way, reach - 1, g).wait_recv()
        value = last[g * part : (g + 1) * part] + arrived[0, reach - 1, span(g)]
        value = value + arrived[1, reach - 1, span(g)]
        total[g * per : (g + 1) * per] = value.reshape(per, total.shape[1], total.shape[2])

        def send(i, carry):
            chip = (y_chip + i) % per
            owner = chip * GROUP + g

            @pl.when(owner != column)
            def _():
                to_owner(g * per + chip, owner).start()

            return carry

        lax.fori_loop(0, per, send, 0)
    seen[column] = total[slot]

    def collect(step, carry):
        from_owner((column + step) % n_z).wait()
        return carry

    for copy in table_z:
        copy.wait()
    lax.fori_loop(1, n_z, collect, 0)

    value = middle(zl, seen[...].reshape(-1, seen.shape[2]), w, zf, zi)
    mixed[...] = value.reshape(mixed.shape)

    def to_cells(step):
        peer = (column + step) % n_z
        return pltpu.make_async_remote_copy(
            src_ref=mixed.at[peer],
            dst_ref=back.at[slot],
            send_sem=in_s.at[step],
            recv_sem=in_r.at[step],
            device_id={"pz": peer},
            device_id_type=MESH,
        )

    def start_back(step, carry):
        to_cells(step).start()
        return carry

    def end_back(step, carry):
        to_cells(step).wait()
        return carry

    lax.fori_loop(1, n_z, start_back, 0)
    back[slot] = mixed[column]
    for copy in table_i:
        copy.wait()
    lax.fori_loop(1, n_z, end_back, 0)

    wide = lambda g: pl.ds(g * per, per)
    passes = lambda way, step, g: step < reach - 1 or (g < GROUP // 2) == (way == 0)

    def relay(way, step, g):
        index = (way * reach + step) * GROUP + g
        source = back.at[wide(g)] if step == 0 else ring.at[way, step - 1, wide(g)]
        target = ring.at[0 if step == reach - 1 else way, step, wide(g)]
        return pltpu.make_async_remote_copy(
            src_ref=source,
            dst_ref=target,
            send_sem=ring_s.at[index],
            recv_sem=ring_r.at[index],
            device_id=neighbours[way],
            device_id_type=MESH,
        )

    def turn(i, owner):
        return pltpu.make_async_remote_copy(
            src_ref=planes.at[1, i],
            dst_ref=r_hbm.at[owner],
            send_sem=turn_s.at[i],
            recv_sem=turn_r.at[i],
            device_id=partner,
            device_id_type=MESH,
        )

    def keep(i, owner):
        return pltpu.make_async_copy(planes.at[0, i], r_hbm.at[owner], keep_s.at[i])

    def spread(i, offset, block):
        owner = half_py(side, z + offset + n_ring)
        high, low = halves(block.reshape(-1, block.shape[2]))
        planes[1, i] = dot3(yi[1, 0], yi[1, 1], high, low)
        turn(i, owner).start()
        planes[0, i] = dot3(yi[0, 0], yi[0, 1], high, low)
        keep(i, owner).start()

    for g in range(GROUP):
        for way in range(2):
            relay(way, 0, g).start()
    spread(0, 0, back[...])
    for step in range(1, reach):
        for g in range(GROUP):
            for way in range(2):
                relay(way, step - 1, g).wait_recv()
                if passes(way, step, g):
                    relay(way, step, g).start()
        for way in range(2):
            spread(2 * step - 1 + way, step if way else -step, ring[way, step - 1])
    for g in range(GROUP):
        for way in range(2):
            if passes(way, reach - 1, g):
                relay(way, reach - 1, g).wait_recv()
    spread(n_ring - 1, reach, ring[0, reach - 1])

    for i in range(n_ring):
        swap(i).wait_send()
    for step in range(reach):
        for g in range(GROUP):
            for way in range(2):
                if carries(way, step, g):
                    hop(way, step, g).wait_send()
                if passes(way, step, g):
                    relay(way, step, g).wait_send()
    for i in range(n_ring):
        keep(i, here).wait()
        turn(i, here).wait()


def x_inverse_kernel(zl, r_ref, f_ref, w_ref, b_ref, th_ref, tl_ref, o_ref, mix_ref, bias_ref):
    channels, rows, length = f_ref.shape
    lanes = channels * zl

    @pl.when(pl.program_id(0) == 0)
    def _():
        row = lax.broadcasted_iota(jnp.int32, (lanes, channels), 0) // zl
        column = lax.broadcasted_iota(jnp.int32, (lanes, channels), 1)
        pick = row == column
        ones = jnp.where(pick, 1.0, 0.0).astype(BF)
        left = dot(ones, w_ref[...], ((1,), (1,))).astype(BF)
        full = dot(left, ones, ((1,), (1,)))
        a = lax.broadcasted_iota(jnp.int32, (lanes, lanes), 0) % zl
        b = lax.broadcasted_iota(jnp.int32, (lanes, lanes), 1) % zl
        mix_ref[...] = jnp.where(a == b, full, 0.0).astype(BF)
        column = jnp.sum(jnp.where(pick, b_ref[...], 0.0), axis=1, keepdims=True)
        bias_ref[...] = jnp.broadcast_to(column, bias_ref.shape)

    block = f_ref[...].astype(F32)
    th, tl, mix, bias = th_ref[...], tl_ref[...], mix_ref[...], bias_ref[...]
    for y in range(rows // zl):
        spectrum = r_ref[:, y].reshape(-1, lanes)
        sh, sl = halves(spectrum)
        field = block[:, y * zl : (y + 1) * zl, :].reshape(lanes, length).astype(BF)
        first = ((0,), (0,))
        value = dot(sh, th, first) + dot(sl, th, first) + dot(sh, tl, first)
        value = value + dot(mix, field) + bias
        out = jax.nn.gelu(value).reshape(channels, zl, length)
        o_ref[:, y * zl : (y + 1) * zl, :] = out.astype(o_ref.dtype)


def params(mib):
    return pltpu.CompilerParams(vmem_limit_bytes=mib * MIB)


def whole(shape):
    return pl.BlockSpec(shape, lambda i: (0,) * len(shape))


def per_device(tables, n_y, n_z, features, spectral_weight, bypass_weight, bias_vector):
    xf, xi, yf, yi, zf, zi = tables
    c, yl, zl, nx = features.shape
    _, kl, _, mz, pairs = spectral_weight.shape
    lanes = c * zl
    part = 2 * kl
    rows = yl * part
    flat = features.reshape(c, yl * zl, nx)
    x_rows = split(xf).reshape(-1, nx)
    y_rows, y_back = split(yf, 1), split(yi, 1)
    z_rows, z_back = split(zf, 1), split(zi, 1)
    weight = spectral_weight.reshape(2, kl * mz, pairs)
    my_rows = y_rows.shape[2]
    modes = my_rows // part
    n_ring = n_y // 2
    reach = n_ring // 2
    operands = [flat] + [jnp.asarray(t) for t in (x_rows, y_rows, y_back, z_rows, z_back)] + [weight]
    sems = [16, n_ring, n_ring] + [2 * reach * GROUP] * 2 + [n_z] * 4 + [2 * reach * GROUP] * 2
    sems += [n_ring] * 3
    planes = pl.pallas_call(
        functools.partial(spectrum_kernel, n_y, n_z, zl),
        out_shape=jax.ShapeDtypeStruct((n_y, rows, lanes), F32),
        in_specs=[pl.BlockSpec(memory_space=pl.ANY)] * len(operands),
        out_specs=pl.BlockSpec(memory_space=pl.ANY),
        scratch_shapes=[
            pltpu.VMEM(flat.shape, BF),
            pltpu.VMEM(x_rows.shape, BF),
            pltpu.VMEM((2, my_rows, 2 * rows), BF),
            pltpu.VMEM((2,) + y_back.shape[1:], BF),
            pltpu.VMEM(z_rows.shape, BF),
            pltpu.VMEM(z_back.shape, BF),
            pltpu.VMEM(weight.shape, BF),
            pltpu.VMEM((n_y, rows, lanes), F32),
            pltpu.VMEM((n_ring, rows, lanes), F32),
            pltpu.VMEM((2, reach, my_rows, lanes), F32),
            pltpu.VMEM((2, reach, my_rows, lanes), F32),
            pltpu.VMEM((modes, part, lanes), F32),
            pltpu.VMEM((n_z, part, lanes), F32),
            pltpu.VMEM((n_z, part, lanes), F32),
            pltpu.VMEM((modes, part, lanes), F32),
            pltpu.VMEM((2, reach, modes, part, lanes), F32),
            pltpu.VMEM((2, n_ring, rows, lanes), F32),
        ]
        + [pltpu.SemaphoreType.DMA((n,)) for n in sems],
        compiler_params=pltpu.CompilerParams(
            collective_id=0, has_side_effects=True, vmem_limit_bytes=60 * MIB
        ),
        name="spectrum",
    )(*operands)

    step = 2
    steps = yl // step
    field_spec = pl.BlockSpec((c, step * zl, nx), lambda i: (0, i, 0))
    th, tl = map(jnp.asarray, split(xi))
    out = pl.pallas_call(
        functools.partial(x_inverse_kernel, zl),
        grid=(steps,),
        in_specs=[
            pl.BlockSpec((n_y, step, part, lanes), lambda i: (0, i, 0, 0)),
            field_spec,
            whole(bypass_weight.shape),
            whole((1, c)),
            whole(th.shape),
            whole(tl.shape),
        ],
        out_specs=field_spec,
        out_shape=jax.ShapeDtypeStruct(flat.shape, BF),
        scratch_shapes=[pltpu.VMEM((lanes, lanes), BF), pltpu.VMEM((lanes, nx), F32)],
        compiler_params=params(60),
        name="x_inverse",
    )(planes.reshape(n_y, yl, part, lanes), flat, bypass_weight, bias_vector.reshape(1, c), th, tl)
    return out.reshape(features.shape)


def solution(mesh):
    n_y, n_z = mesh.shape["py"], mesh.shape["pz"]

    def run(features, spectral_weight, bypass_weight, bias_vector):
        _, ny, nz, nx = features.shape
        _, mx, my, mz, _ = spectral_weight.shape
        tables = make_tables(nx, ny, nz, mx, my, mz, n_y, n_z)
        return jax.shard_map(
            functools.partial(per_device, tables, n_y, n_z),
            mesh=mesh,
            in_specs=(P(None, "py", "pz", None), P(None, "py", "pz", None, None), P(), P()),
            out_specs=P(None, "py", "pz", None),
            check_vma=False,
        )(features, spectral_weight, bypass_weight, bias_vector)

    return run
```

```python
import functools
import math

import jax
import jax.numpy as jnp
import ml_dtypes
import numpy as np
from jax import lax
from jax.experimental import pallas as pl
from jax.experimental.pallas import tpu as pltpu
from jax.sharding import PartitionSpec as P

MESH = pl.DeviceIdType.MESH
BF = jnp.bfloat16
F32 = jnp.float32
MIB = 1 << 20
GROUP = 4


def centred(count):
    index = np.arange(count)
    return np.where(index < count // 2, index, index - count)


def split(table, axis=0):
    high = table.astype(ml_dtypes.bfloat16)
    low = (table - high.astype(np.float64)).astype(ml_dtypes.bfloat16)
    return np.stack([high, low], axis)


def thrice(table):
    high, low = split(table)
    return np.concatenate([high, high, low], -1)


def pair(frequencies, positions, period, sign):
    angle = 2.0 * np.pi * ((positions[:, None] * frequencies[None, :]) % period) / period
    c, s = np.cos(angle), np.sin(angle)
    return np.stack([np.stack([c, sign * s]), np.stack([-sign * s, c])])


def make_tables(nx, ny, nz, mx, my, mz, py, pz):
    k = mx // py
    zl = nz // pz
    yl = ny // py
    norm = 1.0 / math.sqrt(nx * ny * nz)
    angle = 2.0 * np.pi * ((np.arange(mx)[:, None] * np.arange(nx)[None, :]) % nx) / nx
    eye = np.eye(k)
    xf = np.stack([np.cos(angle) * norm, -np.sin(angle) * norm], 1).reshape(2 * mx, nx)
    weight = np.where(np.arange(mx) == 0, 1.0, 2.0)[:, None] * norm
    xi = np.stack([np.cos(angle) * weight, -np.sin(angle) * weight], 1).reshape(2 * mx, nx)
    order = np.arange(my).reshape(pz // GROUP, GROUP).T.reshape(-1)
    yf = pair(centred(my), np.arange(ny), ny, -1.0)[..., order].reshape(2, 2, py, yl, my)
    yf = np.einsum("pqdyj,kl->djkqylp", yf, eye).reshape(py, my * k * 2, yl * k * 2)
    yi = pair(centred(my), np.arange(ny), ny, 1.0)[..., order].reshape(2, 2, py, yl, my)
    yi = np.einsum("qrdyj,kl->dykrjlq", yi, eye).reshape(py, yl * k * 2, my * k * 2)
    zf = pair(centred(mz), np.arange(nz), nz, -1.0).reshape(2, 2, pz, zl, mz)
    zf = np.einsum("pqszm->zqmps", zf).reshape(zl, 2 * mz, 2 * pz)
    zi = pair(centred(mz), np.arange(nz), nz, 1.0).reshape(2, 2, pz // GROUP, GROUP, zl, mz)
    zi = np.einsum("qrjgzm->gzrjqm", zi).reshape(GROUP, zl * 2 * pz // GROUP, 2 * mz)
    return xf, xi, yf, yi, zf, zi


def halves(value):
    high = value.astype(BF)
    return high, (value - high.astype(F32)).astype(BF)


def triple(value):
    high, low = halves(value)
    return jnp.concatenate([high, low, high], 0)


def dot(a, b, dims=((1,), (0,))):
    return lax.dot_general(a, b, (dims, ((), ())), preferred_element_type=F32)


def dot3(ah, al, bh, bl):
    return dot(ah, bh) + dot(al, bh) + dot(ah, bl)


def x_forward(zl, field, table, out, first, last):
    def step(i, carry):
        block = field[:, pl.ds(pl.multiple_of(i * 2 * zl, 2 * zl), 2 * zl), :].astype(F32)
        channels, _, length = block.shape
        for y in range(2):
            plane = block[:, y * zl : (y + 1) * zl, :].reshape(channels * zl, length).astype(BF)
            both = dot(table[...], plane, ((1,), (1,)))
            half = both.shape[0] // 2
            rows = out.shape[1] // (field.shape[1] // zl)
            start = pl.multiple_of((i * 2 + y) * rows, rows)
            out[:, pl.ds(start, rows), :] = (both[:half] + both[half:]).reshape(
                out.shape[0], rows, out.shape[2]
            )
        return carry

    lax.fori_loop(first, last, step, 0)


def middle(zl, x, w, forward):
    cells, part, lanes = x.shape
    kl = part // 2
    channels = lanes // zl
    column = lambda k: jnp.concatenate([x[:, 2 * k, :], x[:, 2 * k + 1, :]], axis=0)
    block = triple(jnp.concatenate([column(k) for k in range(kl)], axis=1))
    inner = lax.broadcasted_iota(jnp.int32, (1, kl * lanes), 1) % zl
    modes = jnp.zeros((forward.shape[1], kl * lanes), F32)
    for z in range(zl):
        modes += jnp.where(inner == z, dot(forward[z], block), 0.0)
    count = modes.shape[0] // 2
    modes = jnp.concatenate(
        [
            modes[p * count : (p + 1) * count, k * lanes : (k + 1) * lanes]
            for p in range(2)
            for k in range(kl)
        ],
        axis=0,
    )
    pairs = w.shape[2]
    lane = lax.broadcasted_iota(jnp.int32, (lanes, pairs), 0) // zl
    both = lax.broadcasted_iota(jnp.int32, (lanes, pairs), 1)
    spread = jnp.where(lane == both // channels, 1.0, 0.0).astype(BF)
    mh, ml = halves(modes)
    wide = dot(mh, spread) + dot(ml, spread)
    half = wide.shape[0] // 2
    re, im = wide[:half], wide[half:]
    wr, wi = w[0].astype(F32), w[1].astype(F32)
    mixed = jnp.concatenate([wr * re - wi * im, wr * im + wi * re], axis=0)
    both = lax.broadcasted_iota(jnp.int32, (pairs, lanes), 0)
    lane = lax.broadcasted_iota(jnp.int32, (pairs, lanes), 1) // zl
    gather = jnp.where(both % channels == lane, 1.0, 0.0).astype(BF)
    ph, plo = halves(mixed)
    summed = dot(ph, gather) + dot(plo, gather)
    row = lambda p, k: summed[(p * kl + k) * count : (p * kl + k + 1) * count]
    columns = [jnp.concatenate([row(0, k), row(1, k)], axis=0) for k in range(kl)]
    return triple(jnp.concatenate(columns, axis=1))


def spectrum_kernel(n_y, n_z, zl, *refs):
    (
        f_hbm, xt_hbm, yt_hbm, yi_hbm, zf_hbm, zi_hbm, w_hbm, r_hbm,
        f, xt, yt, yi, zf, zi, w, a, theirs, summing, arrived, total, seen, mixed, back, ring, planes,
        load_sem, swap_s, swap_r, sum_s, sum_r, out_s, out_r, in_s, in_r, ring_s, ring_r,
        turn_s, turn_r, keep_s,
    ) = refs
    here, column = lax.axis_index("py"), lax.axis_index("pz")
    n_ring = n_y // 2
    side, z = here // n_ring, here % n_ring
    other = 1 - side
    half_py = lambda s, at: s * n_ring + at % n_ring
    partner = {"py": half_py(other, z)}
    neighbours = ({"py": half_py(side, z + 1)}, {"py": half_py(side, z + n_ring - 1)})

    loads = []

    def load(source, target):
        copy = pltpu.make_async_copy(source, target, load_sem.at[len(loads)])
        copy.start()
        loads.append(copy)
        return copy

    pieces = 4
    rows = f.shape[1] // pieces
    table_x = load(xt_hbm, xt)
    fields = [
        load(f_hbm.at[:, pl.ds(i * rows, rows), :], f.at[:, pl.ds(i * rows, rows), :])
        for i in range(pieces)
    ]
    depth = yt_hbm.shape[3]
    table_y = [
        load(yt_hbm.at[half_py(s, z)], yt.at[:, :, pl.ds(i * depth, depth)])
        for i, s in enumerate((side, other))
    ]
    table_z = [load(zf_hbm, zf), load(w_hbm, w), load(zi_hbm, zi)]
    table_i = [load(yi_hbm.at[half_py(s, z)], yi.at[i]) for i, s in enumerate((side, other))]

    barrier = pltpu.get_barrier_semaphore()
    for peer in (partner,) + neighbours:
        pl.semaphore_signal(barrier, inc=1, device_id=peer, device_id_type=MESH)

    def greet(step, carry):
        pl.semaphore_signal(
            barrier, inc=1, device_id={"pz": (column + step) % n_z}, device_id_type=MESH
        )
        return carry

    lax.fori_loop(1, n_z, greet, 0)

    table_x.wait()
    turns = f.shape[1] // (2 * zl) // pieces
    for i in range(pieces):
        fields[i].wait()
        x_forward(zl, f, xt, a, i * turns, (i + 1) * turns)
    pl.semaphore_wait(barrier, n_z + 2)

    reach = n_ring // 2
    offsets = [reach] + [o * s for o in range(reach - 1, 0, -1) for s in (1, -1)] + [0]

    def swap(i):
        at = (z + offsets[i] + n_ring) % n_ring
        return pltpu.make_async_remote_copy(
            src_ref=a.at[half_py(other, at)],
            dst_ref=theirs.at[at],
            send_sem=swap_s.at[i],
            recv_sem=swap_r.at[i],
            device_id=partner,
            device_id_type=MESH,
        )

    for i in range(n_ring):
        swap(i).start()
    for copy in table_y:
        copy.wait()

    def partial(i):
        at = (z + offsets[i] + n_ring) % n_ring
        swap(i).wait_recv()
        block = jnp.concatenate([a[half_py(side, at)], theirs[at]], axis=0)
        high, low = halves(block)
        return dot3(yt[0], yt[1], high, low)

    part = total.shape[0] * total.shape[1] // GROUP
    span = lambda g: pl.ds(g * part, part)
    carries = lambda way, step, g: step > 0 or (g < GROUP // 2) == (way == 0)

    def hop(way, step, g):
        index = (way * reach + step) * GROUP + g
        return pltpu.make_async_remote_copy(
            src_ref=summing.at[way, step, span(g)],
            dst_ref=arrived.at[way, step, span(g)],
            send_sem=sum_s.at[index],
            recv_sem=sum_r.at[index],
            device_id=neighbours[way],
            device_id_type=MESH,
        )

    block = partial(0)
    for g in range(GROUP):
        way = 0 if g < GROUP // 2 else 1
        summing[way, 0, g * part : (g + 1) * part] = block[g * part : (g + 1) * part]
        hop(way, 0, g).start()
    for step in range(1, reach):
        for way in range(2):
            summing[way, step] = partial(2 * step - 1 + way)
        for g in range(GROUP):
            for way in range(2):
                if carries(way, step - 1, g):
                    hop(way, step - 1, g).wait_recv()
                    summing[way, step, span(g)] += arrived[way, step - 1, span(g)]
                hop(way, step, g).start()

    per = n_z // GROUP
    y_chip, place = column // GROUP, column % GROUP
    slot = place * per + y_chip
    last = partial(n_ring - 1)

    def to_owner(source, owner):
        return pltpu.make_async_remote_copy(
            src_ref=total.at[source],
            dst_ref=seen.at[column],
            send_sem=out_s.at[owner],
            recv_sem=out_r.at[column],
            device_id={"pz": owner},
            device_id_type=MESH,
        )

    def from_owner(owner):
        return pltpu.make_async_remote_copy(
            src_ref=total.at[0],
            dst_ref=seen.at[owner],
            send_sem=out_s.at[owner],
            recv_sem=out_r.at[owner],
            device_id={"pz": owner},
            device_id_type=MESH,
        )

    for g in range(GROUP):
        for way in range(2):
            hop(way, reach - 1, g).wait_recv()
        value = last[g * part : (g + 1) * part] + arrived[0, reach - 1, span(g)]
        value = value + arrived[1, reach - 1, span(g)]
        total[g * per : (g + 1) * per] = value.reshape(per, total.shape[1], total.shape[2])

        def send(i, carry):
            chip = (y_chip + i) % per
            owner = chip * GROUP + g

            @pl.when(owner != column)
            def _():
                to_owner(g * per + chip, owner).start()

            return carry

        lax.fori_loop(0, per, send, 0)
    seen[column] = total[slot]

    def collect(step, carry):
        from_owner((column + step) % n_z).wait()
        return carry

    for copy in table_z:
        copy.wait()
    lax.fori_loop(1, n_z, collect, 0)

    modes = middle(zl, seen, w, zf)
    lanes = seen.shape[2]
    kl = seen.shape[1] // 2
    inner = lax.broadcasted_iota(jnp.int32, (1, modes.shape[1]), 1) % zl

    def to_cells(source, peer, target, sender):
        return pltpu.make_async_remote_copy(
            src_ref=mixed.at[source],
            dst_ref=back.at[target],
            send_sem=in_s.at[peer],
            recv_sem=in_r.at[sender],
            device_id={"pz": peer},
            device_id_type=MESH,
        )

    for g in range(GROUP):
        value = dot(zi[g], modes)
        size = 2 * per
        cells = jnp.zeros((size, modes.shape[1]), F32)
        for i in range(zl):
            cells += jnp.where(inner == i, value[i * size : (i + 1) * size], 0.0)
        for p in range(2):
            for k in range(kl):
                mixed[g * per : (g + 1) * per, 2 * k + p, :] = cells[
                    p * per : (p + 1) * per, k * lanes : (k + 1) * lanes
                ]

        def send_back(i, carry):
            chip = (y_chip + i) % per
            peer = chip * GROUP + g

            @pl.when(peer != column)
            def _():
                to_cells(g * per + chip, peer, slot, column).start()

            return carry

        lax.fori_loop(0, per, send_back, 0)

    def end_back(step, carry):
        peer = (column + step) % n_z
        to_cells(0, peer, 0, peer).wait()
        return carry

    back[slot] = mixed[slot]
    for copy in table_i:
        copy.wait()
    lax.fori_loop(1, n_z, end_back, 0)

    wide = lambda g: pl.ds(g * per, per)
    passes = lambda way, step, g: step < reach - 1 or (g < GROUP // 2) == (way == 0)

    def relay(way, step, g):
        index = (way * reach + step) * GROUP + g
        source = back.at[wide(g)] if step == 0 else ring.at[way, step - 1, wide(g)]
        target = ring.at[0 if step == reach - 1 else way, step, wide(g)]
        return pltpu.make_async_remote_copy(
            src_ref=source,
            dst_ref=target,
            send_sem=ring_s.at[index],
            recv_sem=ring_r.at[index],
            device_id=neighbours[way],
            device_id_type=MESH,
        )

    def turn(i, owner):
        return pltpu.make_async_remote_copy(
            src_ref=planes.at[1, i],
            dst_ref=r_hbm.at[owner],
            send_sem=turn_s.at[i],
            recv_sem=turn_r.at[i],
            device_id=partner,
            device_id_type=MESH,
        )

    def keep(i, owner):
        return pltpu.make_async_copy(planes.at[0, i], r_hbm.at[owner], keep_s.at[i])

    def spread(i, offset, block):
        owner = half_py(side, z + offset + n_ring)
        high, low = halves(block.reshape(-1, block.shape[2]))
        planes[1, i] = dot3(yi[1, 0], yi[1, 1], high, low)
        turn(i, owner).start()
        planes[0, i] = dot3(yi[0, 0], yi[0, 1], high, low)
        keep(i, owner).start()

    for g in range(GROUP):
        for way in range(2):
            relay(way, 0, g).start()
    spread(0, 0, back[...])
    for step in range(1, reach):
        for g in range(GROUP):
            for way in range(2):
                relay(way, step - 1, g).wait_recv()
                if passes(way, step, g):
                    relay(way, step, g).start()
        for way in range(2):
            spread(2 * step - 1 + way, step if way else -step, ring[way, step - 1])
    for g in range(GROUP):
        for way in range(2):
            if passes(way, reach - 1, g):
                relay(way, reach - 1, g).wait_recv()
    spread(n_ring - 1, reach, ring[0, reach - 1])

    for i in range(n_ring):
        swap(i).wait_send()
    for step in range(reach):
        for g in range(GROUP):
            for way in range(2):
                if carries(way, step, g):
                    hop(way, step, g).wait_send()
                if passes(way, step, g):
                    relay(way, step, g).wait_send()
    for i in range(n_ring):
        keep(i, here).wait()
        turn(i, here).wait()


def x_inverse_kernel(zl, r_ref, f_ref, w_ref, b_ref, th_ref, tl_ref, o_ref, mix_ref, bias_ref):
    channels, rows, length = f_ref.shape
    lanes = channels * zl

    @pl.when(pl.program_id(0) == 0)
    def _():
        row = lax.broadcasted_iota(jnp.int32, (lanes, channels), 0) // zl
        column = lax.broadcasted_iota(jnp.int32, (lanes, channels), 1)
        pick = row == column
        ones = jnp.where(pick, 1.0, 0.0).astype(BF)
        left = dot(ones, w_ref[...], ((1,), (1,))).astype(BF)
        full = dot(left, ones, ((1,), (1,)))
        a = lax.broadcasted_iota(jnp.int32, (lanes, lanes), 0) % zl
        b = lax.broadcasted_iota(jnp.int32, (lanes, lanes), 1) % zl
        mix_ref[...] = jnp.where(a == b, full, 0.0).astype(BF)
        column = jnp.sum(jnp.where(pick, b_ref[...], 0.0), axis=1, keepdims=True)
        bias_ref[...] = jnp.broadcast_to(column, bias_ref.shape)

    block = f_ref[...].astype(F32)
    th, tl, mix, bias = th_ref[...], tl_ref[...], mix_ref[...], bias_ref[...]
    for y in range(rows // zl):
        spectrum = r_ref[:, y].reshape(-1, lanes)
        sh, sl = halves(spectrum)
        field = block[:, y * zl : (y + 1) * zl, :].reshape(lanes, length).astype(BF)
        first = ((0,), (0,))
        value = dot(jnp.concatenate([sh, sl], 0), th, first) + dot(sh, tl, first)
        value = value + dot(mix, field) + bias
        out = jax.nn.gelu(value).reshape(channels, zl, length)
        o_ref[:, y * zl : (y + 1) * zl, :] = out.astype(o_ref.dtype)


def params(mib):
    return pltpu.CompilerParams(vmem_limit_bytes=mib * MIB)


def whole(shape):
    return pl.BlockSpec(shape, lambda i: (0,) * len(shape))


def per_device(tables, n_y, n_z, features, spectral_weight, bypass_weight, bias_vector):
    xf, xi, yf, yi, zf, zi = tables
    c, yl, zl, nx = features.shape
    _, kl, _, mz, pairs = spectral_weight.shape
    lanes = c * zl
    part = 2 * kl
    rows = yl * part
    flat = features.reshape(c, yl * zl, nx)
    x_rows = split(xf).reshape(-1, nx)
    y_rows, y_back = split(yf, 1), split(yi, 1)
    z_rows, z_back = thrice(zf), thrice(zi)
    weight = spectral_weight.reshape(2, kl * mz, pairs)
    my_rows = y_rows.shape[2]
    modes = my_rows // part
    n_ring = n_y // 2
    reach = n_ring // 2
    operands = [flat] + [jnp.asarray(t) for t in (x_rows, y_rows, y_back, z_rows, z_back)] + [weight]
    sems = [16, n_ring, n_ring] + [2 * reach * GROUP] * 2 + [n_z] * 4 + [2 * reach * GROUP] * 2
    sems += [n_ring] * 3
    planes = pl.pallas_call(
        functools.partial(spectrum_kernel, n_y, n_z, zl),
        out_shape=jax.ShapeDtypeStruct((n_y, rows, lanes), F32),
        in_specs=[pl.BlockSpec(memory_space=pl.ANY)] * len(operands),
        out_specs=pl.BlockSpec(memory_space=pl.ANY),
        scratch_shapes=[
            pltpu.VMEM(flat.shape, BF),
            pltpu.VMEM(x_rows.shape, BF),
            pltpu.VMEM((2, my_rows, 2 * rows), BF),
            pltpu.VMEM((2,) + y_back.shape[1:], BF),
            pltpu.VMEM(z_rows.shape, BF),
            pltpu.VMEM(z_back.shape, BF),
            pltpu.VMEM(weight.shape, BF),
            pltpu.VMEM((n_y, rows, lanes), F32),
            pltpu.VMEM((n_ring, rows, lanes), F32),
            pltpu.VMEM((2, reach, my_rows, lanes), F32),
            pltpu.VMEM((2, reach, my_rows, lanes), F32),
            pltpu.VMEM((modes, part, lanes), F32),
            pltpu.VMEM((n_z, part, lanes), F32),
            pltpu.VMEM((n_z, part, lanes), F32),
            pltpu.VMEM((modes, part, lanes), F32),
            pltpu.VMEM((2, reach, modes, part, lanes), F32),
            pltpu.VMEM((2, n_ring, rows, lanes), F32),
        ]
        + [pltpu.SemaphoreType.DMA((n,)) for n in sems],
        compiler_params=pltpu.CompilerParams(
            collective_id=0, has_side_effects=True, vmem_limit_bytes=62 * MIB
        ),
        name="spectrum",
    )(*operands)

    step = 4
    steps = yl // step
    field_spec = pl.BlockSpec((c, step * zl, nx), lambda i: (0, i, 0))
    high, tl = split(xi)
    th = np.concatenate([high, high], 0)
    out = pl.pallas_call(
        functools.partial(x_inverse_kernel, zl),
        grid=(steps,),
        in_specs=[
            pl.BlockSpec((n_y, step, part, lanes), lambda i: (0, i, 0, 0)),
            field_spec,
            whole(bypass_weight.shape),
            whole((1, c)),
            whole(th.shape),
            whole(tl.shape),
        ],
        out_specs=field_spec,
        out_shape=jax.ShapeDtypeStruct(flat.shape, BF),
        scratch_shapes=[pltpu.VMEM((lanes, lanes), BF), pltpu.VMEM((lanes, nx), F32)],
        compiler_params=params(62),
        name="x_inverse",
    )(planes.reshape(n_y, yl, part, lanes), flat, bypass_weight, bias_vector.reshape(1, c), jnp.asarray(th), jnp.asarray(tl))
    return out.reshape(features.shape)


def solution(mesh):
    n_y, n_z = mesh.shape["py"], mesh.shape["pz"]

    def run(features, spectral_weight, bypass_weight, bias_vector):
        _, ny, nz, nx = features.shape
        _, mx, my, mz, _ = spectral_weight.shape
        tables = make_tables(nx, ny, nz, mx, my, mz, n_y, n_z)
        return jax.shard_map(
            functools.partial(per_device, tables, n_y, n_z),
            mesh=mesh,
            in_specs=(P(None, "py", "pz", None), P(None, "py", "pz", None, None), P(), P()),
            out_specs=P(None, "py", "pz", None),
            check_vma=False,
        )(features, spectral_weight, bypass_weight, bias_vector)

    return run
```

```python
import functools
import math

import jax
import jax.numpy as jnp
import ml_dtypes
import numpy as np
from jax import lax
from jax.experimental import pallas as pl
from jax.experimental.pallas import tpu as pltpu
from jax.sharding import PartitionSpec as P

MESH = pl.DeviceIdType.MESH
BF = jnp.bfloat16
F32 = jnp.float32
MIB = 1 << 20
HALVES = 2
GROUP = 4


def centred(count):
    index = np.arange(count)
    return np.where(index < count // 2, index, index - count)


def split(table, axis=0):
    high = table.astype(ml_dtypes.bfloat16)
    low = (table - high.astype(np.float64)).astype(ml_dtypes.bfloat16)
    return np.stack([high, low], axis)


def thrice(table):
    high, low = split(table)
    return np.concatenate([high, high, low], -1)


def pair(frequencies, positions, period, sign):
    angle = 2.0 * np.pi * ((positions[:, None] * frequencies[None, :]) % period) / period
    c, s = np.cos(angle), np.sin(angle)
    return np.stack([np.stack([c, sign * s]), np.stack([-sign * s, c])])


def make_tables(nx, ny, nz, mx, my, mz, py, pz):
    k = mx // py
    zl = nz // pz
    yl = ny // py
    norm = 1.0 / math.sqrt(nx * ny * nz)
    angle = 2.0 * np.pi * ((np.arange(mx)[:, None] * np.arange(nx)[None, :]) % nx) / nx
    eye = np.eye(k)
    xf = np.stack([np.cos(angle) * norm, -np.sin(angle) * norm], 1).reshape(2 * mx, nx)
    weight = np.where(np.arange(mx) == 0, 1.0, 2.0)[:, None] * norm
    xi = np.stack([np.cos(angle) * weight, -np.sin(angle) * weight], 1).reshape(2 * mx, nx)
    order = np.arange(my).reshape(pz // GROUP, GROUP).T.reshape(-1)
    yf = pair(centred(my), np.arange(ny), ny, -1.0)[..., order].reshape(2, 2, py, yl, my)
    yf = np.einsum("pqdyj,kl->djkqylp", yf, eye).reshape(py, my * k * 2, yl * k * 2)
    yi = pair(centred(my), np.arange(ny), ny, 1.0)[..., order].reshape(2, 2, py, yl, my)
    yi = np.einsum("qrdyj,kl->dykrjlq", yi, eye).reshape(py, yl * k * 2, my * k * 2)
    zf = pair(centred(mz), np.arange(nz), nz, -1.0).reshape(2, 2, pz, zl, mz)
    zf = np.einsum("pqszm->zqmps", zf).reshape(zl, 2 * mz, 2 * pz)
    zi = pair(centred(mz), np.arange(nz), nz, 1.0).reshape(2, 2, pz // GROUP, GROUP, zl, mz)
    zi = np.einsum("qrjgzm->gzrjqm", zi).reshape(GROUP, zl * 2 * pz // GROUP, 2 * mz)
    return xf, xi, yf, yi, zf, zi


def halves(value):
    high = value.astype(BF)
    return high, (value - high.astype(F32)).astype(BF)


def triple(value):
    high, low = halves(value)
    return jnp.concatenate([high, low, high], 0)


def dot(a, b, dims=((1,), (0,))):
    return lax.dot_general(a, b, (dims, ((), ())), preferred_element_type=F32)


def dot3(ah, al, bh, bl):
    return dot(ah, bh) + dot(al, bh) + dot(ah, bl)


def x_forward(zl, field, table, out, h, first, last):
    channels = field.shape[0] // HALVES
    rows = out.shape[2] // (field.shape[1] // zl)

    def step(i, carry):
        start = pl.multiple_of(i * 2 * zl, 2 * zl)
        block = field[h * channels : (h + 1) * channels, pl.ds(start, 2 * zl), :].astype(F32)
        for y in range(2):
            plane = block[:, y * zl : (y + 1) * zl, :].reshape(channels * zl, -1).astype(BF)
            both = dot(table[...], plane, ((1,), (1,)))
            half = both.shape[0] // 2
            at = pl.multiple_of((i * 2 + y) * rows, rows)
            out[h, :, pl.ds(at, rows), :] = (both[:half] + both[half:]).reshape(
                out.shape[1], rows, out.shape[3]
            )
        return carry

    lax.fori_loop(first, last, step, 0)


def mix_modes(zl, x, w, forward, h):
    cells, part, lanes = x.shape
    kl = part // 2
    channels = lanes // zl
    column = lambda k: jnp.concatenate([x[:, 2 * k, :], x[:, 2 * k + 1, :]], axis=0)
    block = triple(jnp.concatenate([column(k) for k in range(kl)], axis=1))
    inner = lax.broadcasted_iota(jnp.int32, (1, kl * lanes), 1) % zl
    modes = jnp.zeros((forward.shape[1], kl * lanes), F32)
    for z in range(zl):
        modes += jnp.where(inner == z, dot(forward[z], block), 0.0)
    count = modes.shape[0] // 2
    modes = jnp.concatenate(
        [
            modes[p * count : (p + 1) * count, k * lanes : (k + 1) * lanes]
            for p in range(2)
            for k in range(kl)
        ],
        axis=0,
    )
    outs = channels * HALVES
    pairs = channels * outs
    lane = lax.broadcasted_iota(jnp.int32, (lanes, pairs), 0) // zl
    both = lax.broadcasted_iota(jnp.int32, (lanes, pairs), 1)
    spread = jnp.where(lane == both // outs, 1.0, 0.0).astype(BF)
    mh, ml = halves(modes)
    wide = dot(mh, spread) + dot(ml, spread)
    half = wide.shape[0] // 2
    re, im = wide[:half], wide[half:]
    wr = w[0, :, h * pairs : (h + 1) * pairs].astype(F32)
    wi = w[1, :, h * pairs : (h + 1) * pairs].astype(F32)
    mixed = jnp.concatenate([wr * re - wi * im, wr * im + wi * re], axis=0)
    both = lax.broadcasted_iota(jnp.int32, (pairs, outs * zl), 0)
    lane = lax.broadcasted_iota(jnp.int32, (pairs, outs * zl), 1) // zl
    gather = jnp.where(both % outs == lane, 1.0, 0.0).astype(BF)
    ph, plo = halves(mixed)
    return dot(ph, gather) + dot(plo, gather)


def bypass_rows(zl, h, w, bias):
    channels = w.shape[0]
    outs = channels // HALVES

    def picks(rows, first):
        row = lax.broadcasted_iota(jnp.int32, (rows * zl, channels), 0) // zl + first
        return row == lax.broadcasted_iota(jnp.int32, (rows * zl, channels), 1)

    pick = picks(outs, h * outs)
    ones = lambda p: jnp.where(p, 1.0, 0.0).astype(BF)
    left = dot(ones(pick), w[...], ((1,), (1,))).astype(BF)
    full = dot(left, ones(picks(channels, 0)), ((1,), (1,)))
    a = lax.broadcasted_iota(jnp.int32, full.shape, 0) % zl
    b = lax.broadcasted_iota(jnp.int32, full.shape, 1) % zl
    column = jnp.sum(jnp.where(pick, bias[...], 0.0), axis=1, keepdims=True)
    return jnp.where(a == b, full, 0.0).astype(BF), column


def field_rows(zl, spectrum, plane, mix, column, th, tl):
    high, low = halves(spectrum)
    first = ((0,), (0,))
    value = dot(jnp.concatenate([high, low], 0), th, first) + dot(high, tl, first)
    value = value + dot(mix, plane) + column
    return jax.nn.gelu(value).reshape(-1, zl, value.shape[1])


def spectrum_kernel(n_y, n_z, zl, *refs):
    (
        f_hbm, xt_hbm, yt_hbm, yi_hbm, zf_hbm, zi_hbm, w_hbm, th_hbm, tl_hbm, bypass, bias,
        r_hbm, o_hbm,
        f, xt, yt, yi, zf, zi, w, th, tl, mix, shift, a, theirs, summing, arrived, total, seen,
        mixed, back, ring, leaving, keeping, mine, done,
        load_sem, swap_s, swap_r, sum_s, sum_r, out_s, out_r, in_s, in_r, ring_s, ring_r,
        turn_s, turn_r, keep_s, done_s,
    ) = refs
    here, column = lax.axis_index("py"), lax.axis_index("pz")
    n_ring = n_y // 2
    side, z = here // n_ring, here % n_ring
    other = 1 - side
    half_py = lambda s, at: s * n_ring + at % n_ring
    partner = {"py": half_py(other, z)}
    neighbours = ({"py": half_py(side, z + 1)}, {"py": half_py(side, z + n_ring - 1)})

    barrier = pltpu.get_barrier_semaphore()
    for peer in (partner,) + neighbours:
        pl.semaphore_signal(barrier, inc=1, device_id=peer, device_id_type=MESH)

    def greet(step, carry):
        pl.semaphore_signal(
            barrier, inc=1, device_id={"pz": (column + step) % n_z}, device_id_type=MESH
        )
        return carry

    loads = []

    def load(source, target):
        copy = pltpu.make_async_copy(source, target, load_sem.at[len(loads)])
        copy.start()
        loads.append(copy)
        return copy

    pieces = 2
    rows = f.shape[1] // pieces
    channels = f.shape[0] // HALVES
    table_x = load(xt_hbm, xt)
    fields = []
    for h in range(HALVES):
        for i in range(pieces):
            at = (pl.ds(h * channels, channels), pl.ds(i * rows, rows), slice(None))
            fields.append(load(f_hbm.at[at], f.at[at]))
    depth = yt_hbm.shape[3]
    table_y = [
        load(yt_hbm.at[half_py(s, z)], yt.at[:, :, pl.ds(i * depth, depth)])
        for i, s in enumerate((side, other))
    ]
    table_z = [load(zf_hbm, zf), load(w_hbm, w)]
    table_b = [load(zi_hbm, zi)]
    table_i = [load(yi_hbm.at[half_py(s, z)], yi.at[i]) for i, s in enumerate((side, other))]
    table_f = [load(th_hbm, th), load(tl_hbm, tl)]
    lax.fori_loop(1, n_z, greet, 0)

    reach = n_ring // 2
    offsets = [reach] + [o * s for o in range(reach - 1, 0, -1) for s in (1, -1)] + [0]

    def swap(h, i):
        at = (z + offsets[i] + n_ring) % n_ring
        return pltpu.make_async_remote_copy(
            src_ref=a.at[h, half_py(other, at)],
            dst_ref=theirs.at[h, at],
            send_sem=swap_s.at[h * n_ring + i],
            recv_sem=swap_r.at[h * n_ring + i],
            device_id=partner,
            device_id_type=MESH,
        )

    table_x.wait()
    turns = f.shape[1] // (2 * zl) // pieces
    for h in range(HALVES):
        for i in range(pieces):
            fields[h * pieces + i].wait()
            x_forward(zl, f, xt, a, h, i * turns, (i + 1) * turns)
        if h == 0:
            pl.semaphore_wait(barrier, n_z + 2)
        for i in range(n_ring):
            swap(h, i).start()
    for copy in table_y:
        copy.wait()

    def partial(h, i):
        at = (z + offsets[i] + n_ring) % n_ring
        swap(h, i).wait_recv()
        block = jnp.concatenate([a[h, half_py(side, at)], theirs[h, at]], axis=0)
        high, low = halves(block)
        return dot3(yt[0], yt[1], high, low)

    part = total.shape[1] * total.shape[2] // GROUP
    span = lambda g: pl.ds(g * part, part)
    carries = lambda way, step, g: step > 0 or (g < GROUP // 2) == (way == 0)

    def hop(h, way, step, g):
        index = ((h * 2 + way) * reach + step) * GROUP + g
        return pltpu.make_async_remote_copy(
            src_ref=summing.at[h, way, step, span(g)],
            dst_ref=arrived.at[h, way, step, span(g)],
            send_sem=sum_s.at[index],
            recv_sem=sum_r.at[index],
            device_id=neighbours[way],
            device_id_type=MESH,
        )

    def set_out(h):
        block = partial(h, 0)
        for g in range(GROUP):
            way = 0 if g < GROUP // 2 else 1
            summing[h, way, 0, g * part : (g + 1) * part] = block[g * part : (g + 1) * part]
            hop(h, way, 0, g).start()

    def move_on(h, step):
        for way in range(2):
            summing[h, way, step] = partial(h, 2 * step - 1 + way)
        for g in range(GROUP):
            for way in range(2):
                if carries(way, step - 1, g):
                    hop(h, way, step - 1, g).wait_recv()
                    summing[h, way, step, span(g)] += arrived[h, way, step - 1, span(g)]
                hop(h, way, step, g).start()

    per = n_z // GROUP
    y_chip, place = column // GROUP, column % GROUP
    slot = place * per + y_chip

    def to_owner(h, source, owner, target):
        return pltpu.make_async_remote_copy(
            src_ref=total.at[h, source],
            dst_ref=seen.at[h, target],
            send_sem=out_s.at[h * n_z + owner],
            recv_sem=out_r.at[h * n_z + target],
            device_id={"pz": owner},
            device_id_type=MESH,
        )

    def arrive(h):
        last = partial(h, n_ring - 1)
        for g in range(GROUP):
            for way in range(2):
                hop(h, way, reach - 1, g).wait_recv()
            value = last[g * part : (g + 1) * part] + arrived[h, 0, reach - 1, span(g)]
            value = value + arrived[h, 1, reach - 1, span(g)]
            total[h, g * per : (g + 1) * per] = value.reshape((per,) + total.shape[2:])

            def send(i, carry):
                chip = (y_chip + i) % per
                owner = chip * GROUP + g

                @pl.when(owner != column)
                def _():
                    to_owner(h, g * per + chip, owner, column).start()

                return carry

            lax.fori_loop(0, per, send, 0)
        seen[h, column] = total[h, slot]

    def collect(h):
        def one(step, carry):
            peer = (column + step) % n_z
            to_owner(h, 0, peer, peer).wait()
            return carry

        lax.fori_loop(1, n_z, one, 0)

    set_out(0)
    for step in range(1, reach):
        move_on(0, step)
    set_out(1)
    arrive(0)
    for step in range(1, reach):
        move_on(1, step)
    for copy in table_z:
        copy.wait()
    collect(0)
    summed = mix_modes(zl, seen.at[0], w, zf, 0)
    arrive(1)
    rows_mix, rows_bias = bypass_rows(zl, 0, bypass, bias)
    mix[...] = rows_mix
    shift[...] = jnp.broadcast_to(rows_bias, shift.shape)
    for copy in table_b:
        copy.wait()
    collect(1)
    summed = summed + mix_modes(zl, seen.at[1], w, zf, 1)

    lanes = seen.shape[3]
    kl = seen.shape[2] // 2
    count = summed.shape[0] // (2 * kl)
    inner = lax.broadcasted_iota(jnp.int32, (1, kl * lanes), 1) % zl

    def to_cells(h, source, peer, target, sender):
        return pltpu.make_async_remote_copy(
            src_ref=mixed.at[h, source],
            dst_ref=back.at[h, target],
            send_sem=in_s.at[h * n_z + peer],
            recv_sem=in_r.at[h * n_z + sender],
            device_id={"pz": peer},
            device_id_type=MESH,
        )

    for h in range(HALVES):
        row = lambda p, k: summed[
            (p * kl + k) * count : (p * kl + k + 1) * count, h * lanes : (h + 1) * lanes
        ]
        columns = [jnp.concatenate([row(0, k), row(1, k)], axis=0) for k in range(kl)]
        modes = triple(jnp.concatenate(columns, axis=1))
        for g in range(GROUP):
            value = dot(zi[g], modes)
            size = 2 * per
            cells = jnp.zeros((size, modes.shape[1]), F32)
            for i in range(zl):
                cells += jnp.where(inner == i, value[i * size : (i + 1) * size], 0.0)
            for p in range(2):
                for k in range(kl):
                    mixed[h, g * per : (g + 1) * per, 2 * k + p, :] = cells[
                        p * per : (p + 1) * per, k * lanes : (k + 1) * lanes
                    ]

            def send_back(i, carry):
                chip = (y_chip + i) % per
                peer = chip * GROUP + g

                @pl.when(peer != column)
                def _():
                    to_cells(h, g * per + chip, peer, slot, column).start()

                return carry

            lax.fori_loop(0, per, send_back, 0)
        back[h, slot] = mixed[h, slot]

    def end_back(h):
        def one(step, carry):
            peer = (column + step) % n_z
            to_cells(h, 0, peer, 0, peer).wait()
            return carry

        lax.fori_loop(1, n_z, one, 0)

    wide = lambda g: pl.ds(g * per, per)
    passes = lambda way, step, g: step < reach - 1 or (g < GROUP // 2) == (way == 0)

    def relay(h, way, step, g):
        index = ((h * 2 + way) * reach + step) * GROUP + g
        source = back.at[h, wide(g)] if step == 0 else ring.at[h, way, step - 1, wide(g)]
        target = ring.at[h, 0 if step == reach - 1 else way, step, wide(g)]
        return pltpu.make_async_remote_copy(
            src_ref=source,
            dst_ref=target,
            send_sem=ring_s.at[index],
            recv_sem=ring_r.at[index],
            device_id=neighbours[way],
            device_id_type=MESH,
        )

    def turn(h, i, owner):
        return pltpu.make_async_remote_copy(
            src_ref=leaving.at[h, i],
            dst_ref=(mine if h == 0 else r_hbm).at[owner],
            send_sem=turn_s.at[h * n_ring + i],
            recv_sem=turn_r.at[h * n_ring + i],
            device_id=partner,
            device_id_type=MESH,
        )

    def keep(i, owner):
        return pltpu.make_async_copy(keeping.at[i], r_hbm.at[owner], keep_s.at[i])

    def spread(h, i, offset, block):
        owner = half_py(side, z + offset + n_ring)
        high, low = halves(block.reshape(-1, block.shape[2]))
        leaving[h, i] = dot3(yi[1, 0], yi[1, 1], high, low)
        turn(h, i, owner).start()
        own = dot3(yi[0, 0], yi[0, 1], high, low)
        if h == 0:
            mine[owner] = own
        else:
            keeping[i] = own
            keep(i, owner).start()

    def send_own(h):
        for g in range(GROUP):
            for way in range(2):
                relay(h, way, 0, g).start()

    def pass_on(h, step):
        for g in range(GROUP):
            for way in range(2):
                if passes(way, step - 1, g):
                    relay(h, way, step - 1, g).wait_recv()
                if step < reach and passes(way, step, g):
                    relay(h, way, step, g).start()

    def spread_pair(h, step):
        if step == reach:
            spread(h, n_ring - 1, reach, ring[h, 0, reach - 1])
        else:
            for way in range(2):
                spread(h, 2 * step - 1 + way, step if way else -step, ring[h, way, step - 1])

    strip = f.shape[1] // reach
    strip_at = lambda i: (slice(None), pl.ds(i * strip, strip), slice(None))

    def finished(i):
        return pltpu.make_async_copy(done.at[strip_at(i)], o_hbm.at[strip_at(i)], done_s.at[i])

    def finish(number):
        def one(i, carry):
            at = pl.ds(pl.multiple_of(i * 2 * zl, 2 * zl), 2 * zl)
            block = f[:, at, :].astype(F32)
            made = []
            for y in range(2):
                plane = block[:, y * zl : (y + 1) * zl, :].reshape(-1, block.shape[2]).astype(BF)
                depth = leaving.shape[2] * zl // f.shape[1]
                start = pl.multiple_of((i * 2 + y) * depth, depth)
                values = mine[:, pl.ds(start, depth), :].reshape(-1, lanes)
                made.append(field_rows(zl, values, plane, mix[...], shift[...], th[...], tl[...]))
            done[:, at, :] = jnp.concatenate(made, axis=1).astype(BF)
            return carry

        each = strip // (2 * zl)
        lax.fori_loop(number * each, (number + 1) * each, one, 0)
        finished(number).start()

    for copy in table_i:
        copy.wait()
    end_back(0)
    send_own(0)
    spread(0, 0, 0, back[0])
    end_back(1)
    spread(1, 0, 0, back[1])
    pass_on(0, 1)
    send_own(1)
    spread_pair(0, 1)
    pass_on(0, 2)
    spread_pair(0, 2)
    pass_on(1, 1)
    for step in range(3, reach):
        pass_on(0, step)
        spread_pair(0, step)
    pass_on(0, reach)
    spread_pair(0, reach)
    spread_pair(1, 1)
    pass_on(1, 2)
    spread_pair(1, 2)
    for copy in table_f:
        copy.wait()
    for i in range(n_ring):
        turn(0, i, here).wait_recv()
    finish(0)
    for step in range(3, reach):
        pass_on(1, step)
        spread_pair(1, step)
    finish(1)
    pass_on(1, reach)
    spread_pair(1, reach)
    for i in range(2, reach):
        finish(i)

    for h in range(HALVES):
        for i in range(n_ring):
            swap(h, i).wait_send()
        for step in range(reach):
            for g in range(GROUP):
                for way in range(2):
                    if carries(way, step, g):
                        hop(h, way, step, g).wait_send()
                    if passes(way, step, g):
                        relay(h, way, step, g).wait_send()
    for i in range(n_ring):
        turn(0, i, here).wait_send()
        keep(i, here).wait()
        turn(1, i, here).wait()
    for i in range(reach):
        finished(i).wait()


def field_kernel(zl, r_ref, f_ref, o_first, w_ref, b_ref, th_ref, tl_ref, o_ref, mix, shift):
    @pl.when(pl.program_id(0) == 0)
    def _():
        rows_mix, rows_bias = bypass_rows(zl, 1, w_ref, b_ref)
        mix[...] = rows_mix
        shift[...] = jnp.broadcast_to(rows_bias, shift.shape)

    outs = o_first.shape[0]
    o_ref[:outs] = o_first[...]
    block = f_ref[...].astype(F32)
    for y in range(f_ref.shape[1] // zl):
        plane = block[:, y * zl : (y + 1) * zl, :].reshape(-1, block.shape[2]).astype(BF)
        values = r_ref[:, y].reshape(-1, r_ref.shape[3])
        made = field_rows(zl, values, plane, mix[...], shift[...], th_ref[...], tl_ref[...])
        o_ref[outs:, y * zl : (y + 1) * zl, :] = made.astype(BF)


def whole(shape):
    return pl.BlockSpec(shape, lambda i: (0,) * len(shape))


def per_device(tables, n_y, n_z, features, spectral_weight, bypass_weight, bias_vector):
    xf, xi, yf, yi, zf, zi = tables
    c, yl, zl, nx = features.shape
    _, kl, _, mz, pairs = spectral_weight.shape
    outs = c // HALVES
    lanes = outs * zl
    part = 2 * kl
    rows = yl * part
    flat = features.reshape(c, yl * zl, nx)
    x_rows = split(xf).reshape(-1, nx)
    y_rows, y_back = split(yf, 1), split(yi, 1)
    z_rows, z_back = thrice(zf), thrice(zi)
    high, tl = split(xi)
    th = np.concatenate([high, high], 0)
    weight = spectral_weight.reshape(2, kl * mz, pairs)
    bias = bias_vector.reshape(1, c)
    my_rows = y_rows.shape[2]
    modes = my_rows // part
    n_ring = n_y // 2
    reach = n_ring // 2
    th, tl = jnp.asarray(th), jnp.asarray(tl)
    operands = [flat] + [jnp.asarray(t) for t in (x_rows, y_rows, y_back, z_rows, z_back)]
    operands += [weight, th, tl]
    hops = HALVES * 2 * reach * GROUP
    sems = [20] + [HALVES * n_ring] * 2 + [hops] * 2 + [HALVES * n_z] * 4 + [hops] * 2
    sems += [HALVES * n_ring] * 2 + [n_ring, reach]
    planes, ready = pl.pallas_call(
        functools.partial(spectrum_kernel, n_y, n_z, zl),
        out_shape=(
            jax.ShapeDtypeStruct((n_y, rows, lanes), F32),
            jax.ShapeDtypeStruct((outs, yl * zl, nx), BF),
        ),
        in_specs=[pl.BlockSpec(memory_space=pl.ANY)] * len(operands)
        + [pl.BlockSpec(memory_space=pltpu.VMEM)] * 2,
        out_specs=(pl.BlockSpec(memory_space=pl.ANY), pl.BlockSpec(memory_space=pl.ANY)),
        scratch_shapes=[
            pltpu.VMEM(flat.shape, BF),
            pltpu.VMEM(x_rows.shape, BF),
            pltpu.VMEM((2, my_rows, 2 * rows), BF),
            pltpu.VMEM((2,) + y_back.shape[1:], BF),
            pltpu.VMEM(z_rows.shape, BF),
            pltpu.VMEM(z_back.shape, BF),
            pltpu.VMEM(weight.shape, BF),
            pltpu.VMEM(th.shape, BF),
            pltpu.VMEM(tl.shape, BF),
            pltpu.VMEM((lanes, c * zl), BF),
            pltpu.VMEM((lanes, nx), F32),
            pltpu.VMEM((HALVES, n_y, rows, lanes), F32),
            pltpu.VMEM((HALVES, n_ring, rows, lanes), F32),
            pltpu.VMEM((HALVES, 2, reach, my_rows, lanes), F32),
            pltpu.VMEM((HALVES, 2, reach, my_rows, lanes), F32),
            pltpu.VMEM((HALVES, modes, part, lanes), F32),
            pltpu.VMEM((HALVES, n_z, part, lanes), F32),
            pltpu.VMEM((HALVES, n_z, part, lanes), F32),
            pltpu.VMEM((HALVES, modes, part, lanes), F32),
            pltpu.VMEM((HALVES, 2, reach, modes, part, lanes), F32),
            pltpu.VMEM((HALVES, n_ring, rows, lanes), F32),
            pltpu.VMEM((n_ring, rows, lanes), F32),
            pltpu.VMEM((n_y, rows, lanes), F32),
            pltpu.VMEM((outs, yl * zl, nx), BF),
        ]
        + [pltpu.SemaphoreType.DMA((n,)) for n in sems],
        compiler_params=pltpu.CompilerParams(
            collective_id=0, has_side_effects=True, vmem_limit_bytes=62 * MIB
        ),
        name="spectrum",
    )(*operands, bypass_weight, bias)

    step = 4
    block = lambda count: pl.BlockSpec((count, step * zl, nx), lambda i: (0, i, 0))
    out = pl.pallas_call(
        functools.partial(field_kernel, zl),
        grid=(yl // step,),
        in_specs=[
            pl.BlockSpec((n_y, step, part, lanes), lambda i: (0, i, 0, 0)),
            block(c),
            block(outs),
            whole(bypass_weight.shape),
            whole(bias.shape),
            whole(th.shape),
            whole(tl.shape),
        ],
        out_specs=block(c),
        out_shape=jax.ShapeDtypeStruct(flat.shape, BF),
        scratch_shapes=[pltpu.VMEM((lanes, c * zl), BF), pltpu.VMEM((lanes, nx), F32)],
        compiler_params=pltpu.CompilerParams(vmem_limit_bytes=62 * MIB),
        name="field",
    )(planes.reshape(n_y, yl, part, lanes), flat, ready, bypass_weight, bias, th, tl)
    return out.reshape(features.shape)


def solution(mesh):
    n_y, n_z = mesh.shape["py"], mesh.shape["pz"]

    def run(features, spectral_weight, bypass_weight, bias_vector):
        _, ny, nz, nx = features.shape
        _, mx, my, mz, _ = spectral_weight.shape
        tables = make_tables(nx, ny, nz, mx, my, mz, n_y, n_z)
        return jax.shard_map(
            functools.partial(per_device, tables, n_y, n_z),
            mesh=mesh,
            in_specs=(P(None, "py", "pz", None), P(None, "py", "pz", None, None), P(), P()),
            out_specs=P(None, "py", "pz", None),
            check_vma=False,
        )(features, spectral_weight, bypass_weight, bias_vector)

    return run
```

```python
import functools
import math

import jax
import jax.numpy as jnp
import ml_dtypes
import numpy as np
from jax import lax
from jax.experimental import pallas as pl
from jax.experimental.pallas import tpu as pltpu
from jax.sharding import PartitionSpec as P

MESH = pl.DeviceIdType.MESH
BF = jnp.bfloat16
F32 = jnp.float32
MIB = 1 << 20
PARTS = 2
LH = 2
GROUP = 4


def centred(count):
    index = np.arange(count)
    return np.where(index < count // 2, index, index - count)


def split(table, axis=0):
    high = table.astype(ml_dtypes.bfloat16)
    low = (table - high.astype(np.float64)).astype(ml_dtypes.bfloat16)
    return np.stack([high, low], axis)


def thrice(table):
    high, low = split(table)
    return np.concatenate([high, high, low], -1)


def pair(frequencies, positions, period, sign):
    angle = 2.0 * np.pi * ((positions[:, None] * frequencies[None, :]) % period) / period
    c, s = np.cos(angle), np.sin(angle)
    return np.stack([np.stack([c, sign * s]), np.stack([-sign * s, c])])


def make_tables(nx, ny, nz, mx, my, mz, py, pz):
    k = mx // py
    zl = nz // pz
    yl = ny // py
    norm = 1.0 / math.sqrt(nx * ny * nz)
    angle = 2.0 * np.pi * ((np.arange(mx)[:, None] * np.arange(nx)[None, :]) % nx) / nx
    kp = k // PARTS
    eye, pairs = np.eye(kp), np.eye(2)
    xf = np.stack([np.cos(angle) * norm, -np.sin(angle) * norm], 1)
    xf = xf.reshape(py, PARTS, kp, 2, nx)
    xf = np.einsum("dtkpx,yw->tdykpwx", xf, pairs).reshape(PARTS, py * 4 * kp, 2 * nx)
    weight = np.where(np.arange(mx) == 0, 1.0, 2.0)[:, None] * norm
    xi = np.stack([np.cos(angle) * weight, -np.sin(angle) * weight], 1)
    xi = xi.reshape(py, PARTS, kp, 2, nx).swapaxes(0, 1).reshape(2 * mx, nx)
    order = np.arange(my).reshape(pz // GROUP, GROUP).T.reshape(-1)
    yf = pair(centred(my), np.arange(ny), ny, -1.0)[..., order].reshape(2, 2, py, yl, my)
    yf = np.einsum("pqdyj,kl,hg->djhkqgylp", yf, eye, pairs)
    yf = yf.reshape(py, my * 4 * kp, yl * 4 * kp)
    yi = pair(centred(my), np.arange(ny), ny, 1.0)[..., order].reshape(2, 2, py, yl, my)
    yi = np.einsum("qrdyj,kl,hg->dhkryjglq", yi, eye, pairs)
    yi = yi.reshape(py, yl * 4 * kp, my * 4 * kp)
    zf = pair(centred(mz), np.arange(nz), nz, -1.0).reshape(2, 2, pz, zl, mz)
    zf = np.einsum("pqszm->zqmps", zf).reshape(zl, 2 * mz, 2 * pz)
    zi = pair(centred(mz), np.arange(nz), nz, 1.0).reshape(2, 2, pz // GROUP, GROUP, zl, mz)
    zi = np.einsum("qrjgzm->gzrjqm", zi).reshape(GROUP, zl * 2 * pz // GROUP, 2 * mz)
    return xf, xi, yf, yi, zf, zi


def halves(value):
    high = value.astype(BF)
    return high, (value - high.astype(F32)).astype(BF)


def triple(value):
    high, low = halves(value)
    return jnp.concatenate([high, low, high], 0)


def dot(a, b, dims=((1,), (0,))):
    return lax.dot_general(a, b, (dims, ((), ())), preferred_element_type=F32)


def dot3(ah, al, bh, bl):
    return dot(ah, bh) + dot(al, bh) + dot(ah, bl)


def x_forward(zl, field, table, out, t, first, last):
    length = field.shape[2]

    def step(i, carry):
        block = field[:, pl.ds(pl.multiple_of(i * 2 * zl, 2 * zl), 2 * zl), :].astype(F32)
        both = None
        for y in range(2):
            plane = block[:, y * zl : (y + 1) * zl, :].reshape(-1, length).astype(BF)
            term = dot(table[t, :, y * length : (y + 1) * length], plane, ((1,), (1,)))
            both = term if both is None else both + term
        half = both.shape[0] // 2
        rows = half // out.shape[1]
        out[t, :, pl.ds(pl.multiple_of(i * rows, rows), rows), :] = (
            both[:half] + both[half:]
        ).reshape(out.shape[1], rows, out.shape[3])
        return carry

    lax.fori_loop(first, last, step, 0)


def mix_modes(zl, x, w, forward, t):
    cells, rows, tile = x.shape
    lanes = LH * tile
    kp = rows // (2 * LH)
    channels = lanes // zl
    row = lambda k, q: jnp.concatenate([x[:, (h * kp + k) * 2 + q, :] for h in range(LH)], axis=1)
    column = lambda k: jnp.concatenate([row(k, 0), row(k, 1)], axis=0)
    block = triple(jnp.concatenate([column(k) for k in range(kp)], axis=1))
    inner = lax.broadcasted_iota(jnp.int32, (1, kp * lanes), 1) % zl
    modes = jnp.zeros((forward.shape[1], kp * lanes), F32)
    for z in range(zl):
        modes += jnp.where(inner == z, dot(forward[z], block), 0.0)
    count = modes.shape[0] // 2
    modes = jnp.concatenate(
        [
            modes[p * count : (p + 1) * count, k * lanes : (k + 1) * lanes]
            for p in range(2)
            for k in range(kp)
        ],
        axis=0,
    )
    pairs = w.shape[2]
    lane = lax.broadcasted_iota(jnp.int32, (lanes, pairs), 0) // zl
    both = lax.broadcasted_iota(jnp.int32, (lanes, pairs), 1)
    spread = jnp.where(lane == both // channels, 1.0, 0.0).astype(BF)
    mh, ml = halves(modes)
    wide = dot(mh, spread) + dot(ml, spread)
    half = wide.shape[0] // 2
    re, im = wide[:half], wide[half:]
    wr = w[0, t * half : (t + 1) * half, :].astype(F32)
    wi = w[1, t * half : (t + 1) * half, :].astype(F32)
    mixed = jnp.concatenate([wr * re - wi * im, wr * im + wi * re], axis=0)
    both = lax.broadcasted_iota(jnp.int32, (pairs, lanes), 0)
    lane = lax.broadcasted_iota(jnp.int32, (pairs, lanes), 1) // zl
    gather = jnp.where(both % channels == lane, 1.0, 0.0).astype(BF)
    ph, plo = halves(mixed)
    summed = dot(ph, gather) + dot(plo, gather)
    part = lambda p, k: summed[(p * kp + k) * count : (p * kp + k + 1) * count]
    columns = [jnp.concatenate([part(0, k), part(1, k)], axis=0) for k in range(kp)]
    return triple(jnp.concatenate(columns, axis=1))


def bypass_rows(zl, w, bias):
    channels = w.shape[0]
    row = lax.broadcasted_iota(jnp.int32, (channels * zl, channels), 0) // zl
    pick = row == lax.broadcasted_iota(jnp.int32, (channels * zl, channels), 1)
    ones = jnp.where(pick, 1.0, 0.0).astype(BF)
    left = dot(ones, w[...], ((1,), (1,))).astype(BF)
    full = dot(left, ones, ((1,), (1,)))
    a = lax.broadcasted_iota(jnp.int32, full.shape, 0) % zl
    b = lax.broadcasted_iota(jnp.int32, full.shape, 1) % zl
    column = jnp.sum(jnp.where(pick, bias[...], 0.0), axis=1, keepdims=True)
    return jnp.where(a == b, full, 0.0).astype(BF), column


def field_rows(zl, spectrum, plane, mix, column, th, tl):
    high, low = halves(spectrum)
    first = ((0,), (0,))
    value = dot(jnp.concatenate([high, low], 0), th, first) + dot(high, tl, first)
    value = value + dot(mix, plane) + column
    return jax.nn.gelu(value).reshape(-1, zl, value.shape[1])


def spectrum_kernel(n_y, n_z, zl, *refs):
    (
        f_hbm, xt_hbm, yt_hbm, yi_hbm, zf_hbm, zi_hbm, w_hbm, r_hbm,
        f, xt, yt, yi, zf, zi, w, a, theirs, summing, arrived, total, seen,
        mixed, back, ring, leaving, keeping,
        load_sem, swap_s, swap_r, sum_s, sum_r, out_s, out_r, in_s, in_r, ring_s, ring_r,
        turn_s, turn_r, keep_s,
    ) = refs
    here, column = lax.axis_index("py"), lax.axis_index("pz")
    n_ring = n_y // 2
    side, z = here // n_ring, here % n_ring
    other = 1 - side
    half_py = lambda s, at: s * n_ring + at % n_ring
    partner = {"py": half_py(other, z)}
    neighbours = ({"py": half_py(side, z + 1)}, {"py": half_py(side, z + n_ring - 1)})

    barrier = pltpu.get_barrier_semaphore()
    for peer in (partner,) + neighbours:
        pl.semaphore_signal(barrier, inc=1, device_id=peer, device_id_type=MESH)

    def greet(step, carry):
        pl.semaphore_signal(
            barrier, inc=1, device_id={"pz": (column + step) % n_z}, device_id_type=MESH
        )
        return carry

    loads = []

    def load(source, target):
        copy = pltpu.make_async_copy(source, target, load_sem.at[len(loads)])
        copy.start()
        loads.append(copy)
        return copy

    pieces = 4
    rows = f.shape[1] // pieces
    table_x = load(xt_hbm, xt)
    fields = [
        load(f_hbm.at[:, pl.ds(i * rows, rows), :], f.at[:, pl.ds(i * rows, rows), :])
        for i in range(pieces)
    ]
    depth = yt_hbm.shape[3]
    table_y = [
        load(yt_hbm.at[half_py(s, z)], yt.at[:, :, pl.ds(i * depth, depth)])
        for i, s in enumerate((side, other))
    ]
    table_z = [load(zf_hbm, zf), load(w_hbm, w), load(zi_hbm, zi)]
    table_i = [load(yi_hbm.at[half_py(s, z)], yi.at[i]) for i, s in enumerate((side, other))]
    lax.fori_loop(1, n_z, greet, 0)

    reach = n_ring // 2
    offsets = [reach] + [o * s for o in range(reach - 1, 0, -1) for s in (1, -1)] + [0]

    def swap(h, i):
        at = (z + offsets[i] + n_ring) % n_ring
        return pltpu.make_async_remote_copy(
            src_ref=a.at[h, half_py(other, at)],
            dst_ref=theirs.at[h, at],
            send_sem=swap_s.at[h * n_ring + i],
            recv_sem=swap_r.at[h * n_ring + i],
            device_id=partner,
            device_id_type=MESH,
        )

    table_x.wait()
    turns = f.shape[1] // (2 * zl) // pieces
    for h in range(PARTS):
        for i in range(pieces):
            if h == 0:
                fields[i].wait()
            x_forward(zl, f, xt, a, h, i * turns, (i + 1) * turns)
        if h == 0:
            pl.semaphore_wait(barrier, n_z + 2)
        for i in range(n_ring):
            swap(h, i).start()
    for copy in table_y:
        copy.wait()

    def partial(h, i):
        at = (z + offsets[i] + n_ring) % n_ring
        swap(h, i).wait_recv()
        rows = (a[h, half_py(side, at)], theirs[h, at])
        tile = summing.shape[4]
        block = jnp.concatenate(
            [r[:, i * tile : (i + 1) * tile] for r in rows for i in range(LH)], axis=0
        )
        high, low = halves(block)
        return dot3(yt[0], yt[1], high, low)

    part = total.shape[1] * total.shape[2] // GROUP
    span = lambda g: pl.ds(g * part, part)
    carries = lambda way, step, g: step > 0 or (g < GROUP // 2) == (way == 0)

    def hop(h, way, step, g):
        index = ((h * 2 + way) * reach + step) * GROUP + g
        return pltpu.make_async_remote_copy(
            src_ref=summing.at[h, way, step, span(g)],
            dst_ref=arrived.at[h, way, step, span(g)],
            send_sem=sum_s.at[index],
            recv_sem=sum_r.at[index],
            device_id=neighbours[way],
            device_id_type=MESH,
        )

    def set_out(h):
        block = partial(h, 0)
        for g in range(GROUP):
            way = 0 if g < GROUP // 2 else 1
            summing[h, way, 0, g * part : (g + 1) * part] = block[g * part : (g + 1) * part]
            hop(h, way, 0, g).start()

    def move_on(h, step):
        for way in range(2):
            summing[h, way, step] = partial(h, 2 * step - 1 + way)
        for g in range(GROUP):
            for way in range(2):
                if carries(way, step - 1, g):
                    hop(h, way, step - 1, g).wait_recv()
                    summing[h, way, step, span(g)] += arrived[h, way, step - 1, span(g)]
                hop(h, way, step, g).start()

    per = n_z // GROUP
    y_chip, place = column // GROUP, column % GROUP
    slot = place * per + y_chip

    def to_owner(h, source, owner, target):
        return pltpu.make_async_remote_copy(
            src_ref=total.at[h, source],
            dst_ref=seen.at[h, target],
            send_sem=out_s.at[h * n_z + owner],
            recv_sem=out_r.at[h * n_z + target],
            device_id={"pz": owner},
            device_id_type=MESH,
        )

    def arrive(h):
        last = partial(h, n_ring - 1)
        for g in range(GROUP):
            for way in range(2):
                hop(h, way, reach - 1, g).wait_recv()
            value = last[g * part : (g + 1) * part] + arrived[h, 0, reach - 1, span(g)]
            value = value + arrived[h, 1, reach - 1, span(g)]
            total[h, g * per : (g + 1) * per] = value.reshape((per,) + total.shape[2:])

            def send(i, carry):
                chip = (y_chip + i) % per
                owner = chip * GROUP + g

                @pl.when(owner != column)
                def _():
                    to_owner(h, g * per + chip, owner, column).start()

                return carry

            lax.fori_loop(0, per, send, 0)
        seen[h, column] = total[h, slot]

    def collect(h):
        def one(step, carry):
            peer = (column + step) % n_z
            to_owner(h, 0, peer, peer).wait()
            return carry

        lax.fori_loop(1, n_z, one, 0)

    def to_cells(h, source, peer, target, sender):
        return pltpu.make_async_remote_copy(
            src_ref=mixed.at[h, source],
            dst_ref=back.at[h, target],
            send_sem=in_s.at[h * n_z + peer],
            recv_sem=in_r.at[h * n_z + sender],
            device_id={"pz": peer},
            device_id_type=MESH,
        )

    tile = seen.shape[3]
    kp = seen.shape[2] // (2 * LH)
    lanes = LH * tile
    inner = lax.broadcasted_iota(jnp.int32, (1, kp * lanes), 1) % zl

    def mix_and_return(h):
        modes = mix_modes(zl, seen.at[h], w, zf, h)
        for g in range(GROUP):
            value = dot(zi[g], modes)
            size = 2 * per
            cells = jnp.zeros((size, modes.shape[1]), F32)
            for i in range(zl):
                cells += jnp.where(inner == i, value[i * size : (i + 1) * size], 0.0)
            for p in range(2):
                for k in range(kp):
                    for i in range(LH):
                        mixed[h, g * per : (g + 1) * per, (i * kp + k) * 2 + p, :] = cells[
                            p * per : (p + 1) * per,
                            k * lanes + i * tile : k * lanes + (i + 1) * tile,
                        ]

            def send_back(i, carry):
                chip = (y_chip + i) % per
                peer = chip * GROUP + g

                @pl.when(peer != column)
                def _():
                    to_cells(h, g * per + chip, peer, slot, column).start()

                return carry

            lax.fori_loop(0, per, send_back, 0)
        back[h, slot] = mixed[h, slot]

    def end_back(h):
        def one(step, carry):
            peer = (column + step) % n_z
            to_cells(h, 0, peer, 0, peer).wait()
            return carry

        lax.fori_loop(1, n_z, one, 0)

    wide = lambda g: pl.ds(g * per, per)
    passes = lambda way, step, g: step < reach - 1 or (g < GROUP // 2) == (way == 0)

    def relay(h, way, step, g):
        index = ((h * 2 + way) * reach + step) * GROUP + g
        source = back.at[h, wide(g)] if step == 0 else ring.at[h, way, step - 1, wide(g)]
        target = ring.at[h, 0 if step == reach - 1 else way, step, wide(g)]
        return pltpu.make_async_remote_copy(
            src_ref=source,
            dst_ref=target,
            send_sem=ring_s.at[index],
            recv_sem=ring_r.at[index],
            device_id=neighbours[way],
            device_id_type=MESH,
        )

    def turn(h, i, owner):
        return pltpu.make_async_remote_copy(
            src_ref=leaving.at[h, i],
            dst_ref=r_hbm.at[:, h, owner],
            send_sem=turn_s.at[h * n_ring + i],
            recv_sem=turn_r.at[h * n_ring + i],
            device_id=partner,
            device_id_type=MESH,
        )

    def keep(h, i, owner):
        return pltpu.make_async_copy(
            keeping.at[h, i], r_hbm.at[:, h, owner], keep_s.at[h * n_ring + i]
        )

    def spread(h, i, offset, block):
        owner = half_py(side, z + offset + n_ring)
        high, low = halves(block.reshape(-1, block.shape[2]))
        leaving[h, i] = dot3(yi[1, 0], yi[1, 1], high, low).reshape(leaving.shape[2:])
        turn(h, i, owner).start()
        keeping[h, i] = dot3(yi[0, 0], yi[0, 1], high, low).reshape(keeping.shape[2:])
        keep(h, i, owner).start()

    def send_own(h):
        for g in range(GROUP):
            for way in range(2):
                relay(h, way, 0, g).start()

    def pass_on(h, step):
        for g in range(GROUP):
            for way in range(2):
                if passes(way, step - 1, g):
                    relay(h, way, step - 1, g).wait_recv()
                if step < reach and passes(way, step, g):
                    relay(h, way, step, g).start()

    def spread_pair(h, step):
        if step == reach:
            spread(h, n_ring - 1, reach, ring[h, 0, reach - 1])
        else:
            for way in range(2):
                spread(h, 2 * step - 1 + way, step if way else -step, ring[h, way, step - 1])

    set_out(0)
    for step in range(1, reach):
        move_on(0, step)
    set_out(1)
    arrive(0)
    for step in range(1, reach):
        move_on(1, step)
    for copy in table_z:
        copy.wait()
    collect(0)
    mix_and_return(0)
    arrive(1)
    for copy in table_i:
        copy.wait()
    end_back(0)
    send_own(0)
    spread(0, 0, 0, back[0])
    collect(1)
    mix_and_return(1)
    for step in range(1, reach):
        pass_on(0, step)
        spread_pair(0, step)
    pass_on(0, reach)
    end_back(1)
    send_own(1)
    spread_pair(0, reach)
    spread(1, 0, 0, back[1])
    for step in range(1, reach + 1):
        pass_on(1, step)
        spread_pair(1, step)

    for h in range(PARTS):
        for i in range(n_ring):
            swap(h, i).wait_send()
            keep(h, i, here).wait()
            turn(h, i, here).wait()
        for step in range(reach):
            for g in range(GROUP):
                for way in range(2):
                    if carries(way, step, g):
                        hop(h, way, step, g).wait_send()
                    if passes(way, step, g):
                        relay(h, way, step, g).wait_send()


def field_kernel(zl, r_ref, f_ref, w_ref, b_ref, th_ref, tl_ref, o_ref, mix, shift):
    @pl.when(pl.program_id(0) == 0)
    def _():
        rows_mix, rows_bias = bypass_rows(zl, w_ref, b_ref)
        mix[...] = rows_mix
        shift[...] = jnp.broadcast_to(rows_bias, shift.shape)

    block = f_ref[...].astype(F32)
    for y in range(f_ref.shape[1] // zl):
        plane = block[:, y * zl : (y + 1) * zl, :].reshape(-1, block.shape[2]).astype(BF)
        values = jnp.concatenate([r_ref[i, :, y, :] for i in range(LH)], axis=1)
        made = field_rows(zl, values, plane, mix[...], shift[...], th_ref[...], tl_ref[...])
        o_ref[:, y * zl : (y + 1) * zl, :] = made.astype(BF)


def whole(shape):
    return pl.BlockSpec(shape, lambda i: (0,) * len(shape))


def per_device(tables, n_y, n_z, features, spectral_weight, bypass_weight, bias_vector):
    xf, xi, yf, yi, zf, zi = tables
    c, yl, zl, nx = features.shape
    _, kl, _, mz, pairs = spectral_weight.shape
    lanes = c * zl
    tile = lanes // LH
    kp = kl // PARTS
    rows = yl * 2 * kp
    part = LH * 2 * kp
    flat = features.reshape(c, yl * zl, nx)
    x_rows = split(xf, 1).reshape(PARTS, -1, 2 * nx)
    y_rows, y_back = split(yf, 1), split(yi, 1)
    z_rows, z_back = thrice(zf), thrice(zi)
    high, tl = split(xi)
    th = np.concatenate([high, high], 0)
    weight = spectral_weight.reshape(2, kl * mz, pairs)
    bias = bias_vector.reshape(1, c)
    my_rows = y_rows.shape[2]
    modes = my_rows // part
    n_ring = n_y // 2
    reach = n_ring // 2
    operands = [flat] + [jnp.asarray(t) for t in (x_rows, y_rows, y_back, z_rows, z_back)] + [weight]
    hops = PARTS * 2 * reach * GROUP
    turns = PARTS * n_ring
    sems = [16] + [turns] * 2 + [hops] * 2 + [PARTS * n_z] * 4 + [hops] * 2 + [turns] * 3
    planes = pl.pallas_call(
        functools.partial(spectrum_kernel, n_y, n_z, zl),
        out_shape=jax.ShapeDtypeStruct((LH, PARTS, n_y, rows, tile), F32),
        in_specs=[pl.BlockSpec(memory_space=pl.ANY)] * len(operands),
        out_specs=pl.BlockSpec(memory_space=pl.ANY),
        scratch_shapes=[
            pltpu.VMEM(flat.shape, BF),
            pltpu.VMEM(x_rows.shape, BF),
            pltpu.VMEM((2, my_rows, 2 * y_rows.shape[3]), BF),
            pltpu.VMEM((2,) + y_back.shape[1:], BF),
            pltpu.VMEM(z_rows.shape, BF),
            pltpu.VMEM(z_back.shape, BF),
            pltpu.VMEM(weight.shape, BF),
            pltpu.VMEM((PARTS, n_y, rows, lanes), F32),
            pltpu.VMEM((PARTS, n_ring, rows, lanes), F32),
            pltpu.VMEM((PARTS, 2, reach, my_rows, tile), F32),
            pltpu.VMEM((PARTS, 2, reach, my_rows, tile), F32),
            pltpu.VMEM((PARTS, modes, part, tile), F32),
            pltpu.VMEM((PARTS, n_z, part, tile), F32),
            pltpu.VMEM((PARTS, n_z, part, tile), F32),
            pltpu.VMEM((PARTS, modes, part, tile), F32),
            pltpu.VMEM((PARTS, 2, reach, modes, part, tile), F32),
            pltpu.VMEM((PARTS, n_ring, LH, rows, tile), F32),
            pltpu.VMEM((PARTS, n_ring, LH, rows, tile), F32),
        ]
        + [pltpu.SemaphoreType.DMA((n,)) for n in sems],
        compiler_params=pltpu.CompilerParams(
            collective_id=0, has_side_effects=True, vmem_limit_bytes=62 * MIB
        ),
        name="spectrum",
    )(*operands)

    step = 8
    count = PARTS * n_y * 2 * kp
    block = pl.BlockSpec((c, step * zl, nx), lambda i: (0, i, 0))
    out = pl.pallas_call(
        functools.partial(field_kernel, zl),
        grid=(yl // step,),
        in_specs=[
            pl.BlockSpec((LH, count, step, tile), lambda i: (0, 0, i, 0)),
            block,
            whole(bypass_weight.shape),
            whole(bias.shape),
            whole(th.shape),
            whole(tl.shape),
        ],
        out_specs=block,
        out_shape=jax.ShapeDtypeStruct(flat.shape, BF),
        scratch_shapes=[pltpu.VMEM((lanes, lanes), BF), pltpu.VMEM((lanes, nx), F32)],
        compiler_params=pltpu.CompilerParams(vmem_limit_bytes=62 * MIB),
        name="field",
    )(planes.reshape(LH, count, yl, tile), flat, bypass_weight, bias, jnp.asarray(th), jnp.asarray(tl))
    return out.reshape(features.shape)


def solution(mesh):
    n_y, n_z = mesh.shape["py"], mesh.shape["pz"]

    def run(features, spectral_weight, bypass_weight, bias_vector):
        _, ny, nz, nx = features.shape
        _, mx, my, mz, _ = spectral_weight.shape
        tables = make_tables(nx, ny, nz, mx, my, mz, n_y, n_z)
        return jax.shard_map(
            functools.partial(per_device, tables, n_y, n_z),
            mesh=mesh,
            in_specs=(P(None, "py", "pz", None), P(None, "py", "pz", None, None), P(), P()),
            out_specs=P(None, "py", "pz", None),
            check_vma=False,
        )(features, spectral_weight, bypass_weight, bias_vector)

    return run
```

```python
import functools
import math

import jax
import jax.numpy as jnp
import ml_dtypes
import numpy as np
from jax import lax
from jax.experimental import pallas as pl
from jax.experimental.pallas import tpu as pltpu
from jax.sharding import PartitionSpec as P

MESH = pl.DeviceIdType.MESH
BF = jnp.bfloat16
F32 = jnp.float32
MIB = 1 << 20
PARTS = 2
STRIP = 8
LH = 2
GROUP = 4


def centred(count):
    index = np.arange(count)
    return np.where(index < count // 2, index, index - count)


def split(table, axis=0):
    high = table.astype(ml_dtypes.bfloat16)
    low = (table - high.astype(np.float64)).astype(ml_dtypes.bfloat16)
    return np.stack([high, low], axis)


def thrice(table):
    high, low = split(table)
    return np.concatenate([high, high, low], -1)


def pair(frequencies, positions, period, sign):
    angle = 2.0 * np.pi * ((positions[:, None] * frequencies[None, :]) % period) / period
    c, s = np.cos(angle), np.sin(angle)
    return np.stack([np.stack([c, sign * s]), np.stack([-sign * s, c])])


def make_tables(nx, ny, nz, mx, my, mz, py, pz):
    k = mx // py
    zl = nz // pz
    yl = ny // py
    norm = 1.0 / math.sqrt(nx * ny * nz)
    angle = 2.0 * np.pi * ((np.arange(mx)[:, None] * np.arange(nx)[None, :]) % nx) / nx
    kp = k // PARTS
    eye, pairs = np.eye(kp), np.eye(2)
    xf = np.stack([np.cos(angle) * norm, -np.sin(angle) * norm], 1)
    xf = xf.reshape(py, PARTS, kp, 2, nx).swapaxes(0, 1).reshape(2 * mx, nx)
    weight = np.where(np.arange(mx) == 0, 1.0, 2.0)[:, None] * norm
    xi = np.stack([np.cos(angle) * weight, -np.sin(angle) * weight], 1)
    xi = xi.reshape(py, PARTS, kp, 2, nx).swapaxes(0, 1).reshape(2 * mx, nx)
    order = np.arange(my).reshape(pz // GROUP, GROUP).T.reshape(-1)
    yf = pair(centred(my), np.arange(ny), ny, -1.0)[..., order].reshape(2, 2, py, yl, my)
    yf = np.einsum("pqdyj,kl,hg->djhkqgylp", yf, eye, pairs)
    yf = yf.reshape(py, my * 4 * kp, yl * 4 * kp)
    yi = pair(centred(my), np.arange(ny), ny, 1.0)[..., order].reshape(2, 2, py, yl, my)
    yi = yi.reshape(2, 2, py, yl // STRIP, STRIP, my)
    yi = np.einsum("qrdwyj,kl,hg->dwhkryjglq", yi, eye, pairs)
    yi = yi.reshape(py, yl * 4 * kp, my * 4 * kp)
    zf = pair(centred(mz), np.arange(nz), nz, -1.0).reshape(2, 2, pz, zl, mz)
    zf = np.einsum("pqszm->zqmps", zf).reshape(zl, 2 * mz, 2 * pz)
    zi = pair(centred(mz), np.arange(nz), nz, 1.0).reshape(2, 2, pz // GROUP, GROUP, zl, mz)
    zi = np.einsum("qrjgzm->gzrjqm", zi).reshape(GROUP, zl * 2 * pz // GROUP, 2 * mz)
    return xf, xi, yf, yi, zf, zi


def halves(value):
    high = value.astype(BF)
    return high, (value - high.astype(F32)).astype(BF)


def triple(value):
    high, low = halves(value)
    return jnp.concatenate([high, low, high], 0)


def dot(a, b, dims=((1,), (0,))):
    return lax.dot_general(a, b, (dims, ((), ())), preferred_element_type=F32)


def dot3(ah, al, bh, bl):
    return dot(ah, bh) + dot(al, bh) + dot(ah, bl)


def x_forward(zl, field, table, out, first, last):
    length = field.shape[2]
    parts, owners, two, _, lanes = out.shape

    def step(i, carry):
        block = field[:, pl.ds(pl.multiple_of(i * 2 * zl, 2 * zl), 2 * zl), :].astype(F32)
        planes = []
        for y in range(2):
            plane = block[:, y * zl : (y + 1) * zl, :].reshape(-1, length).astype(BF)
            both = dot(table[...], plane, ((1,), (1,)))
            half = both.shape[0] // 2
            planes.append((both[:half] + both[half:]).reshape(parts * owners, -1, lanes))
        first_y, second_y = planes
        rows = first_y.shape[1]
        upper = lax.broadcasted_iota(jnp.int32, (1, rows, 1), 1) < rows // 2
        turned = lambda v: pltpu.roll(v, rows // 2, 1)
        even = jnp.where(upper, first_y, turned(second_y))
        odd = jnp.where(upper, turned(first_y), second_y)
        at = pl.ds(pl.multiple_of(i * rows, rows), rows)
        for t in range(parts):
            out[t, :, 0, at, :] = even[t * owners : (t + 1) * owners]
            out[t, :, 1, at, :] = odd[t * owners : (t + 1) * owners]
        return carry

    lax.fori_loop(first, last, step, 0)


def mix_modes(zl, x, w, forward, t):
    cells, rows, tile = x.shape
    lanes = LH * tile
    kp = rows // (2 * LH)
    channels = lanes // zl
    row = lambda k, q: jnp.concatenate([x[:, (h * kp + k) * 2 + q, :] for h in range(LH)], axis=1)
    column = lambda k: jnp.concatenate([row(k, 0), row(k, 1)], axis=0)
    block = triple(jnp.concatenate([column(k) for k in range(kp)], axis=1))
    inner = lax.broadcasted_iota(jnp.int32, (1, kp * lanes), 1) % zl
    modes = jnp.zeros((forward.shape[1], kp * lanes), F32)
    for z in range(zl):
        modes += jnp.where(inner == z, dot(forward[z], block), 0.0)
    count = modes.shape[0] // 2
    modes = jnp.concatenate(
        [
            modes[p * count : (p + 1) * count, k * lanes : (k + 1) * lanes]
            for p in range(2)
            for k in range(kp)
        ],
        axis=0,
    )
    pairs = w.shape[2]
    lane = lax.broadcasted_iota(jnp.int32, (lanes, pairs), 0) // zl
    both = lax.broadcasted_iota(jnp.int32, (lanes, pairs), 1)
    spread = jnp.where(lane == both // channels, 1.0, 0.0).astype(BF)
    mh, ml = halves(modes)
    wide = dot(mh, spread) + dot(ml, spread)
    half = wide.shape[0] // 2
    re, im = wide[:half], wide[half:]
    wr = w[0, t * half : (t + 1) * half, :].astype(F32)
    wi = w[1, t * half : (t + 1) * half, :].astype(F32)
    mixed = jnp.concatenate([wr * re - wi * im, wr * im + wi * re], axis=0)
    both = lax.broadcasted_iota(jnp.int32, (pairs, lanes), 0)
    lane = lax.broadcasted_iota(jnp.int32, (pairs, lanes), 1) // zl
    gather = jnp.where(both % channels == lane, 1.0, 0.0).astype(BF)
    ph, plo = halves(mixed)
    summed = dot(ph, gather) + dot(plo, gather)
    part = lambda p, k: summed[(p * kp + k) * count : (p * kp + k + 1) * count]
    columns = [jnp.concatenate([part(0, k), part(1, k)], axis=0) for k in range(kp)]
    return triple(jnp.concatenate(columns, axis=1))


def bypass_rows(zl, w, bias):
    channels = w.shape[0]
    row = lax.broadcasted_iota(jnp.int32, (channels * zl, channels), 0) // zl
    pick = row == lax.broadcasted_iota(jnp.int32, (channels * zl, channels), 1)
    ones = jnp.where(pick, 1.0, 0.0).astype(BF)
    left = dot(ones, w[...], ((1,), (1,))).astype(BF)
    full = dot(left, ones, ((1,), (1,)))
    a = lax.broadcasted_iota(jnp.int32, full.shape, 0) % zl
    b = lax.broadcasted_iota(jnp.int32, full.shape, 1) % zl
    column = jnp.sum(jnp.where(pick, bias[...], 0.0), axis=1, keepdims=True)
    return jnp.where(a == b, full, 0.0).astype(BF), column


def field_rows(zl, spectrum, plane, mix, column, th, tl):
    high, low = halves(spectrum)
    first = ((0,), (0,))
    value = dot(jnp.concatenate([high, low], 0), th, first) + dot(high, tl, first)
    value = value + dot(mix, plane) + column
    return jax.nn.gelu(value).reshape(-1, zl, value.shape[1])


def spectrum_kernel(n_y, n_z, zl, *refs):
    (
        f_hbm, xt_hbm, yt_hbm, yi_hbm, zf_hbm, zi_hbm, w_hbm, r_hbm,
        f, xt, yt, yi, zf, zi, w, a, theirs, summing, arrived, total, seen,
        mixed, back, ring, leaving, keeping,
        load_sem, swap_s, swap_r, sum_s, sum_r, out_s, out_r, in_s, in_r, ring_s, ring_r,
        turn_s, turn_r, keep_s,
    ) = refs
    here, column = lax.axis_index("py"), lax.axis_index("pz")
    n_ring = n_y // 2
    side, z = here // n_ring, here % n_ring
    other = 1 - side
    half_py = lambda s, at: s * n_ring + at % n_ring
    partner = {"py": half_py(other, z)}
    neighbours = ({"py": half_py(side, z + 1)}, {"py": half_py(side, z + n_ring - 1)})

    barrier = pltpu.get_barrier_semaphore()
    for peer in (partner,) + neighbours:
        pl.semaphore_signal(barrier, inc=1, device_id=peer, device_id_type=MESH)

    def greet(step, carry):
        pl.semaphore_signal(
            barrier, inc=1, device_id={"pz": (column + step) % n_z}, device_id_type=MESH
        )
        return carry

    loads = []

    def load(source, target):
        copy = pltpu.make_async_copy(source, target, load_sem.at[len(loads)])
        copy.start()
        loads.append(copy)
        return copy

    pieces = 4
    rows = f.shape[1] // pieces
    table_x = load(xt_hbm, xt)
    fields = [
        load(f_hbm.at[:, pl.ds(i * rows, rows), :], f.at[:, pl.ds(i * rows, rows), :])
        for i in range(pieces)
    ]
    lax.fori_loop(1, n_z, greet, 0)

    reach = n_ring // 2
    offsets = [reach] + [o * s for o in range(reach - 1, 0, -1) for s in (1, -1)] + [0]

    def swap(h, i):
        at = (z + offsets[i] + n_ring) % n_ring
        return pltpu.make_async_remote_copy(
            src_ref=a.at[h, half_py(other, at) // 2, at % 2],
            dst_ref=theirs.at[h, at],
            send_sem=swap_s.at[h * n_ring + i],
            recv_sem=swap_r.at[h * n_ring + i],
            device_id=partner,
            device_id_type=MESH,
        )

    table_x.wait()
    turns = f.shape[1] // (2 * zl) // pieces
    for i in range(pieces):
        fields[i].wait()
        x_forward(zl, f, xt, a, i * turns, (i + 1) * turns)
    depth = yt_hbm.shape[3]
    table_y = [
        load(yt_hbm.at[half_py(s, z)], yt.at[:, :, pl.ds(i * depth, depth)])
        for i, s in enumerate((side, other))
    ]
    table_z = [load(zf_hbm, zf), load(w_hbm, w), load(zi_hbm, zi)]
    table_i = [load(yi_hbm.at[half_py(s, z)], yi.at[i]) for i, s in enumerate((side, other))]
    pl.semaphore_wait(barrier, n_z + 2)
    for h in range(PARTS):
        for i in range(n_ring):
            swap(h, i).start()
    for copy in table_y:
        copy.wait()

    def partial(h, i):
        at = (z + offsets[i] + n_ring) % n_ring
        swap(h, i).wait_recv()
        rows = (a[h, half_py(side, at) // 2, at % 2], theirs[h, at])
        tile = summing.shape[4]
        block = jnp.concatenate(
            [r[:, i * tile : (i + 1) * tile] for r in rows for i in range(LH)], axis=0
        )
        high, low = halves(block)
        return dot3(yt[0], yt[1], high, low)

    part = total.shape[1] * total.shape[2] // GROUP
    span = lambda g: pl.ds(g * part, part)
    carries = lambda way, step, g: step > 0 or (g < GROUP // 2) == (way == 0)

    def hop(h, way, step, g):
        index = ((h * 2 + way) * reach + step) * GROUP + g
        return pltpu.make_async_remote_copy(
            src_ref=summing.at[h, way, step, span(g)],
            dst_ref=arrived.at[h, way, step, span(g)],
            send_sem=sum_s.at[index],
            recv_sem=sum_r.at[index],
            device_id=neighbours[way],
            device_id_type=MESH,
        )

    def set_out(h):
        block = partial(h, 0)
        for g in range(GROUP):
            way = 0 if g < GROUP // 2 else 1
            summing[h, way, 0, g * part : (g + 1) * part] = block[g * part : (g + 1) * part]
            hop(h, way, 0, g).start()

    def move_on(h, step):
        for way in range(2):
            summing[h, way, step] = partial(h, 2 * step - 1 + way)
        for g in range(GROUP):
            for way in range(2):
                if carries(way, step - 1, g):
                    hop(h, way, step - 1, g).wait_recv()
                    summing[h, way, step, span(g)] += arrived[h, way, step - 1, span(g)]
                hop(h, way, step, g).start()

    per = n_z // GROUP
    y_chip, place = column // GROUP, column % GROUP
    far_first = lambda i: (y_chip + per // 2 + (i + 1) // 2 * (1 - i % 2 * 2) + per) % per
    slot = place * per + y_chip

    def to_owner(h, source, owner, target):
        return pltpu.make_async_remote_copy(
            src_ref=total.at[h, source],
            dst_ref=seen.at[h, target],
            send_sem=out_s.at[h * n_z + owner],
            recv_sem=out_r.at[h * n_z + target],
            device_id={"pz": owner},
            device_id_type=MESH,
        )

    def arrive(h):
        last = partial(h, n_ring - 1)
        for g in range(GROUP):
            for way in range(2):
                hop(h, way, reach - 1, g).wait_recv()
            value = last[g * part : (g + 1) * part] + arrived[h, 0, reach - 1, span(g)]
            value = value + arrived[h, 1, reach - 1, span(g)]
            total[h, g * per : (g + 1) * per] = value.reshape((per,) + total.shape[2:])

            def send(i, carry):
                chip = far_first(i)
                owner = chip * GROUP + g

                @pl.when(owner != column)
                def _():
                    to_owner(h, g * per + chip, owner, column).start()

                return carry

            lax.fori_loop(0, per, send, 0)
        seen[h, column] = total[h, slot]

    def collect(h):
        def one(step, carry):
            peer = (column + step) % n_z
            to_owner(h, 0, peer, peer).wait()
            return carry

        lax.fori_loop(1, n_z, one, 0)

    def to_cells(h, source, peer, target, sender):
        return pltpu.make_async_remote_copy(
            src_ref=mixed.at[h, source],
            dst_ref=back.at[h, target],
            send_sem=in_s.at[h * n_z + peer],
            recv_sem=in_r.at[h * n_z + sender],
            device_id={"pz": peer},
            device_id_type=MESH,
        )

    tile = seen.shape[3]
    kp = seen.shape[2] // (2 * LH)
    lanes = LH * tile
    inner = lax.broadcasted_iota(jnp.int32, (1, kp * lanes), 1) % zl

    def mix_and_return(h):
        modes = mix_modes(zl, seen.at[h], w, zf, h)
        for g in range(GROUP):
            value = dot(zi[g], modes)
            size = 2 * per
            cells = jnp.zeros((size, modes.shape[1]), F32)
            for i in range(zl):
                cells += jnp.where(inner == i, value[i * size : (i + 1) * size], 0.0)
            for p in range(2):
                for k in range(kp):
                    for i in range(LH):
                        mixed[h, g * per : (g + 1) * per, (i * kp + k) * 2 + p, :] = cells[
                            p * per : (p + 1) * per,
                            k * lanes + i * tile : k * lanes + (i + 1) * tile,
                        ]

            def send_back(i, carry):
                chip = far_first(i)
                peer = chip * GROUP + g

                @pl.when(peer != column)
                def _():
                    to_cells(h, g * per + chip, peer, slot, column).start()

                return carry

            lax.fori_loop(0, per, send_back, 0)
        back[h, slot] = mixed[h, slot]

    def end_back(h):
        def one(step, carry):
            peer = (column + step) % n_z
            to_cells(h, 0, peer, 0, peer).wait()
            return carry

        lax.fori_loop(1, n_z, one, 0)

    wide = lambda g: pl.ds(g * per, per)
    passes = lambda way, step, g: step < reach - 1 or (g < GROUP // 2) == (way == 0)

    def relay(h, way, step, g):
        index = ((h * 2 + way) * reach + step) * GROUP + g
        source = back.at[h, wide(g)] if step == 0 else ring.at[h, way, step - 1, wide(g)]
        target = ring.at[h, 0 if step == reach - 1 else way, step, wide(g)]
        return pltpu.make_async_remote_copy(
            src_ref=source,
            dst_ref=target,
            send_sem=ring_s.at[index],
            recv_sem=ring_r.at[index],
            device_id=neighbours[way],
            device_id_type=MESH,
        )

    def turn(h, i, owner):
        return pltpu.make_async_remote_copy(
            src_ref=leaving.at[h, i],
            dst_ref=r_hbm.at[:, :, h, owner],
            send_sem=turn_s.at[h * n_ring + i],
            recv_sem=turn_r.at[h * n_ring + i],
            device_id=partner,
            device_id_type=MESH,
        )

    def keep(h, i, owner):
        return pltpu.make_async_copy(
            keeping.at[h, i], r_hbm.at[:, :, h, owner], keep_s.at[h * n_ring + i]
        )

    def spread(h, i, offset, block):
        owner = half_py(side, z + offset + n_ring)
        high, low = halves(block.reshape(-1, block.shape[2]))
        leaving[h, i] = dot3(yi[1, 0], yi[1, 1], high, low).reshape(leaving.shape[2:])
        turn(h, i, owner).start()
        keeping[h, i] = dot3(yi[0, 0], yi[0, 1], high, low).reshape(keeping.shape[2:])
        keep(h, i, owner).start()

    def send_own(h):
        for g in range(GROUP):
            for way in range(2):
                relay(h, way, 0, g).start()

    def pass_on(h, step):
        for g in range(GROUP):
            for way in range(2):
                if passes(way, step - 1, g):
                    relay(h, way, step - 1, g).wait_recv()
                if step < reach and passes(way, step, g):
                    relay(h, way, step, g).start()

    def spread_pair(h, step):
        if step == reach:
            spread(h, n_ring - 1, reach, ring[h, 0, reach - 1])
        else:
            for way in range(2):
                spread(h, 2 * step - 1 + way, step if way else -step, ring[h, way, step - 1])

    set_out(0)
    for step in range(1, reach):
        move_on(0, step)
    set_out(1)
    arrive(0)
    for step in range(1, reach):
        move_on(1, step)
    for copy in table_z:
        copy.wait()
    collect(0)
    mix_and_return(0)
    arrive(1)
    for copy in table_i:
        copy.wait()
    end_back(0)
    send_own(0)
    spread(0, 0, 0, back[0])
    collect(1)
    mix_and_return(1)
    for step in range(1, reach - 1):
        pass_on(0, step)
        spread_pair(0, step)
    end_back(1)
    send_own(1)
    spread(1, 0, 0, back[1])
    for step in range(reach - 1, reach + 1):
        pass_on(0, step)
        spread_pair(0, step)
    for step in range(1, reach + 1):
        pass_on(1, step)
        spread_pair(1, step)

    for h in range(PARTS):
        for i in range(n_ring):
            swap(h, i).wait_send()
            keep(h, i, here).wait()
            turn(h, i, here).wait()
        for step in range(reach):
            for g in range(GROUP):
                for way in range(2):
                    if carries(way, step, g):
                        hop(h, way, step, g).wait_send()
                    if passes(way, step, g):
                        relay(h, way, step, g).wait_send()


def field_kernel(zl, r_ref, f_ref, w_ref, b_ref, th_ref, tl_ref, o_ref, mix, shift):
    @pl.when(pl.program_id(0) == 0)
    def _():
        rows_mix, rows_bias = bypass_rows(zl, w_ref, b_ref)
        mix[...] = rows_mix
        shift[...] = jnp.broadcast_to(rows_bias, shift.shape)

    def part(first):
        block = f_ref[...].astype(F32)
        for y in range(f_ref.shape[1] // zl):
            plane = block[:, y * zl : (y + 1) * zl, :].reshape(-1, block.shape[2]).astype(BF)
            values = jnp.concatenate([r_ref[0, i, :, first + y, :] for i in range(LH)], axis=1)
            made = field_rows(zl, values, plane, mix[...], shift[...], th_ref[...], tl_ref[...])
            o_ref[:, y * zl : (y + 1) * zl, :] = made.astype(BF)

    @pl.when(pl.program_id(0) % 2 == 0)
    def _():
        part(0)

    @pl.when(pl.program_id(0) % 2 == 1)
    def _():
        part(STRIP // 2)


def whole(shape):
    return pl.BlockSpec(shape, lambda i: (0,) * len(shape))


def per_device(tables, n_y, n_z, features, spectral_weight, bypass_weight, bias_vector):
    xf, xi, yf, yi, zf, zi = tables
    c, yl, zl, nx = features.shape
    _, kl, _, mz, pairs = spectral_weight.shape
    lanes = c * zl
    tile = lanes // LH
    kp = kl // PARTS
    rows = yl * 2 * kp
    part = LH * 2 * kp
    flat = features.reshape(c, yl * zl, nx)
    x_rows = split(xf).reshape(-1, nx)
    y_rows, y_back = split(yf, 1), split(yi, 1)
    z_rows, z_back = thrice(zf), thrice(zi)
    high, tl = split(xi)
    th = np.concatenate([high, high], 0)
    weight = spectral_weight.reshape(2, kl * mz, pairs)
    bias = bias_vector.reshape(1, c)
    my_rows = y_rows.shape[2]
    modes = my_rows // part
    n_ring = n_y // 2
    reach = n_ring // 2
    strips = yl // STRIP
    operands = [flat] + [jnp.asarray(t) for t in (x_rows, y_rows, y_back, z_rows, z_back)] + [weight]
    hops = PARTS * 2 * reach * GROUP
    turns = PARTS * n_ring
    sems = [16] + [turns] * 2 + [hops] * 2 + [PARTS * n_z] * 4 + [hops] * 2 + [turns] * 3
    planes = pl.pallas_call(
        functools.partial(spectrum_kernel, n_y, n_z, zl),
        out_shape=jax.ShapeDtypeStruct((strips, LH, PARTS, n_y, rows // strips, tile), F32),
        in_specs=[pl.BlockSpec(memory_space=pl.ANY)] * len(operands),
        out_specs=pl.BlockSpec(memory_space=pl.ANY),
        scratch_shapes=[
            pltpu.VMEM(flat.shape, BF),
            pltpu.VMEM(x_rows.shape, BF),
            pltpu.VMEM((2, my_rows, 2 * y_rows.shape[3]), BF),
            pltpu.VMEM((2,) + y_back.shape[1:], BF),
            pltpu.VMEM(z_rows.shape, BF),
            pltpu.VMEM(z_back.shape, BF),
            pltpu.VMEM(weight.shape, BF),
            pltpu.VMEM((PARTS, n_y // 2, 2, rows, lanes), F32),
            pltpu.VMEM((PARTS, n_ring, rows, lanes), F32),
            pltpu.VMEM((PARTS, 2, reach, my_rows, tile), F32),
            pltpu.VMEM((PARTS, 2, reach, my_rows, tile), F32),
            pltpu.VMEM((PARTS, modes, part, tile), F32),
            pltpu.VMEM((PARTS, n_z, part, tile), F32),
            pltpu.VMEM((PARTS, n_z, part, tile), F32),
            pltpu.VMEM((PARTS, modes, part, tile), F32),
            pltpu.VMEM((PARTS, 2, reach, modes, part, tile), F32),
            pltpu.VMEM((PARTS, n_ring, strips, LH, rows // strips, tile), F32),
            pltpu.VMEM((PARTS, n_ring, strips, LH, rows // strips, tile), F32),
        ]
        + [pltpu.SemaphoreType.DMA((n,)) for n in sems],
        compiler_params=pltpu.CompilerParams(
            collective_id=0, has_side_effects=True, vmem_limit_bytes=62 * MIB
        ),
        name="spectrum",
    )(*operands)

    step = STRIP // 2
    count = PARTS * n_y * 2 * kp
    block = pl.BlockSpec((c, step * zl, nx), lambda i: (0, i, 0))
    out = pl.pallas_call(
        functools.partial(field_kernel, zl),
        grid=(yl // step,),
        in_specs=[
            pl.BlockSpec((1, LH, count, STRIP, tile), lambda i: (i // 2, 0, 0, 0, 0)),
            block,
            whole(bypass_weight.shape),
            whole(bias.shape),
            whole(th.shape),
            whole(tl.shape),
        ],
        out_specs=block,
        out_shape=jax.ShapeDtypeStruct(flat.shape, BF),
        scratch_shapes=[pltpu.VMEM((lanes, lanes), BF), pltpu.VMEM((lanes, nx), F32)],
        compiler_params=pltpu.CompilerParams(vmem_limit_bytes=62 * MIB),
        name="field",
    )(planes.reshape(strips, LH, count, STRIP, tile), flat, bypass_weight, bias, jnp.asarray(th), jnp.asarray(tl))
    return out.reshape(features.shape)


def solution(mesh):
    n_y, n_z = mesh.shape["py"], mesh.shape["pz"]

    def run(features, spectral_weight, bypass_weight, bias_vector):
        _, ny, nz, nx = features.shape
        _, mx, my, mz, _ = spectral_weight.shape
        tables = make_tables(nx, ny, nz, mx, my, mz, n_y, n_z)
        return jax.shard_map(
            functools.partial(per_device, tables, n_y, n_z),
            mesh=mesh,
            in_specs=(P(None, "py", "pz", None), P(None, "py", "pz", None, None), P(), P()),
            out_specs=P(None, "py", "pz", None),
            check_vma=False,
        )(features, spectral_weight, bypass_weight, bias_vector)

    return run
```

```python
import functools
import math

import jax
import jax.numpy as jnp
import ml_dtypes
import numpy as np
from jax import lax
from jax.experimental import pallas as pl
from jax.experimental.pallas import tpu as pltpu
from jax.sharding import PartitionSpec as P

MESH = pl.DeviceIdType.MESH
BF = jnp.bfloat16
F32 = jnp.float32
MIB = 1 << 20
PARTS = 2
STRIP = 8
LH = 2
GROUP = 4


def centred(count):
    index = np.arange(count)
    return np.where(index < count // 2, index, index - count)


def split(table, axis=0):
    high = table.astype(ml_dtypes.bfloat16)
    low = (table - high.astype(np.float64)).astype(ml_dtypes.bfloat16)
    return np.stack([high, low], axis)


def thrice(table):
    high, low = split(table)
    return np.concatenate([high, high, low], -1)


def pair(frequencies, positions, period, sign):
    angle = 2.0 * np.pi * ((positions[:, None] * frequencies[None, :]) % period) / period
    c, s = np.cos(angle), np.sin(angle)
    return np.stack([np.stack([c, sign * s]), np.stack([-sign * s, c])])


def make_tables(nx, ny, nz, mx, my, mz, py, pz):
    k = mx // py
    zl = nz // pz
    yl = ny // py
    norm = 1.0 / math.sqrt(nx * ny * nz)
    angle = 2.0 * np.pi * ((np.arange(mx)[:, None] * np.arange(nx)[None, :]) % nx) / nx
    kp = k // PARTS
    eye, pairs = np.eye(kp), np.eye(2)
    xf = np.stack([np.cos(angle) * norm, -np.sin(angle) * norm], 1)
    xf = xf.reshape(py, PARTS, kp, 2, nx).swapaxes(0, 1).reshape(2 * mx, nx)
    weight = np.where(np.arange(mx) == 0, 1.0, 2.0)[:, None] * norm
    xi = np.stack([np.cos(angle) * weight, -np.sin(angle) * weight], 1)
    xi = xi.reshape(py, PARTS, kp, 2, nx).swapaxes(0, 1).reshape(2 * mx, nx)
    order = np.arange(my).reshape(pz // GROUP, GROUP).T.reshape(-1)
    yf = pair(centred(my), np.arange(ny), ny, -1.0)[..., order].reshape(2, 2, py, yl, my)
    yf = np.einsum("pqdyj,kl,hg->djhkqgylp", yf, eye, pairs)
    yf = yf.reshape(py, my * 4 * kp, yl * 4 * kp)
    yi = pair(centred(my), np.arange(ny), ny, 1.0)[..., order].reshape(2, 2, py, yl, my)
    yi = yi.reshape(2, 2, py, yl // STRIP, STRIP, my)
    yi = np.einsum("qrdwyj,kl,hg->dwhkryjglq", yi, eye, pairs)
    yi = yi.reshape(py, yl * 4 * kp, my * 4 * kp)
    zf = pair(centred(mz), np.arange(nz), nz, -1.0).reshape(2, 2, pz, zl, mz)
    zf = np.einsum("pqszm->zqmps", zf).reshape(zl, 2 * mz, 2 * pz)
    zi = pair(centred(mz), np.arange(nz), nz, 1.0).reshape(2, 2, pz // GROUP, GROUP, zl, mz)
    zi = np.einsum("qrjgzm->gzrjqm", zi).reshape(GROUP, zl * 2 * pz // GROUP, 2 * mz)
    return xf, xi, yf, yi, zf, zi


def halves(value):
    high = value.astype(BF)
    return high, (value - high.astype(F32)).astype(BF)


def triple(value):
    high, low = halves(value)
    return jnp.concatenate([high, low, high], 0)


def dot(a, b, dims=((1,), (0,))):
    return lax.dot_general(a, b, (dims, ((), ())), preferred_element_type=F32)


def dot3(ah, al, bh, bl):
    return dot(ah, bh) + dot(al, bh) + dot(ah, bl)


def x_forward(zl, field, table, out, first, last):
    length = field.shape[2]
    parts, owners, two, _, lanes = out.shape

    def step(i, carry):
        block = field[:, pl.ds(pl.multiple_of(i * 2 * zl, 2 * zl), 2 * zl), :].astype(F32)
        planes = []
        for y in range(2):
            plane = block[:, y * zl : (y + 1) * zl, :].reshape(-1, length).astype(BF)
            both = dot(table[...], plane, ((1,), (1,)))
            half = both.shape[0] // 2
            planes.append((both[:half] + both[half:]).reshape(parts * owners, -1, lanes))
        first_y, second_y = planes
        rows = first_y.shape[1]
        upper = lax.broadcasted_iota(jnp.int32, (1, rows, 1), 1) < rows // 2
        turned = lambda v: pltpu.roll(v, rows // 2, 1)
        even = jnp.where(upper, first_y, turned(second_y))
        odd = jnp.where(upper, turned(first_y), second_y)
        at = pl.ds(pl.multiple_of(i * rows, rows), rows)
        for t in range(parts):
            out[t, :, 0, at, :] = even[t * owners : (t + 1) * owners]
            out[t, :, 1, at, :] = odd[t * owners : (t + 1) * owners]
        return carry

    lax.fori_loop(first, last, step, 0)


def mix_modes(zl, x, w, forward, t):
    cells, rows, tile = x.shape
    lanes = LH * tile
    kp = rows // (2 * LH)
    channels = lanes // zl
    row = lambda k, q: jnp.concatenate([x[:, (h * kp + k) * 2 + q, :] for h in range(LH)], axis=1)
    column = lambda k: jnp.concatenate([row(k, 0), row(k, 1)], axis=0)
    block = triple(jnp.concatenate([column(k) for k in range(kp)], axis=1))
    inner = lax.broadcasted_iota(jnp.int32, (1, kp * lanes), 1) % zl
    modes = jnp.zeros((forward.shape[1], kp * lanes), F32)
    for z in range(zl):
        modes += jnp.where(inner == z, dot(forward[z], block), 0.0)
    count = modes.shape[0] // 2
    modes = jnp.concatenate(
        [
            modes[p * count : (p + 1) * count, k * lanes : (k + 1) * lanes]
            for p in range(2)
            for k in range(kp)
        ],
        axis=0,
    )
    pairs = w.shape[2]
    lane = lax.broadcasted_iota(jnp.int32, (lanes, pairs), 0) // zl
    both = lax.broadcasted_iota(jnp.int32, (lanes, pairs), 1)
    spread = jnp.where(lane == both // channels, 1.0, 0.0).astype(BF)
    mh, ml = halves(modes)
    wide = dot(mh, spread) + dot(ml, spread)
    half = wide.shape[0] // 2
    re, im = wide[:half], wide[half:]
    wr = w[0, t * half : (t + 1) * half, :].astype(F32)
    wi = w[1, t * half : (t + 1) * half, :].astype(F32)
    mixed = jnp.concatenate([wr * re - wi * im, wr * im + wi * re], axis=0)
    both = lax.broadcasted_iota(jnp.int32, (pairs, lanes), 0)
    lane = lax.broadcasted_iota(jnp.int32, (pairs, lanes), 1) // zl
    gather = jnp.where(both % channels == lane, 1.0, 0.0).astype(BF)
    ph, plo = halves(mixed)
    summed = dot(ph, gather) + dot(plo, gather)
    part = lambda p, k: summed[(p * kp + k) * count : (p * kp + k + 1) * count]
    columns = [jnp.concatenate([part(0, k), part(1, k)], axis=0) for k in range(kp)]
    return triple(jnp.concatenate(columns, axis=1))


def bypass_rows(zl, w, bias):
    channels = w.shape[0]
    row = lax.broadcasted_iota(jnp.int32, (channels * zl, channels), 0) // zl
    pick = row == lax.broadcasted_iota(jnp.int32, (channels * zl, channels), 1)
    ones = jnp.where(pick, 1.0, 0.0).astype(BF)
    left = dot(ones, w[...], ((1,), (1,))).astype(BF)
    full = dot(left, ones, ((1,), (1,)))
    a = lax.broadcasted_iota(jnp.int32, full.shape, 0) % zl
    b = lax.broadcasted_iota(jnp.int32, full.shape, 1) % zl
    column = jnp.sum(jnp.where(pick, bias[...], 0.0), axis=1, keepdims=True)
    return jnp.where(a == b, full, 0.0).astype(BF), column


def field_rows(zl, spectrum, plane, mix, column, th, tl):
    high, low = halves(spectrum)
    first = ((0,), (0,))
    value = dot(jnp.concatenate([high, low], 0), th, first) + dot(high, tl, first)
    value = value + dot(mix, plane) + column
    return jax.nn.gelu(value).reshape(-1, zl, value.shape[1])


def spectrum_kernel(n_y, n_z, zl, *refs):
    (
        f_hbm, xt_hbm, yt_hbm, yi_hbm, zf_hbm, zi_hbm, w_hbm, r_hbm,
        f, xt, yt, yi, zf, zi, w, a, theirs, summing, arrived, total, seen,
        mixed, back, ring, leaving, keeping,
        load_sem, swap_s, swap_r, sum_s, sum_r, out_s, out_r, in_s, in_r, ring_s, ring_r,
        turn_s, turn_r, keep_s,
    ) = refs
    here, column = lax.axis_index("py"), lax.axis_index("pz")
    n_ring = n_y // 2
    side, z = here // n_ring, here % n_ring
    other = 1 - side
    half_py = lambda s, at: s * n_ring + at % n_ring
    partner = {"py": half_py(other, z)}
    neighbours = ({"py": half_py(side, z + 1)}, {"py": half_py(side, z + n_ring - 1)})

    barrier = pltpu.get_barrier_semaphore()
    for peer in (partner,) + neighbours:
        pl.semaphore_signal(barrier, inc=1, device_id=peer, device_id_type=MESH)

    def greet(step, carry):
        pl.semaphore_signal(
            barrier, inc=1, device_id={"pz": (column + step) % n_z}, device_id_type=MESH
        )
        return carry

    loads = []

    def load(source, target):
        copy = pltpu.make_async_copy(source, target, load_sem.at[len(loads)])
        copy.start()
        loads.append(copy)
        return copy

    pieces = 4
    rows = f.shape[1] // pieces
    table_x = load(xt_hbm, xt)
    fields = [
        load(f_hbm.at[:, pl.ds(i * rows, rows), :], f.at[:, pl.ds(i * rows, rows), :])
        for i in range(pieces)
    ]
    lax.fori_loop(1, n_z, greet, 0)

    reach = n_ring // 2
    offsets = [reach] + [o * s for o in range(reach - 1, 0, -1) for s in (1, -1)] + [0]

    def swap(h, i):
        at = (z + offsets[i] + n_ring) % n_ring
        return pltpu.make_async_remote_copy(
            src_ref=a.at[h, half_py(other, at) // 2, at % 2],
            dst_ref=theirs.at[h, at],
            send_sem=swap_s.at[h * n_ring + i],
            recv_sem=swap_r.at[h * n_ring + i],
            device_id=partner,
            device_id_type=MESH,
        )

    table_x.wait()
    turns = f.shape[1] // (2 * zl) // pieces
    for i in range(pieces):
        fields[i].wait()
        x_forward(zl, f, xt, a, i * turns, (i + 1) * turns)
    depth = yt_hbm.shape[3]
    table_y = [
        load(yt_hbm.at[half_py(s, z)], yt.at[:, :, pl.ds(i * depth, depth)])
        for i, s in enumerate((side, other))
    ]
    table_z = [load(zf_hbm, zf), load(w_hbm, w), load(zi_hbm, zi)]
    table_i = [load(yi_hbm.at[half_py(s, z)], yi.at[i]) for i, s in enumerate((side, other))]
    pl.semaphore_wait(barrier, n_z + 2)
    for h in range(PARTS):
        for i in range(n_ring):
            swap(h, i).start()
    for copy in table_y:
        copy.wait()

    def partial(h, i):
        at = (z + offsets[i] + n_ring) % n_ring
        swap(h, i).wait_recv()
        rows = (a[h, half_py(side, at) // 2, at % 2], theirs[h, at])
        tile = summing.shape[4]
        block = jnp.concatenate(
            [r[:, i * tile : (i + 1) * tile] for r in rows for i in range(LH)], axis=0
        )
        high, low = halves(block)
        return dot3(yt[0], yt[1], high, low)

    part = total.shape[1] * total.shape[2] // GROUP
    span = lambda g: pl.ds(g * part, part)
    carries = lambda way, step, g: step > 0 or (g < GROUP // 2) == (way == 0)

    def hop(h, way, step, g):
        index = ((h * 2 + way) * reach + step) * GROUP + g
        return pltpu.make_async_remote_copy(
            src_ref=summing.at[h, way, step, span(g)],
            dst_ref=arrived.at[h, way, step, span(g)],
            send_sem=sum_s.at[index],
            recv_sem=sum_r.at[index],
            device_id=neighbours[way],
            device_id_type=MESH,
        )

    def set_out(h):
        block = partial(h, 0)
        for g in range(GROUP):
            way = 0 if g < GROUP // 2 else 1
            summing[h, way, 0, g * part : (g + 1) * part] = block[g * part : (g + 1) * part]
            hop(h, way, 0, g).start()

    def move_on(h, step):
        for way in range(2):
            summing[h, way, step] = partial(h, 2 * step - 1 + way)
        for g in range(GROUP):
            for way in range(2):
                if carries(way, step - 1, g):
                    hop(h, way, step - 1, g).wait_recv()
                    summing[h, way, step, span(g)] += arrived[h, way, step - 1, span(g)]
                hop(h, way, step, g).start()

    per = n_z // GROUP
    y_chip, place = column // GROUP, column % GROUP
    far_first = lambda i: (y_chip + per // 2 + (i + 1) // 2 * (1 - i % 2 * 2) + per) % per
    slot = place * per + y_chip

    def to_owner(h, source, owner, target):
        return pltpu.make_async_remote_copy(
            src_ref=total.at[h, source],
            dst_ref=seen.at[h, target],
            send_sem=out_s.at[h * n_z + owner],
            recv_sem=out_r.at[h * n_z + target],
            device_id={"pz": owner},
            device_id_type=MESH,
        )

    def arrive(h):
        last = partial(h, n_ring - 1)
        for g in range(GROUP):
            for way in range(2):
                hop(h, way, reach - 1, g).wait_recv()
            value = last[g * part : (g + 1) * part] + arrived[h, 0, reach - 1, span(g)]
            value = value + arrived[h, 1, reach - 1, span(g)]
            total[h, g * per : (g + 1) * per] = value.reshape((per,) + total.shape[2:])

            def send(i, carry):
                chip = far_first(i)
                owner = chip * GROUP + g

                @pl.when(owner != column)
                def _():
                    to_owner(h, g * per + chip, owner, column).start()

                return carry

            lax.fori_loop(0, per, send, 0)
        seen[h, column] = total[h, slot]

    def collect(h):
        def one(step, carry):
            peer = (column + step) % n_z
            to_owner(h, 0, peer, peer).wait()
            return carry

        lax.fori_loop(1, n_z, one, 0)

    def to_cells(h, source, peer, target, sender):
        return pltpu.make_async_remote_copy(
            src_ref=mixed.at[h, source],
            dst_ref=back.at[h, target],
            send_sem=in_s.at[h * n_z + peer],
            recv_sem=in_r.at[h * n_z + sender],
            device_id={"pz": peer},
            device_id_type=MESH,
        )

    tile = seen.shape[3]
    kp = seen.shape[2] // (2 * LH)
    lanes = LH * tile
    inner = lax.broadcasted_iota(jnp.int32, (1, kp * lanes), 1) % zl

    def mix_and_return(h):
        modes = mix_modes(zl, seen.at[h], w, zf, h)
        for g in range(GROUP):
            value = dot(zi[g], modes)
            size = 2 * per
            cells = jnp.zeros((size, modes.shape[1]), F32)
            for i in range(zl):
                cells += jnp.where(inner == i, value[i * size : (i + 1) * size], 0.0)
            for p in range(2):
                for k in range(kp):
                    for i in range(LH):
                        mixed[h, g * per : (g + 1) * per, (i * kp + k) * 2 + p, :] = cells[
                            p * per : (p + 1) * per,
                            k * lanes + i * tile : k * lanes + (i + 1) * tile,
                        ]

            def send_back(i, carry):
                chip = far_first(i)
                peer = chip * GROUP + g

                @pl.when(peer != column)
                def _():
                    to_cells(h, g * per + chip, peer, slot, column).start()

                return carry

            lax.fori_loop(0, per, send_back, 0)
        back[h, slot] = mixed[h, slot]

    def end_back(h):
        def one(step, carry):
            peer = (column + step) % n_z
            to_cells(h, 0, peer, 0, peer).wait()
            return carry

        lax.fori_loop(1, n_z, one, 0)

    wide = lambda g: pl.ds(g * per, per)
    passes = lambda way, step, g: step < reach - 1 or (g < GROUP // 2) == (way == 0)

    def relay(h, way, step, g):
        index = ((h * 2 + way) * reach + step) * GROUP + g
        source = back.at[h, wide(g)] if step == 0 else ring.at[h, way, step - 1, wide(g)]
        target = ring.at[h, 0 if step == reach - 1 else way, step, wide(g)]
        return pltpu.make_async_remote_copy(
            src_ref=source,
            dst_ref=target,
            send_sem=ring_s.at[index],
            recv_sem=ring_r.at[index],
            device_id=neighbours[way],
            device_id_type=MESH,
        )

    def turn(h, i, owner):
        return pltpu.make_async_remote_copy(
            src_ref=leaving.at[h, i],
            dst_ref=r_hbm.at[:, :, h, owner],
            send_sem=turn_s.at[h * n_ring + i],
            recv_sem=turn_r.at[h * n_ring + i],
            device_id=partner,
            device_id_type=MESH,
        )

    def keep(h, i, owner):
        return pltpu.make_async_copy(
            keeping.at[h, i], r_hbm.at[:, :, h, owner], keep_s.at[h * n_ring + i]
        )

    def spread(h, i, offset, block):
        owner = half_py(side, z + offset + n_ring)
        high, low = halves(block.reshape(-1, block.shape[2]))
        leaving[h, i] = dot3(yi[1, 0], yi[1, 1], high, low).reshape(leaving.shape[2:])
        turn(h, i, owner).start()
        keeping[h, i] = dot3(yi[0, 0], yi[0, 1], high, low).reshape(keeping.shape[2:])
        keep(h, i, owner).start()

    def send_own(h):
        for g in range(GROUP):
            for way in range(2):
                relay(h, way, 0, g).start()

    def pass_on(h, step):
        for g in range(GROUP):
            for way in range(2):
                if passes(way, step - 1, g):
                    relay(h, way, step - 1, g).wait_recv()
                if step < reach and passes(way, step, g):
                    relay(h, way, step, g).start()

    def spread_pair(h, step):
        if step == reach:
            spread(h, n_ring - 1, reach, ring[h, 0, reach - 1])
        else:
            for way in range(2):
                spread(h, 2 * step - 1 + way, step if way else -step, ring[h, way, step - 1])

    set_out(0)
    for step in range(1, reach):
        move_on(0, step)
    set_out(1)
    arrive(0)
    for step in range(1, reach - 1):
        move_on(1, step)
    for copy in table_z:
        copy.wait()
    collect(0)
    mix_and_return(0)
    move_on(1, reach - 1)
    arrive(1)
    for copy in table_i:
        copy.wait()
    end_back(0)
    send_own(0)
    spread(0, 0, 0, back[0])
    pass_on(0, 1)
    spread_pair(0, 1)
    collect(1)
    mix_and_return(1)
    for step in range(2, reach):
        pass_on(0, step)
        spread_pair(0, step)
    end_back(1)
    send_own(1)
    spread(1, 0, 0, back[1])
    pass_on(0, reach)
    spread_pair(0, reach)
    for step in range(1, reach + 1):
        pass_on(1, step)
        spread_pair(1, step)

    for h in range(PARTS):
        for i in range(n_ring):
            swap(h, i).wait_send()
            keep(h, i, here).wait()
            turn(h, i, here).wait()
        for step in range(reach):
            for g in range(GROUP):
                for way in range(2):
                    if carries(way, step, g):
                        hop(h, way, step, g).wait_send()
                    if passes(way, step, g):
                        relay(h, way, step, g).wait_send()


def field_kernel(
    zl, r_hbm, f_hbm, w_ref, b_ref, th_ref, tl_ref, o_hbm, r, f, o, mix, shift, r_sem, f_sem, o_sem
):
    strips, pieces = r.shape[0], 4
    rows = f.shape[1] // pieces
    at = lambda i: (slice(None), pl.ds(i * rows, rows), slice(None))
    strip = lambda i: pltpu.make_async_copy(r_hbm.at[i], r.at[i], r_sem.at[i])
    fetch = lambda i: pltpu.make_async_copy(f_hbm.at[at(i)], f.at[at(i)], f_sem.at[i])
    store = lambda i: pltpu.make_async_copy(o.at[at(i)], o_hbm.at[at(i)], o_sem.at[i])
    each = pieces // strips
    for i in range(strips):
        strip(i).start()
        for j in range(each):
            fetch(i * each + j).start()
    rows_mix, rows_bias = bypass_rows(zl, w_ref, b_ref)
    mix[...] = rows_mix
    shift[...] = jnp.broadcast_to(rows_bias, shift.shape)
    for i in range(pieces):
        if i % each == 0:
            strip(i // each).wait()
        fetch(i).wait()
        block = f[:, i * rows : (i + 1) * rows, :].astype(F32)
        for y in range(rows // zl):
            plane = block[:, y * zl : (y + 1) * zl, :].reshape(-1, block.shape[2]).astype(BF)
            within = i % each * (rows // zl) + y
            values = jnp.concatenate([r[i // each, h, :, within, :] for h in range(LH)], axis=1)
            made = field_rows(zl, values, plane, mix[...], shift[...], th_ref[...], tl_ref[...])
            o[:, i * rows + y * zl : i * rows + (y + 1) * zl, :] = made.astype(BF)
        store(i).start()
    for i in range(pieces):
        store(i).wait()


def per_device(tables, n_y, n_z, features, spectral_weight, bypass_weight, bias_vector):
    xf, xi, yf, yi, zf, zi = tables
    c, yl, zl, nx = features.shape
    _, kl, _, mz, pairs = spectral_weight.shape
    lanes = c * zl
    tile = lanes // LH
    kp = kl // PARTS
    rows = yl * 2 * kp
    part = LH * 2 * kp
    flat = features.reshape(c, yl * zl, nx)
    x_rows = split(xf).reshape(-1, nx)
    y_rows, y_back = split(yf, 1), split(yi, 1)
    z_rows, z_back = thrice(zf), thrice(zi)
    high, tl = split(xi)
    th = np.concatenate([high, high], 0)
    weight = spectral_weight.reshape(2, kl * mz, pairs)
    bias = bias_vector.reshape(1, c)
    my_rows = y_rows.shape[2]
    modes = my_rows // part
    n_ring = n_y // 2
    reach = n_ring // 2
    strips = yl // STRIP
    operands = [flat] + [jnp.asarray(t) for t in (x_rows, y_rows, y_back, z_rows, z_back)] + [weight]
    hops = PARTS * 2 * reach * GROUP
    turns = PARTS * n_ring
    sems = [16] + [turns] * 2 + [hops] * 2 + [PARTS * n_z] * 4 + [hops] * 2 + [turns] * 3
    planes = pl.pallas_call(
        functools.partial(spectrum_kernel, n_y, n_z, zl),
        out_shape=jax.ShapeDtypeStruct((strips, LH, PARTS, n_y, rows // strips, tile), F32),
        in_specs=[pl.BlockSpec(memory_space=pl.ANY)] * len(operands),
        out_specs=pl.BlockSpec(memory_space=pl.ANY),
        scratch_shapes=[
            pltpu.VMEM(flat.shape, BF),
            pltpu.VMEM(x_rows.shape, BF),
            pltpu.VMEM((2, my_rows, 2 * y_rows.shape[3]), BF),
            pltpu.VMEM((2,) + y_back.shape[1:], BF),
            pltpu.VMEM(z_rows.shape, BF),
            pltpu.VMEM(z_back.shape, BF),
            pltpu.VMEM(weight.shape, BF),
            pltpu.VMEM((PARTS, n_y // 2, 2, rows, lanes), F32),
            pltpu.VMEM((PARTS, n_ring, rows, lanes), F32),
            pltpu.VMEM((PARTS, 2, reach, my_rows, tile), F32),
            pltpu.VMEM((PARTS, 2, reach, my_rows, tile), F32),
            pltpu.VMEM((PARTS, modes, part, tile), F32),
            pltpu.VMEM((PARTS, n_z, part, tile), F32),
            pltpu.VMEM((PARTS, n_z, part, tile), F32),
            pltpu.VMEM((PARTS, modes, part, tile), F32),
            pltpu.VMEM((PARTS, 2, reach, modes, part, tile), F32),
            pltpu.VMEM((PARTS, n_ring, strips, LH, rows // strips, tile), F32),
            pltpu.VMEM((PARTS, n_ring, strips, LH, rows // strips, tile), F32),
        ]
        + [pltpu.SemaphoreType.DMA((n,)) for n in sems],
        compiler_params=pltpu.CompilerParams(
            collective_id=0, has_side_effects=True, vmem_limit_bytes=62 * MIB
        ),
        name="spectrum",
    )(*operands)

    count = PARTS * n_y * 2 * kp
    out = pl.pallas_call(
        functools.partial(field_kernel, zl),
        in_specs=[pl.BlockSpec(memory_space=pl.ANY)] * 2 + [pl.BlockSpec(memory_space=pltpu.VMEM)] * 4,
        out_specs=pl.BlockSpec(memory_space=pl.ANY),
        out_shape=jax.ShapeDtypeStruct(flat.shape, BF),
        scratch_shapes=[
            pltpu.VMEM((strips, LH, count, STRIP, tile), F32),
            pltpu.VMEM(flat.shape, BF),
            pltpu.VMEM(flat.shape, BF),
            pltpu.VMEM((lanes, lanes), BF),
            pltpu.VMEM((lanes, nx), F32),
            pltpu.SemaphoreType.DMA((strips,)),
            pltpu.SemaphoreType.DMA((4,)),
            pltpu.SemaphoreType.DMA((4,)),
        ],
        compiler_params=pltpu.CompilerParams(vmem_limit_bytes=62 * MIB),
        name="field",
    )(
        planes.reshape(strips, LH, count, STRIP, tile),
        flat,
        bypass_weight,
        bias,
        jnp.asarray(th),
        jnp.asarray(tl),
    )
    return out.reshape(features.shape)


def solution(mesh):
    n_y, n_z = mesh.shape["py"], mesh.shape["pz"]

    def run(features, spectral_weight, bypass_weight, bias_vector):
        _, ny, nz, nx = features.shape
        _, mx, my, mz, _ = spectral_weight.shape
        tables = make_tables(nx, ny, nz, mx, my, mz, n_y, n_z)
        return jax.shard_map(
            functools.partial(per_device, tables, n_y, n_z),
            mesh=mesh,
            in_specs=(P(None, "py", "pz", None), P(None, "py", "pz", None, None), P(), P()),
            out_specs=P(None, "py", "pz", None),
            check_vma=False,
        )(features, spectral_weight, bypass_weight, bias_vector)

    return run
```

```python
import functools
import math

import jax
import jax.numpy as jnp
import ml_dtypes
import numpy as np
from jax import lax
from jax.experimental import pallas as pl
from jax.experimental.pallas import tpu as pltpu
from jax.sharding import PartitionSpec as P

MESH = pl.DeviceIdType.MESH
BF = jnp.bfloat16
F32 = jnp.float32
MIB = 1 << 20
PARTS = 2
STRIP = 4
LH = 2
GROUP = 4


def centred(count):
    index = np.arange(count)
    return np.where(index < count // 2, index, index - count)


def split(table, axis=0):
    high = table.astype(ml_dtypes.bfloat16)
    low = (table - high.astype(np.float64)).astype(ml_dtypes.bfloat16)
    return np.stack([high, low], axis)


def thrice(table):
    high, low = split(table)
    return np.concatenate([high, high, low], -1)


def pair(frequencies, positions, period, sign):
    angle = 2.0 * np.pi * ((positions[:, None] * frequencies[None, :]) % period) / period
    c, s = np.cos(angle), np.sin(angle)
    return np.stack([np.stack([c, sign * s]), np.stack([-sign * s, c])])


def make_tables(nx, ny, nz, mx, my, mz, py, pz):
    k = mx // py
    zl = nz // pz
    yl = ny // py
    norm = 1.0 / math.sqrt(nx * ny * nz)
    angle = 2.0 * np.pi * ((np.arange(mx)[:, None] * np.arange(nx)[None, :]) % nx) / nx
    kp = k // PARTS
    eye, pairs = np.eye(kp), np.eye(2)
    xf = np.stack([np.cos(angle) * norm, -np.sin(angle) * norm], 1)
    xf = xf.reshape(py, PARTS, kp, 2, nx).swapaxes(0, 1).reshape(2 * mx, nx)
    weight = np.where(np.arange(mx) == 0, 1.0, 2.0)[:, None] * norm
    xi = np.stack([np.cos(angle) * weight, -np.sin(angle) * weight], 1)
    xi = xi.reshape(py, PARTS, kp, 2, nx).swapaxes(0, 1).reshape(2 * mx, nx)
    order = np.arange(my).reshape(pz // GROUP, GROUP).T.reshape(-1)
    yf = pair(centred(my), np.arange(ny), ny, -1.0)[..., order].reshape(2, 2, py, yl, my)
    yf = np.einsum("pqdyj,kl,hg->djhkqgylp", yf, eye, pairs)
    yf = yf.reshape(py, my * 4 * kp, yl * 4 * kp)
    yi = pair(centred(my), np.arange(ny), ny, 1.0)[..., order].reshape(2, 2, py, yl, my)
    yi = yi.reshape(2, 2, py, yl // STRIP, STRIP, my)
    yi = np.einsum("qrdwyj,kl,hg->dwhykrjglq", yi, eye, pairs)
    yi = yi.reshape(py, yl * 4 * kp, my * 4 * kp)
    zf = pair(centred(mz), np.arange(nz), nz, -1.0).reshape(2, 2, pz, zl, mz)
    zf = np.einsum("pqszm->zqmps", zf).reshape(zl, 2 * mz, 2 * pz)
    zi = pair(centred(mz), np.arange(nz), nz, 1.0).reshape(2, 2, pz // GROUP, GROUP, zl, mz)
    zi = np.einsum("qrjgzm->gzrjqm", zi).reshape(GROUP, zl * 2 * pz // GROUP, 2 * mz)
    return xf, xi, yf, yi, zf, zi


def halves(value):
    high = value.astype(BF)
    return high, (value - high.astype(F32)).astype(BF)


def triple(value):
    high, low = halves(value)
    return jnp.concatenate([high, low, high], 0)


def dot(a, b, dims=((1,), (0,))):
    return lax.dot_general(a, b, (dims, ((), ())), preferred_element_type=F32)


def dot3(ah, al, bh, bl):
    return dot(ah, bh) + dot(al, bh) + dot(ah, bl)


def x_forward(zl, field, table, out, first, last):
    length = field.shape[2]
    parts, owners, two, _, lanes = out.shape

    def step(i, carry):
        block = field[:, pl.ds(pl.multiple_of(i * 2 * zl, 2 * zl), 2 * zl), :].astype(F32)
        planes = []
        for y in range(2):
            plane = block[:, y * zl : (y + 1) * zl, :].reshape(-1, length).astype(BF)
            both = dot(table[...], plane, ((1,), (1,)))
            half = both.shape[0] // 2
            planes.append((both[:half] + both[half:]).reshape(parts * owners, -1, lanes))
        first_y, second_y = planes
        rows = first_y.shape[1]
        upper = lax.broadcasted_iota(jnp.int32, (1, rows, 1), 1) < rows // 2
        turned = lambda v: pltpu.roll(v, rows // 2, 1)
        even = jnp.where(upper, first_y, turned(second_y))
        odd = jnp.where(upper, turned(first_y), second_y)
        at = pl.ds(pl.multiple_of(i * rows, rows), rows)
        for t in range(parts):
            out[t, :, 0, at, :] = even[t * owners : (t + 1) * owners]
            out[t, :, 1, at, :] = odd[t * owners : (t + 1) * owners]
        return carry

    lax.fori_loop(first, last, step, 0)


def mix_modes(zl, x, w, forward, t):
    cells, rows, tile = x.shape
    lanes = LH * tile
    kp = rows // (2 * LH)
    channels = lanes // zl
    row = lambda k, q: jnp.concatenate([x[:, (h * kp + k) * 2 + q, :] for h in range(LH)], axis=1)
    column = lambda k: jnp.concatenate([row(k, 0), row(k, 1)], axis=0)
    block = triple(jnp.concatenate([column(k) for k in range(kp)], axis=1))
    inner = lax.broadcasted_iota(jnp.int32, (1, kp * lanes), 1) % zl
    modes = jnp.zeros((forward.shape[1], kp * lanes), F32)
    for z in range(zl):
        modes += jnp.where(inner == z, dot(forward[z], block), 0.0)
    count = modes.shape[0] // 2
    modes = jnp.concatenate(
        [
            modes[p * count : (p + 1) * count, k * lanes : (k + 1) * lanes]
            for p in range(2)
            for k in range(kp)
        ],
        axis=0,
    )
    pairs = w.shape[2]
    lane = lax.broadcasted_iota(jnp.int32, (lanes, pairs), 0) // zl
    both = lax.broadcasted_iota(jnp.int32, (lanes, pairs), 1)
    spread = jnp.where(lane == both // channels, 1.0, 0.0).astype(BF)
    mh, ml = halves(modes)
    wide = dot(mh, spread) + dot(ml, spread)
    half = wide.shape[0] // 2
    re, im = wide[:half], wide[half:]
    wr = w[0, t * half : (t + 1) * half, :].astype(F32)
    wi = w[1, t * half : (t + 1) * half, :].astype(F32)
    mixed = jnp.concatenate([wr * re - wi * im, wr * im + wi * re], axis=0)
    both = lax.broadcasted_iota(jnp.int32, (pairs, lanes), 0)
    lane = lax.broadcasted_iota(jnp.int32, (pairs, lanes), 1) // zl
    gather = jnp.where(both % channels == lane, 1.0, 0.0).astype(BF)
    ph, plo = halves(mixed)
    summed = dot(ph, gather) + dot(plo, gather)
    part = lambda p, k: summed[(p * kp + k) * count : (p * kp + k + 1) * count]
    columns = [jnp.concatenate([part(0, k), part(1, k)], axis=0) for k in range(kp)]
    return triple(jnp.concatenate(columns, axis=1))


def bypass_rows(zl, w, bias):
    channels = w.shape[0]
    row = lax.broadcasted_iota(jnp.int32, (channels * zl, channels), 0) // zl
    pick = row == lax.broadcasted_iota(jnp.int32, (channels * zl, channels), 1)
    ones = jnp.where(pick, 1.0, 0.0).astype(BF)
    left = dot(ones, w[...], ((1,), (1,))).astype(BF)
    full = dot(left, ones, ((1,), (1,)))
    a = lax.broadcasted_iota(jnp.int32, full.shape, 0) % zl
    b = lax.broadcasted_iota(jnp.int32, full.shape, 1) % zl
    column = jnp.sum(jnp.where(pick, bias[...], 0.0), axis=1, keepdims=True)
    return jnp.where(a == b, full, 0.0).astype(BF), column


def spectrum_kernel(n_y, n_z, zl, *refs):
    (
        f_hbm, xt_hbm, yt_hbm, yi_hbm, zf_hbm, zi_hbm, w_hbm, r_hbm,
        f, xt, yt, yi, zf, zi, w, a, theirs, summing, arrived, total, seen,
        mixed, back, ring, leaving, keeping,
        load_sem, swap_s, swap_r, sum_s, sum_r, out_s, out_r, in_s, in_r, ring_s, ring_r,
        turn_s, turn_r, keep_s,
    ) = refs
    here, column = lax.axis_index("py"), lax.axis_index("pz")
    n_ring = n_y // 2
    side, z = here // n_ring, here % n_ring
    other = 1 - side
    half_py = lambda s, at: s * n_ring + at % n_ring
    partner = {"py": half_py(other, z)}
    neighbours = ({"py": half_py(side, z + 1)}, {"py": half_py(side, z + n_ring - 1)})

    barrier = pltpu.get_barrier_semaphore()
    for peer in (partner,) + neighbours:
        pl.semaphore_signal(barrier, inc=1, device_id=peer, device_id_type=MESH)

    def greet(step, carry):
        pl.semaphore_signal(
            barrier, inc=1, device_id={"pz": (column + step) % n_z}, device_id_type=MESH
        )
        return carry

    loads = []

    def load(source, target):
        copy = pltpu.make_async_copy(source, target, load_sem.at[len(loads)])
        copy.start()
        loads.append(copy)
        return copy

    pieces = 4
    rows = f.shape[1] // pieces
    table_x = load(xt_hbm, xt)
    fields = [
        load(f_hbm.at[:, pl.ds(i * rows, rows), :], f.at[:, pl.ds(i * rows, rows), :])
        for i in range(pieces)
    ]
    lax.fori_loop(1, n_z, greet, 0)

    reach = n_ring // 2
    offsets = [reach] + [o * s for o in range(reach - 1, 0, -1) for s in (1, -1)] + [0]

    def swap(h, i, s):
        at = (z + offsets[i] + n_ring) % n_ring
        half = theirs.shape[2] // 2
        index = (h * n_ring + i) * 2 + s
        return pltpu.make_async_remote_copy(
            src_ref=a.at[h, half_py(other, at) // 2, at % 2, pl.ds(s * half, half)],
            dst_ref=theirs.at[h, at, pl.ds(s * half, half)],
            send_sem=swap_s.at[index],
            recv_sem=swap_r.at[index],
            device_id=partner,
            device_id_type=MESH,
        )

    table_x.wait()
    turns = f.shape[1] // (2 * zl) // pieces
    early = 2
    for i in range(pieces):
        fields[i].wait()
        x_forward(zl, f, xt, a, i * turns, (i + 1) * turns)
        if i == pieces // 2 - 1:
            pl.semaphore_wait(barrier, n_z + 2)
            for j in range(early):
                swap(0, j, 0).start()
    for h in range(PARTS):
        for i in range(n_ring):
            for s in range(2):
                if h > 0 or i >= early or s > 0:
                    swap(h, i, s).start()
    depth = yt_hbm.shape[3]
    table_y = [
        load(yt_hbm.at[half_py(s, z)], yt.at[:, :, pl.ds(i * depth, depth)])
        for i, s in enumerate((side, other))
    ]
    table_z = [load(zf_hbm, zf), load(w_hbm, w), load(zi_hbm, zi)]
    table_i = [load(yi_hbm.at[half_py(s, z)], yi.at[i]) for i, s in enumerate((side, other))]
    for copy in table_y:
        copy.wait()

    def partial(h, i):
        at = (z + offsets[i] + n_ring) % n_ring
        for s in range(2):
            swap(h, i, s).wait_recv()
        rows = (a[h, half_py(side, at) // 2, at % 2], theirs[h, at])
        tile = summing.shape[4]
        block = jnp.concatenate(
            [r[:, i * tile : (i + 1) * tile] for r in rows for i in range(LH)], axis=0
        )
        high, low = halves(block)
        return dot3(yt[0], yt[1], high, low)

    part = total.shape[1] * total.shape[2] // GROUP
    span = lambda g: pl.ds(g * part, part)
    carries = lambda way, step, g: step > 0 or (g < GROUP // 2) == (way == 0)

    def hop(h, way, step, g):
        index = ((h * 2 + way) * reach + step) * GROUP + g
        return pltpu.make_async_remote_copy(
            src_ref=summing.at[h, way, step, span(g)],
            dst_ref=arrived.at[h, way, step, span(g)],
            send_sem=sum_s.at[index],
            recv_sem=sum_r.at[index],
            device_id=neighbours[way],
            device_id_type=MESH,
        )

    def set_out(h):
        block = partial(h, 0)
        for g in range(GROUP):
            way = 0 if g < GROUP // 2 else 1
            summing[h, way, 0, g * part : (g + 1) * part] = block[g * part : (g + 1) * part]
            hop(h, way, 0, g).start()

    def move_on(h, step):
        for way in range(2):
            summing[h, way, step] = partial(h, 2 * step - 1 + way)
        for g in range(GROUP):
            for way in range(2):
                if carries(way, step - 1, g):
                    hop(h, way, step - 1, g).wait_recv()
                    summing[h, way, step, span(g)] += arrived[h, way, step - 1, span(g)]
                hop(h, way, step, g).start()

    per = n_z // GROUP
    y_chip, place = column // GROUP, column % GROUP
    far_first = lambda i: (y_chip + per // 2 + (i + 1) // 2 * (1 - i % 2 * 2) + per) % per
    slot = place * per + y_chip

    def to_owner(h, source, owner, target):
        return pltpu.make_async_remote_copy(
            src_ref=total.at[h, source],
            dst_ref=seen.at[h, target],
            send_sem=out_s.at[h * n_z + owner],
            recv_sem=out_r.at[h * n_z + target],
            device_id={"pz": owner},
            device_id_type=MESH,
        )

    def arrive(h):
        last = partial(h, n_ring - 1)
        for g in range(GROUP):
            for way in range(2):
                hop(h, way, reach - 1, g).wait_recv()
            value = last[g * part : (g + 1) * part] + arrived[h, 0, reach - 1, span(g)]
            value = value + arrived[h, 1, reach - 1, span(g)]
            total[h, g * per : (g + 1) * per] = value.reshape((per,) + total.shape[2:])

            def send(i, carry):
                chip = far_first(i)
                owner = chip * GROUP + g

                @pl.when(owner != column)
                def _():
                    to_owner(h, g * per + chip, owner, column).start()

                return carry

            lax.fori_loop(0, per, send, 0)
        seen[h, column] = total[h, slot]

    def collect(h):
        def one(step, carry):
            peer = (column + step) % n_z
            to_owner(h, 0, peer, peer).wait()
            return carry

        lax.fori_loop(1, n_z, one, 0)

    def to_cells(h, source, peer, target, sender):
        return pltpu.make_async_remote_copy(
            src_ref=mixed.at[h, source],
            dst_ref=back.at[h, target],
            send_sem=in_s.at[h * n_z + peer],
            recv_sem=in_r.at[h * n_z + sender],
            device_id={"pz": peer},
            device_id_type=MESH,
        )

    tile = seen.shape[3]
    kp = seen.shape[2] // (2 * LH)
    lanes = LH * tile
    inner = lax.broadcasted_iota(jnp.int32, (1, kp * lanes), 1) % zl

    def mix_and_return(h):
        modes = mix_modes(zl, seen.at[h], w, zf, h)
        for g in range(GROUP):
            value = dot(zi[g], modes)
            size = 2 * per
            cells = jnp.zeros((size, modes.shape[1]), F32)
            for i in range(zl):
                cells += jnp.where(inner == i, value[i * size : (i + 1) * size], 0.0)
            for p in range(2):
                for k in range(kp):
                    for i in range(LH):
                        mixed[h, g * per : (g + 1) * per, (i * kp + k) * 2 + p, :] = cells[
                            p * per : (p + 1) * per,
                            k * lanes + i * tile : k * lanes + (i + 1) * tile,
                        ]

            def send_back(i, carry):
                chip = far_first(i)
                peer = chip * GROUP + g

                @pl.when(peer != column)
                def _():
                    to_cells(h, g * per + chip, peer, slot, column).start()

                return carry

            lax.fori_loop(0, per, send_back, 0)
        back[h, slot] = mixed[h, slot]

    def end_back(h):
        def one(step, carry):
            peer = (column + step) % n_z
            to_cells(h, 0, peer, 0, peer).wait()
            return carry

        lax.fori_loop(1, n_z, one, 0)

    wide = lambda g: pl.ds(g * per, per)
    passes = lambda way, step, g: step < reach - 1 or (g < GROUP // 2) == (way == 0)

    def relay(h, way, step, g):
        index = ((h * 2 + way) * reach + step) * GROUP + g
        source = back.at[h, wide(g)] if step == 0 else ring.at[h, way, step - 1, wide(g)]
        target = ring.at[h, 0 if step == reach - 1 else way, step, wide(g)]
        return pltpu.make_async_remote_copy(
            src_ref=source,
            dst_ref=target,
            send_sem=ring_s.at[index],
            recv_sem=ring_r.at[index],
            device_id=neighbours[way],
            device_id_type=MESH,
        )

    def turn(h, i, owner):
        return pltpu.make_async_remote_copy(
            src_ref=leaving.at[h, i],
            dst_ref=r_hbm.at[:, :, h, owner],
            send_sem=turn_s.at[h * n_ring + i],
            recv_sem=turn_r.at[h * n_ring + i],
            device_id=partner,
            device_id_type=MESH,
        )

    def keep(h, i, owner):
        return pltpu.make_async_copy(
            keeping.at[h, i], r_hbm.at[:, :, h, owner], keep_s.at[h * n_ring + i]
        )

    def spread(h, i, offset, block):
        owner = half_py(side, z + offset + n_ring)
        high, low = halves(block.reshape(-1, block.shape[2]))
        leaving[h, i] = dot3(yi[1, 0], yi[1, 1], high, low).reshape(leaving.shape[2:])
        turn(h, i, owner).start()
        keeping[h, i] = dot3(yi[0, 0], yi[0, 1], high, low).reshape(keeping.shape[2:])
        keep(h, i, owner).start()

    def send_own(h):
        for g in range(GROUP):
            for way in range(2):
                relay(h, way, 0, g).start()

    def pass_on(h, step):
        for g in range(GROUP):
            for way in range(2):
                if passes(way, step - 1, g):
                    relay(h, way, step - 1, g).wait_recv()
                if step < reach and passes(way, step, g):
                    relay(h, way, step, g).start()

    def spread_pair(h, step):
        if step == reach:
            spread(h, n_ring - 1, reach, ring[h, 0, reach - 1])
        else:
            for way in range(2):
                spread(h, 2 * step - 1 + way, step if way else -step, ring[h, way, step - 1])

    set_out(0)
    for step in range(1, reach):
        move_on(0, step)
    set_out(1)
    arrive(0)
    for step in range(1, reach - 1):
        move_on(1, step)
    for copy in table_z:
        copy.wait()
    collect(0)
    mix_and_return(0)
    move_on(1, reach - 1)
    arrive(1)
    for copy in table_i:
        copy.wait()
    end_back(0)
    send_own(0)
    spread(0, 0, 0, back[0])
    pass_on(0, 1)
    spread_pair(0, 1)
    collect(1)
    mix_and_return(1)
    for step in range(2, reach):
        pass_on(0, step)
        spread_pair(0, step)
    end_back(1)
    send_own(1)
    spread(1, 0, 0, back[1])
    pass_on(0, reach)
    spread_pair(0, reach)
    for step in range(1, reach + 1):
        pass_on(1, step)
        spread_pair(1, step)

    for h in range(PARTS):
        for i in range(n_ring):
            for s in range(2):
                swap(h, i, s).wait_send()
            keep(h, i, here).wait()
            turn(h, i, here).wait()
        for step in range(reach):
            for g in range(GROUP):
                for way in range(2):
                    if carries(way, step, g):
                        hop(h, way, step, g).wait_send()
                    if passes(way, step, g):
                        relay(h, way, step, g).wait_send()


def field_kernel(zl, r_ref, f_ref, w_ref, b_ref, th_ref, tl_ref, o_ref, mix, shift):
    @pl.when(pl.program_id(0) == 0)
    def _():
        rows_mix, rows_bias = bypass_rows(zl, w_ref, b_ref)
        mix[...] = rows_mix
        shift[...] = jnp.broadcast_to(rows_bias, shift.shape)

    block = f_ref[...].astype(F32)
    rows = r_ref.shape[3] * 2 // STRIP
    for pair in range(STRIP // 2):
        tiles = [
            r_ref[0, h, :, pair * rows : (pair + 1) * rows, :].reshape(-1, r_ref.shape[4])
            for h in range(LH)
        ]
        high, low = halves(jnp.concatenate(tiles, axis=1).T)
        for i in range(2):
            y = pair * 2 + i
            plane = block[:, y * zl : (y + 1) * zl, :].reshape(-1, block.shape[2]).astype(BF)
            value = dot(high, th_ref[i]) + dot(low, th_ref[i]) + dot(high, tl_ref[i])
            value = value + dot(mix[...], plane) + shift[...]
            out = jax.nn.gelu(value).reshape(block.shape[0], zl, block.shape[2])
            o_ref[:, y * zl : (y + 1) * zl, :] = out.astype(BF)


def whole(shape):
    return pl.BlockSpec(shape, lambda i: (0,) * len(shape))


def per_device(tables, n_y, n_z, features, spectral_weight, bypass_weight, bias_vector):
    xf, xi, yf, yi, zf, zi = tables
    c, yl, zl, nx = features.shape
    _, kl, _, mz, pairs = spectral_weight.shape
    lanes = c * zl
    tile = lanes // LH
    kp = kl // PARTS
    rows = yl * 2 * kp
    part = LH * 2 * kp
    flat = features.reshape(c, yl * zl, nx)
    x_rows = split(xf).reshape(-1, nx)
    y_rows, y_back = split(yf, 1), split(yi, 1)
    z_rows, z_back = thrice(zf), thrice(zi)
    pair_rows = np.einsum("ekx,yw->weykx", xi.reshape(PARTS * n_y, -1, nx), np.eye(2))
    th, tl = split(pair_rows.reshape(2, -1, nx))
    weight = spectral_weight.reshape(2, kl * mz, pairs)
    bias = bias_vector.reshape(1, c)
    my_rows = y_rows.shape[2]
    modes = my_rows // part
    n_ring = n_y // 2
    reach = n_ring // 2
    strips = yl // STRIP
    operands = [flat] + [jnp.asarray(t) for t in (x_rows, y_rows, y_back, z_rows, z_back)] + [weight]
    hops = PARTS * 2 * reach * GROUP
    turns = PARTS * n_ring
    sems = [16] + [turns * 2] * 2 + [hops] * 2 + [PARTS * n_z] * 4 + [hops] * 2 + [turns] * 3
    planes = pl.pallas_call(
        functools.partial(spectrum_kernel, n_y, n_z, zl),
        out_shape=jax.ShapeDtypeStruct((strips, LH, PARTS, n_y, rows // strips, tile), F32),
        in_specs=[pl.BlockSpec(memory_space=pl.ANY)] * len(operands),
        out_specs=pl.BlockSpec(memory_space=pl.ANY),
        scratch_shapes=[
            pltpu.VMEM(flat.shape, BF),
            pltpu.VMEM(x_rows.shape, BF),
            pltpu.VMEM((2, my_rows, 2 * y_rows.shape[3]), BF),
            pltpu.VMEM((2,) + y_back.shape[1:], BF),
            pltpu.VMEM(z_rows.shape, BF),
            pltpu.VMEM(z_back.shape, BF),
            pltpu.VMEM(weight.shape, BF),
            pltpu.VMEM((PARTS, n_y // 2, 2, rows, lanes), F32),
            pltpu.VMEM((PARTS, n_ring, rows, lanes), F32),
            pltpu.VMEM((PARTS, 2, reach, my_rows, tile), F32),
            pltpu.VMEM((PARTS, 2, reach, my_rows, tile), F32),
            pltpu.VMEM((PARTS, modes, part, tile), F32),
            pltpu.VMEM((PARTS, n_z, part, tile), F32),
            pltpu.VMEM((PARTS, n_z, part, tile), F32),
            pltpu.VMEM((PARTS, modes, part, tile), F32),
            pltpu.VMEM((PARTS, 2, reach, modes, part, tile), F32),
            pltpu.VMEM((PARTS, n_ring, strips, LH, rows // strips, tile), F32),
            pltpu.VMEM((PARTS, n_ring, strips, LH, rows // strips, tile), F32),
        ]
        + [pltpu.SemaphoreType.DMA((n,)) for n in sems],
        compiler_params=pltpu.CompilerParams(
            collective_id=0, has_side_effects=True, vmem_limit_bytes=62 * MIB
        ),
        name="spectrum",
    )(*operands)

    block = pl.BlockSpec((c, STRIP * zl, nx), lambda i: (0, i, 0))
    planes = planes.reshape(strips, LH, PARTS * n_y, rows // strips, tile)
    out = pl.pallas_call(
        functools.partial(field_kernel, zl),
        grid=(strips,),
        in_specs=[
            pl.BlockSpec((1,) + planes.shape[1:], lambda i: (i, 0, 0, 0, 0)),
            block,
            whole(bypass_weight.shape),
            whole(bias.shape),
            whole(th.shape),
            whole(tl.shape),
        ],
        out_specs=block,
        out_shape=jax.ShapeDtypeStruct(flat.shape, BF),
        scratch_shapes=[pltpu.VMEM((lanes, lanes), BF), pltpu.VMEM((lanes, nx), F32)],
        compiler_params=pltpu.CompilerParams(vmem_limit_bytes=62 * MIB),
        name="field",
    )(planes, flat, bypass_weight, bias, jnp.asarray(th), jnp.asarray(tl))
    return out.reshape(features.shape)


def solution(mesh):
    n_y, n_z = mesh.shape["py"], mesh.shape["pz"]

    def run(features, spectral_weight, bypass_weight, bias_vector):
        _, ny, nz, nx = features.shape
        _, mx, my, mz, _ = spectral_weight.shape
        tables = make_tables(nx, ny, nz, mx, my, mz, n_y, n_z)
        return jax.shard_map(
            functools.partial(per_device, tables, n_y, n_z),
            mesh=mesh,
            in_specs=(P(None, "py", "pz", None), P(None, "py", "pz", None, None), P(), P()),
            out_specs=P(None, "py", "pz", None),
            check_vma=False,
        )(features, spectral_weight, bypass_weight, bias_vector)

    return run
```

```python
import functools
import math

import jax
import jax.numpy as jnp
import ml_dtypes
import numpy as np
from jax import lax
from jax.experimental import pallas as pl
from jax.experimental.pallas import tpu as pltpu
from jax.sharding import PartitionSpec as P

MESH = pl.DeviceIdType.MESH
BF = jnp.bfloat16
F32 = jnp.float32
MIB = 1 << 20
PARTS = 2
STRIP = 4
LH = 2
GROUP = 4


def centred(count):
    index = np.arange(count)
    return np.where(index < count // 2, index, index - count)


def split(table, axis=0):
    high = table.astype(ml_dtypes.bfloat16)
    low = (table - high.astype(np.float64)).astype(ml_dtypes.bfloat16)
    return np.stack([high, low], axis)


def thrice(table):
    high, low = split(table)
    return np.concatenate([high, high, low], -1)


def pair(frequencies, positions, period, sign):
    angle = 2.0 * np.pi * ((positions[:, None] * frequencies[None, :]) % period) / period
    c, s = np.cos(angle), np.sin(angle)
    return np.stack([np.stack([c, sign * s]), np.stack([-sign * s, c])])


def make_tables(nx, ny, nz, mx, my, mz, py, pz):
    k = mx // py
    zl = nz // pz
    yl = ny // py
    norm = 1.0 / math.sqrt(nx * ny * nz)
    angle = 2.0 * np.pi * ((np.arange(mx)[:, None] * np.arange(nx)[None, :]) % nx) / nx
    kp = k // PARTS
    eye, pairs = np.eye(kp), np.eye(2)
    xf = np.stack([np.cos(angle) * norm, -np.sin(angle) * norm], 1)
    xf = xf.reshape(py, PARTS, kp, 2, nx).swapaxes(0, 1).reshape(2 * mx, nx)
    weight = np.where(np.arange(mx) == 0, 1.0, 2.0)[:, None] * norm
    xi = np.stack([np.cos(angle) * weight, -np.sin(angle) * weight], 1)
    xi = xi.reshape(py, PARTS, kp, 2, nx).swapaxes(0, 1).reshape(2 * mx, nx)
    order = np.arange(my).reshape(pz // GROUP, GROUP).T.reshape(-1)
    yf = pair(centred(my), np.arange(ny), ny, -1.0)[..., order].reshape(2, 2, py, yl, my)
    yf = np.einsum("pqdyj,kl,hg->djhkqgylp", yf, eye, pairs)
    yf = yf.reshape(py, my * 4 * kp, yl * 4 * kp)
    yi = pair(centred(my), np.arange(ny), ny, 1.0)[..., order].reshape(2, 2, py, yl, my)
    yi = yi.reshape(2, 2, py, yl // STRIP, STRIP, my)
    yi = np.einsum("qrdwyj,kl,hg->dwhykrjglq", yi, eye, pairs)
    yi = yi.reshape(py, yl * 4 * kp, my * 4 * kp)
    zf = pair(centred(mz), np.arange(nz), nz, -1.0).reshape(2, 2, pz, zl, mz)
    zf = np.einsum("pqszm->zqmps", zf).reshape(zl, 2 * mz, 2 * pz)
    zi = pair(centred(mz), np.arange(nz), nz, 1.0).reshape(2, 2, pz // GROUP, GROUP, zl, mz)
    zi = np.einsum("qrjgzm->gzrjqm", zi).reshape(GROUP, zl * 2 * pz // GROUP, 2 * mz)
    return xf, xi, yf, yi, zf, zi


def halves(value):
    high = value.astype(BF)
    return high, (value - high.astype(F32)).astype(BF)


def triple(value):
    high, low = halves(value)
    return jnp.concatenate([high, low, high], 0)


def dot(a, b, dims=((1,), (0,))):
    return lax.dot_general(a, b, (dims, ((), ())), preferred_element_type=F32)


def dot3(ah, al, bh, bl):
    return dot(ah, bh) + dot(al, bh) + dot(ah, bl)


def x_forward(zl, field, table, out, first, last):
    length = field.shape[2]
    parts, owners, two, _, lanes = out.shape

    def step(i, carry):
        block = field[:, pl.ds(pl.multiple_of(i * 2 * zl, 2 * zl), 2 * zl), :].astype(F32)
        planes = []
        for y in range(2):
            plane = block[:, y * zl : (y + 1) * zl, :].reshape(-1, length).astype(BF)
            both = dot(table[...], plane, ((1,), (1,)))
            half = both.shape[0] // 2
            planes.append((both[:half] + both[half:]).reshape(parts * owners, -1, lanes))
        first_y, second_y = planes
        rows = first_y.shape[1]
        upper = lax.broadcasted_iota(jnp.int32, (1, rows, 1), 1) < rows // 2
        turned = lambda v: pltpu.roll(v, rows // 2, 1)
        even = jnp.where(upper, first_y, turned(second_y))
        odd = jnp.where(upper, turned(first_y), second_y)
        at = pl.ds(pl.multiple_of(i * rows, rows), rows)
        for t in range(parts):
            out[t, :, 0, at, :] = even[t * owners : (t + 1) * owners]
            out[t, :, 1, at, :] = odd[t * owners : (t + 1) * owners]
        return carry

    lax.fori_loop(first, last, step, 0)


def mix_modes(zl, x, w, forward, t):
    cells, rows, tile = x.shape
    lanes = LH * tile
    kp = rows // (2 * LH)
    channels = lanes // zl
    row = lambda k, q: jnp.concatenate([x[:, (h * kp + k) * 2 + q, :] for h in range(LH)], axis=1)
    column = lambda k: jnp.concatenate([row(k, 0), row(k, 1)], axis=0)
    block = triple(jnp.concatenate([column(k) for k in range(kp)], axis=1))
    inner = lax.broadcasted_iota(jnp.int32, (1, kp * lanes), 1) % zl
    modes = jnp.zeros((forward.shape[1], kp * lanes), F32)
    for z in range(zl):
        modes += jnp.where(inner == z, dot(forward[z], block), 0.0)
    count = modes.shape[0] // 2
    modes = jnp.concatenate(
        [
            modes[p * count : (p + 1) * count, k * lanes : (k + 1) * lanes]
            for p in range(2)
            for k in range(kp)
        ],
        axis=0,
    )
    pairs = w.shape[2]
    lane = lax.broadcasted_iota(jnp.int32, (lanes, pairs), 0) // zl
    both = lax.broadcasted_iota(jnp.int32, (lanes, pairs), 1)
    spread = jnp.where(lane == both // channels, 1.0, 0.0).astype(BF)
    mh, ml = halves(modes)
    wide = dot(mh, spread) + dot(ml, spread)
    half = wide.shape[0] // 2
    re, im = wide[:half], wide[half:]
    wr = w[0, t * half : (t + 1) * half, :].astype(F32)
    wi = w[1, t * half : (t + 1) * half, :].astype(F32)
    mixed = jnp.concatenate([wr * re - wi * im, wr * im + wi * re], axis=0)
    both = lax.broadcasted_iota(jnp.int32, (pairs, lanes), 0)
    lane = lax.broadcasted_iota(jnp.int32, (pairs, lanes), 1) // zl
    gather = jnp.where(both % channels == lane, 1.0, 0.0).astype(BF)
    ph, plo = halves(mixed)
    summed = dot(ph, gather) + dot(plo, gather)
    part = lambda p, k: summed[(p * kp + k) * count : (p * kp + k + 1) * count]
    columns = [jnp.concatenate([part(0, k), part(1, k)], axis=0) for k in range(kp)]
    return triple(jnp.concatenate(columns, axis=1))


def bypass_rows(zl, w, bias):
    channels = w.shape[0]
    row = lax.broadcasted_iota(jnp.int32, (channels * zl, channels), 0) // zl
    pick = row == lax.broadcasted_iota(jnp.int32, (channels * zl, channels), 1)
    ones = jnp.where(pick, 1.0, 0.0).astype(BF)
    left = dot(ones, w[...], ((1,), (1,))).astype(BF)
    full = dot(left, ones, ((1,), (1,)))
    a = lax.broadcasted_iota(jnp.int32, full.shape, 0) % zl
    b = lax.broadcasted_iota(jnp.int32, full.shape, 1) % zl
    column = jnp.sum(jnp.where(pick, bias[...], 0.0), axis=1, keepdims=True)
    return jnp.where(a == b, full, 0.0).astype(BF), column


def spectrum_kernel(n_y, n_z, zl, *refs):
    (
        f_hbm, xt_hbm, yt_hbm, yi_hbm, zf_hbm, zi_hbm, w_hbm, r_hbm,
        f, xt, yt, yi, zf, zi, w, a, theirs, summing, arrived, total, seen,
        mixed, back, ring, leaving, keeping,
        load_sem, swap_s, swap_r, sum_s, sum_r, out_s, out_r, in_s, in_r, ring_s, ring_r,
        turn_s, turn_r, keep_s,
    ) = refs
    here, column = lax.axis_index("py"), lax.axis_index("pz")
    n_ring = n_y // 2
    side, z = here // n_ring, here % n_ring
    other = 1 - side
    half_py = lambda s, at: s * n_ring + at % n_ring
    partner = {"py": half_py(other, z)}
    neighbours = ({"py": half_py(side, z + 1)}, {"py": half_py(side, z + n_ring - 1)})

    barrier = pltpu.get_barrier_semaphore()
    for peer in (partner,) + neighbours:
        pl.semaphore_signal(barrier, inc=1, device_id=peer, device_id_type=MESH)

    def greet(step, carry):
        pl.semaphore_signal(
            barrier, inc=1, device_id={"pz": (column + step) % n_z}, device_id_type=MESH
        )
        return carry

    loads = []

    def load(source, target):
        copy = pltpu.make_async_copy(source, target, load_sem.at[len(loads)])
        copy.start()
        loads.append(copy)
        return copy

    pieces = 4
    rows = f.shape[1] // pieces
    table_x = load(xt_hbm, xt)
    fields = [
        load(f_hbm.at[:, pl.ds(i * rows, rows), :], f.at[:, pl.ds(i * rows, rows), :])
        for i in range(pieces)
    ]
    lax.fori_loop(1, n_z, greet, 0)

    reach = n_ring // 2
    offsets = [reach] + [o * s for o in range(reach - 1, 0, -1) for s in (1, -1)] + [0]

    def swap(h, i, s):
        at = (z + offsets[i] + n_ring) % n_ring
        half = theirs.shape[2] // 2
        index = (h * n_ring + i) * 2 + s
        return pltpu.make_async_remote_copy(
            src_ref=a.at[h, half_py(other, at) // 2, at % 2, pl.ds(s * half, half)],
            dst_ref=theirs.at[h, at, pl.ds(s * half, half)],
            send_sem=swap_s.at[index],
            recv_sem=swap_r.at[index],
            device_id=partner,
            device_id_type=MESH,
        )

    table_x.wait()
    turns = f.shape[1] // (2 * zl) // pieces
    early = 2
    for i in range(pieces):
        fields[i].wait()
        x_forward(zl, f, xt, a, i * turns, (i + 1) * turns)
        if i == pieces // 2 - 1:
            pl.semaphore_wait(barrier, n_z + 2)
            for j in range(early):
                swap(0, j, 0).start()
    for h in range(PARTS):
        for i in range(n_ring):
            for s in range(2):
                if h > 0 or i >= early or s > 0:
                    swap(h, i, s).start()
    depth = yt_hbm.shape[3]
    table_y = [
        load(yt_hbm.at[half_py(s, z)], yt.at[:, :, pl.ds(i * depth, depth)])
        for i, s in enumerate((side, other))
    ]
    table_z = [load(zf_hbm, zf), load(w_hbm, w), load(zi_hbm, zi)]
    table_i = [load(yi_hbm.at[half_py(s, z)], yi.at[i]) for i, s in enumerate((side, other))]
    for copy in table_y:
        copy.wait()

    def partial(h, i):
        at = (z + offsets[i] + n_ring) % n_ring
        for s in range(2):
            swap(h, i, s).wait_recv()
        rows = (a[h, half_py(side, at) // 2, at % 2], theirs[h, at])
        tile = summing.shape[4]
        block = jnp.concatenate(
            [r[:, i * tile : (i + 1) * tile] for r in rows for i in range(LH)], axis=0
        )
        high, low = halves(block)
        return dot3(yt[0], yt[1], high, low)

    part = total.shape[1] * total.shape[2] // GROUP
    span = lambda g: pl.ds(g * part, part)
    carries = lambda way, step, g: step > 0 or (g < GROUP // 2) == (way == 0)

    def hop(h, way, step, g):
        index = ((h * 2 + way) * reach + step) * GROUP + g
        return pltpu.make_async_remote_copy(
            src_ref=summing.at[h, way, step, span(g)],
            dst_ref=arrived.at[h, way, step, span(g)],
            send_sem=sum_s.at[index],
            recv_sem=sum_r.at[index],
            device_id=neighbours[way],
            device_id_type=MESH,
        )

    def set_out(h):
        block = partial(h, 0)
        for g in range(GROUP):
            way = 0 if g < GROUP // 2 else 1
            summing[h, way, 0, g * part : (g + 1) * part] = block[g * part : (g + 1) * part]
            hop(h, way, 0, g).start()

    def move_on(h, step):
        for way in range(2):
            summing[h, way, step] = partial(h, 2 * step - 1 + way)
        for g in range(GROUP):
            for way in range(2):
                if carries(way, step - 1, g):
                    hop(h, way, step - 1, g).wait_recv()
                    summing[h, way, step, span(g)] += arrived[h, way, step - 1, span(g)]
                hop(h, way, step, g).start()

    per = n_z // GROUP
    y_chip, place = column // GROUP, column % GROUP
    far_first = lambda i: (y_chip + per // 2 + (i + 1) // 2 * (1 - i % 2 * 2) + per) % per
    slot = place * per + y_chip

    def to_owner(h, source, owner, target):
        return pltpu.make_async_remote_copy(
            src_ref=total.at[h, source],
            dst_ref=seen.at[h, target],
            send_sem=out_s.at[h * n_z + owner],
            recv_sem=out_r.at[h * n_z + target],
            device_id={"pz": owner},
            device_id_type=MESH,
        )

    def arrive(h):
        last = partial(h, n_ring - 1)
        for g in range(GROUP):
            for way in range(2):
                hop(h, way, reach - 1, g).wait_recv()
            value = last[g * part : (g + 1) * part] + arrived[h, 0, reach - 1, span(g)]
            value = value + arrived[h, 1, reach - 1, span(g)]
            total[h, g * per : (g + 1) * per] = value.reshape((per,) + total.shape[2:])

            def send(i, carry):
                chip = far_first(i)
                owner = chip * GROUP + g

                @pl.when(owner != column)
                def _():
                    to_owner(h, g * per + chip, owner, column).start()

                return carry

            lax.fori_loop(0, per, send, 0)
        seen[h, column] = total[h, slot]

    def collect(h):
        def one(step, carry):
            peer = (column + step) % n_z
            to_owner(h, 0, peer, peer).wait()
            return carry

        lax.fori_loop(1, n_z, one, 0)

    def to_cells(h, source, peer, target, sender):
        return pltpu.make_async_remote_copy(
            src_ref=mixed.at[h, source],
            dst_ref=back.at[h, target],
            send_sem=in_s.at[h * n_z + peer],
            recv_sem=in_r.at[h * n_z + sender],
            device_id={"pz": peer},
            device_id_type=MESH,
        )

    tile = seen.shape[3]
    kp = seen.shape[2] // (2 * LH)
    lanes = LH * tile
    inner = lax.broadcasted_iota(jnp.int32, (1, kp * lanes), 1) % zl

    def mix_and_return(h):
        modes = mix_modes(zl, seen.at[h], w, zf, h)
        for g in range(GROUP):
            value = dot(zi[g], modes)
            size = 2 * per
            cells = jnp.zeros((size, modes.shape[1]), F32)
            for i in range(zl):
                cells += jnp.where(inner == i, value[i * size : (i + 1) * size], 0.0)
            for p in range(2):
                for k in range(kp):
                    for i in range(LH):
                        mixed[h, g * per : (g + 1) * per, (i * kp + k) * 2 + p, :] = cells[
                            p * per : (p + 1) * per,
                            k * lanes + i * tile : k * lanes + (i + 1) * tile,
                        ]

            def send_back(i, carry):
                chip = far_first(i)
                peer = chip * GROUP + g

                @pl.when(peer != column)
                def _():
                    to_cells(h, g * per + chip, peer, slot, column).start()

                return carry

            lax.fori_loop(0, per, send_back, 0)
        back[h, slot] = mixed[h, slot]

    def end_back(h):
        def one(step, carry):
            peer = (column + step) % n_z
            to_cells(h, 0, peer, 0, peer).wait()
            return carry

        lax.fori_loop(1, n_z, one, 0)

    wide = lambda g: pl.ds(g * per, per)
    passes = lambda way, step, g: step < reach - 1 or (g < GROUP // 2) == (way == 0)

    def relay(h, way, step, g):
        index = ((h * 2 + way) * reach + step) * GROUP + g
        source = back.at[h, wide(g)] if step == 0 else ring.at[h, way, step - 1, wide(g)]
        target = ring.at[h, 0 if step == reach - 1 else way, step, wide(g)]
        return pltpu.make_async_remote_copy(
            src_ref=source,
            dst_ref=target,
            send_sem=ring_s.at[index],
            recv_sem=ring_r.at[index],
            device_id=neighbours[way],
            device_id_type=MESH,
        )

    def turn(h, i, owner):
        return pltpu.make_async_remote_copy(
            src_ref=leaving.at[h, i],
            dst_ref=r_hbm.at[h, owner],
            send_sem=turn_s.at[h * n_ring + i],
            recv_sem=turn_r.at[h * n_ring + i],
            device_id=partner,
            device_id_type=MESH,
        )

    def keep(h, i, owner):
        return pltpu.make_async_copy(
            keeping.at[h, i], r_hbm.at[h, owner], keep_s.at[h * n_ring + i]
        )

    def spread(h, i, offset, block):
        owner = half_py(side, z + offset + n_ring)
        high, low = halves(block.reshape(-1, block.shape[2]))
        leaving[h, i] = dot3(yi[1, 0], yi[1, 1], high, low).reshape(leaving.shape[2:])
        turn(h, i, owner).start()
        keeping[h, i] = dot3(yi[0, 0], yi[0, 1], high, low).reshape(keeping.shape[2:])
        keep(h, i, owner).start()

    def send_own(h):
        for g in range(GROUP):
            for way in range(2):
                relay(h, way, 0, g).start()

    def pass_on(h, step):
        for g in range(GROUP):
            for way in range(2):
                if passes(way, step - 1, g):
                    relay(h, way, step - 1, g).wait_recv()
                if step < reach and passes(way, step, g):
                    relay(h, way, step, g).start()

    def spread_pair(h, step):
        if step == reach:
            spread(h, n_ring - 1, reach, ring[h, 0, reach - 1])
        else:
            for way in range(2):
                spread(h, 2 * step - 1 + way, step if way else -step, ring[h, way, step - 1])

    set_out(0)
    for step in range(1, reach):
        move_on(0, step)
    set_out(1)
    arrive(0)
    for step in range(1, reach - 1):
        move_on(1, step)
    for copy in table_z:
        copy.wait()
    collect(0)
    mix_and_return(0)
    move_on(1, reach - 1)
    arrive(1)
    for copy in table_i:
        copy.wait()
    end_back(0)
    send_own(0)
    spread(0, 0, 0, back[0])
    pass_on(0, 1)
    spread_pair(0, 1)
    collect(1)
    mix_and_return(1)
    for step in range(2, reach):
        pass_on(0, step)
        spread_pair(0, step)
    end_back(1)
    send_own(1)
    spread(1, 0, 0, back[1])
    pass_on(0, reach)
    spread_pair(0, reach)
    for step in range(1, reach + 1):
        pass_on(1, step)
        spread_pair(1, step)

    for h in range(PARTS):
        for i in range(n_ring):
            for s in range(2):
                swap(h, i, s).wait_send()
            keep(h, i, here).wait()
            turn(h, i, here).wait()
        for step in range(reach):
            for g in range(GROUP):
                for way in range(2):
                    if carries(way, step, g):
                        hop(h, way, step, g).wait_send()
                    if passes(way, step, g):
                        relay(h, way, step, g).wait_send()


def field_kernel(zl, r_ref, f_ref, w_ref, b_ref, th_ref, tl_ref, o_ref, mix, shift):
    @pl.when(pl.program_id(0) == 0)
    def _():
        rows_mix, rows_bias = bypass_rows(zl, w_ref, b_ref)
        mix[...] = rows_mix
        shift[...] = jnp.broadcast_to(rows_bias, shift.shape)

    block = f_ref[...].astype(F32)
    rows = r_ref.shape[3] * 2 // STRIP
    for pair in range(STRIP // 2):
        tiles = [
            r_ref[:, 0, h, pair * rows : (pair + 1) * rows, :].reshape(-1, r_ref.shape[4])
            for h in range(LH)
        ]
        high, low = halves(jnp.concatenate(tiles, axis=1).T)
        for i in range(2):
            y = pair * 2 + i
            plane = block[:, y * zl : (y + 1) * zl, :].reshape(-1, block.shape[2]).astype(BF)
            value = dot(high, th_ref[i]) + dot(low, th_ref[i]) + dot(high, tl_ref[i])
            value = value + dot(mix[...], plane) + shift[...]
            out = jax.nn.gelu(value).reshape(block.shape[0], zl, block.shape[2])
            o_ref[:, y * zl : (y + 1) * zl, :] = out.astype(BF)


def whole(shape):
    return pl.BlockSpec(shape, lambda i: (0,) * len(shape))


def per_device(tables, n_y, n_z, features, spectral_weight, bypass_weight, bias_vector):
    xf, xi, yf, yi, zf, zi = tables
    c, yl, zl, nx = features.shape
    _, kl, _, mz, pairs = spectral_weight.shape
    lanes = c * zl
    tile = lanes // LH
    kp = kl // PARTS
    rows = yl * 2 * kp
    part = LH * 2 * kp
    flat = features.reshape(c, yl * zl, nx)
    x_rows = split(xf).reshape(-1, nx)
    y_rows, y_back = split(yf, 1), split(yi, 1)
    z_rows, z_back = thrice(zf), thrice(zi)
    pair_rows = np.einsum("ekx,yw->weykx", xi.reshape(PARTS * n_y, -1, nx), np.eye(2))
    th, tl = split(pair_rows.reshape(2, -1, nx))
    weight = spectral_weight.reshape(2, kl * mz, pairs)
    bias = bias_vector.reshape(1, c)
    my_rows = y_rows.shape[2]
    modes = my_rows // part
    n_ring = n_y // 2
    reach = n_ring // 2
    strips = yl // STRIP
    operands = [flat] + [jnp.asarray(t) for t in (x_rows, y_rows, y_back, z_rows, z_back)] + [weight]
    hops = PARTS * 2 * reach * GROUP
    turns = PARTS * n_ring
    sems = [16] + [turns * 2] * 2 + [hops] * 2 + [PARTS * n_z] * 4 + [hops] * 2 + [turns] * 3
    planes = pl.pallas_call(
        functools.partial(spectrum_kernel, n_y, n_z, zl),
        out_shape=jax.ShapeDtypeStruct((PARTS, n_y, strips, LH, rows // strips, tile), F32),
        in_specs=[pl.BlockSpec(memory_space=pl.ANY)] * len(operands),
        out_specs=pl.BlockSpec(memory_space=pl.ANY),
        scratch_shapes=[
            pltpu.VMEM(flat.shape, BF),
            pltpu.VMEM(x_rows.shape, BF),
            pltpu.VMEM((2, my_rows, 2 * y_rows.shape[3]), BF),
            pltpu.VMEM((2,) + y_back.shape[1:], BF),
            pltpu.VMEM(z_rows.shape, BF),
            pltpu.VMEM(z_back.shape, BF),
            pltpu.VMEM(weight.shape, BF),
            pltpu.VMEM((PARTS, n_y // 2, 2, rows, lanes), F32),
            pltpu.VMEM((PARTS, n_ring, rows, lanes), F32),
            pltpu.VMEM((PARTS, 2, reach, my_rows, tile), F32),
            pltpu.VMEM((PARTS, 2, reach, my_rows, tile), F32),
            pltpu.VMEM((PARTS, modes, part, tile), F32),
            pltpu.VMEM((PARTS, n_z, part, tile), F32),
            pltpu.VMEM((PARTS, n_z, part, tile), F32),
            pltpu.VMEM((PARTS, modes, part, tile), F32),
            pltpu.VMEM((PARTS, 2, reach, modes, part, tile), F32),
            pltpu.VMEM((PARTS, n_ring, strips, LH, rows // strips, tile), F32),
            pltpu.VMEM((PARTS, n_ring, strips, LH, rows // strips, tile), F32),
        ]
        + [pltpu.SemaphoreType.DMA((n,)) for n in sems],
        compiler_params=pltpu.CompilerParams(
            collective_id=0, has_side_effects=True, vmem_limit_bytes=62 * MIB
        ),
        name="spectrum",
    )(*operands)

    block = pl.BlockSpec((c, STRIP * zl, nx), lambda i: (0, i, 0))
    planes = planes.reshape(PARTS * n_y, strips, LH, rows // strips, tile)
    out = pl.pallas_call(
        functools.partial(field_kernel, zl),
        grid=(strips,),
        in_specs=[
            pl.BlockSpec((PARTS * n_y, 1) + planes.shape[2:], lambda i: (0, i, 0, 0, 0)),
            block,
            whole(bypass_weight.shape),
            whole(bias.shape),
            whole(th.shape),
            whole(tl.shape),
        ],
        out_specs=block,
        out_shape=jax.ShapeDtypeStruct(flat.shape, BF),
        scratch_shapes=[pltpu.VMEM((lanes, lanes), BF), pltpu.VMEM((lanes, nx), F32)],
        compiler_params=pltpu.CompilerParams(vmem_limit_bytes=62 * MIB),
        name="field",
    )(planes, flat, bypass_weight, bias, jnp.asarray(th), jnp.asarray(tl))
    return out.reshape(features.shape)


def solution(mesh):
    n_y, n_z = mesh.shape["py"], mesh.shape["pz"]

    def run(features, spectral_weight, bypass_weight, bias_vector):
        _, ny, nz, nx = features.shape
        _, mx, my, mz, _ = spectral_weight.shape
        tables = make_tables(nx, ny, nz, mx, my, mz, n_y, n_z)
        return jax.shard_map(
            functools.partial(per_device, tables, n_y, n_z),
            mesh=mesh,
            in_specs=(P(None, "py", "pz", None), P(None, "py", "pz", None, None), P(), P()),
            out_specs=P(None, "py", "pz", None),
            check_vma=False,
        )(features, spectral_weight, bypass_weight, bias_vector)

    return run
```

```python
import functools
import math

import jax
import jax.numpy as jnp
import ml_dtypes
import numpy as np
from jax import lax
from jax.experimental import pallas as pl
from jax.experimental.pallas import tpu as pltpu
from jax.sharding import PartitionSpec as P

MESH = pl.DeviceIdType.MESH
BF = jnp.bfloat16
F32 = jnp.float32
MIB = 1 << 20
PARTS = 2
STRIP = 4
LH = 2
GROUP = 4


def centred(count):
    index = np.arange(count)
    return np.where(index < count // 2, index, index - count)


def split(table, axis=0):
    high = table.astype(ml_dtypes.bfloat16)
    low = (table - high.astype(np.float64)).astype(ml_dtypes.bfloat16)
    return np.stack([high, low], axis)


def thrice(table):
    high, low = split(table)
    return np.concatenate([high, high, low], -1)


def pair(frequencies, positions, period, sign):
    angle = 2.0 * np.pi * ((positions[:, None] * frequencies[None, :]) % period) / period
    c, s = np.cos(angle), np.sin(angle)
    return np.stack([np.stack([c, sign * s]), np.stack([-sign * s, c])])


def make_tables(nx, ny, nz, mx, my, mz, py, pz):
    k = mx // py
    zl = nz // pz
    yl = ny // py
    norm = 1.0 / math.sqrt(nx * ny * nz)
    angle = 2.0 * np.pi * ((np.arange(mx)[:, None] * np.arange(nx)[None, :]) % nx) / nx
    kp = k // PARTS
    eye, pairs = np.eye(kp), np.eye(2)
    xf = np.stack([np.cos(angle) * norm, -np.sin(angle) * norm], 1)
    xf = xf.reshape(py, PARTS, kp, 2, nx).swapaxes(0, 1).reshape(2 * mx, nx)
    weight = np.where(np.arange(mx) == 0, 1.0, 2.0)[:, None] * norm
    xi = np.stack([np.cos(angle) * weight, -np.sin(angle) * weight], 1)
    xi = xi.reshape(py, PARTS, kp, 2, nx).swapaxes(0, 1).reshape(2 * mx, nx)
    order = np.arange(my).reshape(pz // GROUP, GROUP).T.reshape(-1)
    yf = pair(centred(my), np.arange(ny), ny, -1.0)[..., order].reshape(2, 2, py, yl, my)
    yf = np.einsum("pqdyj,kl,hg->djhkqgylp", yf, eye, pairs)
    yf = yf.reshape(py, my * 4 * kp, yl * 4 * kp)
    yi = pair(centred(my), np.arange(ny), ny, 1.0)[..., order].reshape(2, 2, py, yl, my)
    yi = yi.reshape(2, 2, py, yl // STRIP, STRIP, my)
    yi = np.einsum("qrdwyj,kl,hg->dwhykrjglq", yi, eye, pairs)
    yi = yi.reshape(py, yl * 4 * kp, my * 4 * kp)
    zf = pair(centred(mz), np.arange(nz), nz, -1.0).reshape(2, 2, pz, zl, mz)
    zf = np.einsum("pqszm->zqmps", zf).reshape(zl, 2 * mz, 2 * pz)
    zi = pair(centred(mz), np.arange(nz), nz, 1.0).reshape(2, 2, pz // GROUP, GROUP, zl, mz)
    zi = np.einsum("qrjgzm->gzrjqm", zi).reshape(GROUP, zl * 2 * pz // GROUP, 2 * mz)
    return xf, xi, yf, yi, zf, zi


def halves(value):
    high = value.astype(BF)
    return high, (value - high.astype(F32)).astype(BF)


def triple(value):
    high, low = halves(value)
    return jnp.concatenate([high, low, high], 0)


def dot(a, b, dims=((1,), (0,))):
    return lax.dot_general(a, b, (dims, ((), ())), preferred_element_type=F32)


def dot3(ah, al, bh, bl):
    return dot(ah, bh) + dot(al, bh) + dot(ah, bl)


def x_forward(zl, field, table, out, first, last):
    length = field.shape[2]
    parts, owners, two, _, lanes = out.shape

    def step(i, carry):
        block = field[:, pl.ds(pl.multiple_of(i * 2 * zl, 2 * zl), 2 * zl), :].astype(F32)
        planes = []
        for y in range(2):
            plane = block[:, y * zl : (y + 1) * zl, :].reshape(-1, length).astype(BF)
            both = dot(table[...], plane, ((1,), (1,)))
            half = both.shape[0] // 2
            planes.append((both[:half] + both[half:]).reshape(parts * owners, -1, lanes))
        first_y, second_y = planes
        rows = first_y.shape[1]
        upper = lax.broadcasted_iota(jnp.int32, (1, rows, 1), 1) < rows // 2
        turned = lambda v: pltpu.roll(v, rows // 2, 1)
        even = jnp.where(upper, first_y, turned(second_y))
        odd = jnp.where(upper, turned(first_y), second_y)
        at = pl.ds(pl.multiple_of(i * rows, rows), rows)
        for t in range(parts):
            out[t, :, 0, at, :] = even[t * owners : (t + 1) * owners]
            out[t, :, 1, at, :] = odd[t * owners : (t + 1) * owners]
        return carry

    lax.fori_loop(first, last, step, 0)


def mix_modes(zl, x, w, forward, t):
    cells, rows, tile = x.shape
    lanes = LH * tile
    kp = rows // (2 * LH)
    channels = lanes // zl
    row = lambda k, q: jnp.concatenate([x[:, (h * kp + k) * 2 + q, :] for h in range(LH)], axis=1)
    column = lambda k: jnp.concatenate([row(k, 0), row(k, 1)], axis=0)
    block = triple(jnp.concatenate([column(k) for k in range(kp)], axis=1))
    inner = lax.broadcasted_iota(jnp.int32, (1, kp * lanes), 1) % zl
    modes = jnp.zeros((forward.shape[1], kp * lanes), F32)
    for z in range(zl):
        modes += jnp.where(inner == z, dot(forward[z], block), 0.0)
    count = modes.shape[0] // 2
    modes = jnp.concatenate(
        [
            modes[p * count : (p + 1) * count, k * lanes : (k + 1) * lanes]
            for p in range(2)
            for k in range(kp)
        ],
        axis=0,
    )
    pairs = w.shape[2]
    lane = lax.broadcasted_iota(jnp.int32, (lanes, pairs), 0) // zl
    both = lax.broadcasted_iota(jnp.int32, (lanes, pairs), 1)
    spread = jnp.where(lane == both // channels, 1.0, 0.0).astype(BF)
    mh, ml = halves(modes)
    wide = dot(mh, spread) + dot(ml, spread)
    half = wide.shape[0] // 2
    re, im = wide[:half], wide[half:]
    wr = w[0, t * half : (t + 1) * half, :].astype(F32)
    wi = w[1, t * half : (t + 1) * half, :].astype(F32)
    mixed = jnp.concatenate([wr * re - wi * im, wr * im + wi * re], axis=0)
    both = lax.broadcasted_iota(jnp.int32, (pairs, lanes), 0)
    lane = lax.broadcasted_iota(jnp.int32, (pairs, lanes), 1) // zl
    gather = jnp.where(both % channels == lane, 1.0, 0.0).astype(BF)
    ph, plo = halves(mixed)
    summed = dot(ph, gather) + dot(plo, gather)
    part = lambda p, k: summed[(p * kp + k) * count : (p * kp + k + 1) * count]
    columns = [jnp.concatenate([part(0, k), part(1, k)], axis=0) for k in range(kp)]
    return triple(jnp.concatenate(columns, axis=1))


def bypass_rows(zl, w, bias):
    channels = w.shape[0]
    row = lax.broadcasted_iota(jnp.int32, (channels * zl, channels), 0) // zl
    pick = row == lax.broadcasted_iota(jnp.int32, (channels * zl, channels), 1)
    ones = jnp.where(pick, 1.0, 0.0).astype(BF)
    left = dot(ones, w[...], ((1,), (1,))).astype(BF)
    full = dot(left, ones, ((1,), (1,)))
    a = lax.broadcasted_iota(jnp.int32, full.shape, 0) % zl
    b = lax.broadcasted_iota(jnp.int32, full.shape, 1) % zl
    column = jnp.sum(jnp.where(pick, bias[...], 0.0), axis=1, keepdims=True)
    return jnp.where(a == b, full, 0.0).astype(BF), column


def spectrum_kernel(n_y, n_z, zl, *refs):
    (
        f_hbm, xt_hbm, yt_hbm, yi_hbm, zf_hbm, zi_hbm, w_hbm, r_hbm,
        f, xt, yt, yi, zf, zi, w, a, theirs, summing, arrived, total, seen,
        mixed, back, ring, leaving, keeping,
        load_sem, swap_s, swap_r, sum_s, sum_r, out_s, out_r, in_s, in_r, ring_s, ring_r,
        turn_s, turn_r, keep_s,
    ) = refs
    here, column = lax.axis_index("py"), lax.axis_index("pz")
    n_ring = n_y // 2
    side, z = here // n_ring, here % n_ring
    other = 1 - side
    half_py = lambda s, at: s * n_ring + at % n_ring
    partner = {"py": half_py(other, z)}
    neighbours = ({"py": half_py(side, z + 1)}, {"py": half_py(side, z + n_ring - 1)})

    barrier = pltpu.get_barrier_semaphore()
    for peer in (partner,) + neighbours:
        pl.semaphore_signal(barrier, inc=1, device_id=peer, device_id_type=MESH)

    def greet(step, carry):
        pl.semaphore_signal(
            barrier, inc=1, device_id={"pz": (column + step) % n_z}, device_id_type=MESH
        )
        return carry

    loads = []

    def load(source, target):
        copy = pltpu.make_async_copy(source, target, load_sem.at[len(loads)])
        copy.start()
        loads.append(copy)
        return copy

    pieces = 4
    rows = f.shape[1] // pieces
    table_x = load(xt_hbm, xt)
    fields = [
        load(f_hbm.at[:, pl.ds(i * rows, rows), :], f.at[:, pl.ds(i * rows, rows), :])
        for i in range(pieces)
    ]
    lax.fori_loop(1, n_z, greet, 0)

    reach = n_ring // 2
    offsets = [reach] + [o * s for o in range(reach - 1, 0, -1) for s in (1, -1)] + [0]

    def swap(h, i, s):
        at = (z + offsets[i] + n_ring) % n_ring
        half = theirs.shape[2] // 2
        index = (h * n_ring + i) * 2 + s
        return pltpu.make_async_remote_copy(
            src_ref=a.at[h, half_py(other, at) // 2, at % 2, pl.ds(s * half, half)],
            dst_ref=theirs.at[h, at, pl.ds(s * half, half)],
            send_sem=swap_s.at[index],
            recv_sem=swap_r.at[index],
            device_id=partner,
            device_id_type=MESH,
        )

    table_x.wait()
    turns = f.shape[1] // (2 * zl) // pieces
    early = 2
    for i in range(pieces):
        fields[i].wait()
        x_forward(zl, f, xt, a, i * turns, (i + 1) * turns)
        if i == pieces // 2 - 1:
            pl.semaphore_wait(barrier, n_z + 2)
            for j in range(early):
                swap(0, j, 0).start()
    for h in range(PARTS):
        for i in range(n_ring):
            for s in range(2):
                if h > 0 or i >= early or s > 0:
                    swap(h, i, s).start()
    depth = yt_hbm.shape[3]
    table_y = [
        load(yt_hbm.at[half_py(s, z)], yt.at[:, :, pl.ds(i * depth, depth)])
        for i, s in enumerate((side, other))
    ]
    table_z = [load(zf_hbm, zf), load(w_hbm, w), load(zi_hbm, zi)]
    table_i = [load(yi_hbm.at[half_py(s, z)], yi.at[i]) for i, s in enumerate((side, other))]
    for copy in table_y:
        copy.wait()

    def partial(h, i):
        at = (z + offsets[i] + n_ring) % n_ring
        for s in range(2):
            swap(h, i, s).wait_recv()
        rows = (a[h, half_py(side, at) // 2, at % 2], theirs[h, at])
        tile = summing.shape[4]
        block = jnp.concatenate(
            [r[:, i * tile : (i + 1) * tile] for r in rows for i in range(LH)], axis=0
        )
        high, low = halves(block)
        return dot3(yt[0], yt[1], high, low)

    part = total.shape[1] * total.shape[2] // GROUP
    span = lambda g: pl.ds(g * part, part)
    carries = lambda way, step, g: step > 0 or (g < GROUP // 2) == (way == 0)

    def hop(h, way, step, g):
        index = ((h * 2 + way) * reach + step) * GROUP + g
        return pltpu.make_async_remote_copy(
            src_ref=summing.at[h, way, step, span(g)],
            dst_ref=arrived.at[h, way, step, span(g)],
            send_sem=sum_s.at[index],
            recv_sem=sum_r.at[index],
            device_id=neighbours[way],
            device_id_type=MESH,
        )

    def set_out(h):
        block = partial(h, 0)
        for g in range(GROUP):
            way = 0 if g < GROUP // 2 else 1
            summing[h, way, 0, g * part : (g + 1) * part] = block[g * part : (g + 1) * part]
            hop(h, way, 0, g).start()

    def move_on(h, step):
        for way in range(2):
            summing[h, way, step] = partial(h, 2 * step - 1 + way)
        for g in range(GROUP):
            for way in range(2):
                if carries(way, step - 1, g):
                    hop(h, way, step - 1, g).wait_recv()
                    summing[h, way, step, span(g)] += arrived[h, way, step - 1, span(g)]
                hop(h, way, step, g).start()

    per = n_z // GROUP
    y_chip, place = column // GROUP, column % GROUP
    far_first = lambda i: (y_chip + per // 2 + (i + 1) // 2 * (1 - i % 2 * 2) + per) % per
    slot = place * per + y_chip

    def to_owner(h, source, owner, target):
        return pltpu.make_async_remote_copy(
            src_ref=total.at[h, source],
            dst_ref=seen.at[h, target],
            send_sem=out_s.at[h * n_z + owner],
            recv_sem=out_r.at[h * n_z + target],
            device_id={"pz": owner},
            device_id_type=MESH,
        )

    def arrive(h):
        last = partial(h, n_ring - 1)
        for g in range(GROUP):
            for way in range(2):
                hop(h, way, reach - 1, g).wait_recv()
            value = last[g * part : (g + 1) * part] + arrived[h, 0, reach - 1, span(g)]
            value = value + arrived[h, 1, reach - 1, span(g)]
            total[h, g * per : (g + 1) * per] = value.reshape((per,) + total.shape[2:])

            def send(i, carry):
                chip = far_first(i)
                owner = chip * GROUP + g

                @pl.when(owner != column)
                def _():
                    to_owner(h, g * per + chip, owner, column).start()

                return carry

            lax.fori_loop(0, per, send, 0)
        seen[h, column] = total[h, slot]

    def collect(h):
        def one(step, carry):
            peer = (column + step) % n_z
            to_owner(h, 0, peer, peer).wait()
            return carry

        lax.fori_loop(1, n_z, one, 0)

    def to_cells(h, source, peer, target, sender):
        return pltpu.make_async_remote_copy(
            src_ref=mixed.at[h, source],
            dst_ref=back.at[h, target],
            send_sem=in_s.at[h * n_z + peer],
            recv_sem=in_r.at[h * n_z + sender],
            device_id={"pz": peer},
            device_id_type=MESH,
        )

    tile = seen.shape[3]
    kp = seen.shape[2] // (2 * LH)
    lanes = LH * tile
    inner = lax.broadcasted_iota(jnp.int32, (1, kp * lanes), 1) % zl

    def mix_and_return(h):
        modes = mix_modes(zl, seen.at[h], w, zf, h)
        for g in range(GROUP):
            value = dot(zi[g], modes)
            size = 2 * per
            cells = jnp.zeros((size, modes.shape[1]), F32)
            for i in range(zl):
                cells += jnp.where(inner == i, value[i * size : (i + 1) * size], 0.0)
            for p in range(2):
                for k in range(kp):
                    for i in range(LH):
                        mixed[h, g * per : (g + 1) * per, (i * kp + k) * 2 + p, :] = cells[
                            p * per : (p + 1) * per,
                            k * lanes + i * tile : k * lanes + (i + 1) * tile,
                        ]

            def send_back(i, carry):
                chip = far_first(i)
                peer = chip * GROUP + g

                @pl.when(peer != column)
                def _():
                    to_cells(h, g * per + chip, peer, slot, column).start()

                return carry

            lax.fori_loop(0, per, send_back, 0)
        back[h, slot] = mixed[h, slot]

    def end_back(h):
        def one(step, carry):
            peer = (column + step) % n_z
            to_cells(h, 0, peer, 0, peer).wait()
            return carry

        lax.fori_loop(1, n_z, one, 0)

    wide = lambda g: pl.ds(g * per, per)
    passes = lambda way, step, g: step < reach - 1 or (g < GROUP // 2) == (way == 0)

    def relay(h, way, step, g):
        index = ((h * 2 + way) * reach + step) * GROUP + g
        source = back.at[h, wide(g)] if step == 0 else ring.at[h, way, step - 1, wide(g)]
        target = ring.at[h, 0 if step == reach - 1 else way, step, wide(g)]
        return pltpu.make_async_remote_copy(
            src_ref=source,
            dst_ref=target,
            send_sem=ring_s.at[index],
            recv_sem=ring_r.at[index],
            device_id=neighbours[way],
            device_id_type=MESH,
        )

    def turn(h, i, owner):
        return pltpu.make_async_remote_copy(
            src_ref=leaving.at[h, i],
            dst_ref=r_hbm.at[h, owner],
            send_sem=turn_s.at[h * n_ring + i],
            recv_sem=turn_r.at[h * n_ring + i],
            device_id=partner,
            device_id_type=MESH,
        )

    def keep(h, i, owner):
        return pltpu.make_async_copy(
            keeping.at[h, i], r_hbm.at[h, owner], keep_s.at[h * n_ring + i]
        )

    def spread(h, i, offset, block):
        owner = half_py(side, z + offset + n_ring)
        high, low = halves(block.reshape(-1, block.shape[2]))
        leaving[h, i] = dot3(yi[1, 0], yi[1, 1], high, low).reshape(leaving.shape[2:])
        turn(h, i, owner).start()
        keeping[h, i] = dot3(yi[0, 0], yi[0, 1], high, low).reshape(keeping.shape[2:])
        keep(h, i, owner).start()

    def send_own(h):
        for g in range(GROUP):
            for way in range(2):
                relay(h, way, 0, g).start()

    def pass_on(h, step):
        for g in range(GROUP):
            for way in range(2):
                if passes(way, step - 1, g):
                    relay(h, way, step - 1, g).wait_recv()
                if step < reach and passes(way, step, g):
                    relay(h, way, step, g).start()

    def spread_pair(h, step):
        if step == reach:
            spread(h, n_ring - 1, reach, ring[h, 0, reach - 1])
        else:
            for way in range(2):
                spread(h, 2 * step - 1 + way, step if way else -step, ring[h, way, step - 1])

    set_out(0)
    for step in range(1, reach):
        move_on(0, step)
    set_out(1)
    arrive(0)
    for step in range(1, reach - 1):
        move_on(1, step)
    for copy in table_z:
        copy.wait()
    collect(0)
    mix_and_return(0)
    move_on(1, reach - 1)
    arrive(1)
    for copy in table_i:
        copy.wait()
    end_back(0)
    send_own(0)
    spread(0, 0, 0, back[0])
    pass_on(0, 1)
    spread_pair(0, 1)
    collect(1)
    mix_and_return(1)
    for step in range(2, reach):
        pass_on(0, step)
        spread_pair(0, step)
    end_back(1)
    send_own(1)
    spread(1, 0, 0, back[1])
    pass_on(0, reach)
    spread_pair(0, reach)
    for step in range(1, reach + 1):
        pass_on(1, step)
        spread_pair(1, step)

    for h in range(PARTS):
        for i in range(n_ring):
            for s in range(2):
                swap(h, i, s).wait_send()
            keep(h, i, here).wait()
            turn(h, i, here).wait()
        for step in range(reach):
            for g in range(GROUP):
                for way in range(2):
                    if carries(way, step, g):
                        hop(h, way, step, g).wait_send()
                    if passes(way, step, g):
                        relay(h, way, step, g).wait_send()


def field_kernel(zl, r_ref, f_ref, w_ref, b_ref, th_ref, tl_ref, o_ref, mix, shift):
    @pl.when(pl.program_id(0) == 0)
    def _():
        rows_mix, rows_bias = bypass_rows(zl, w_ref, b_ref)
        mix[...] = rows_mix
        shift[...] = jnp.broadcast_to(rows_bias, shift.shape)

    block = f_ref[...].astype(F32)
    rows = r_ref.shape[3] * 2 // STRIP
    for pair in range(STRIP // 2):
        tiles = [
            r_ref[:, 0, h, pair * rows : (pair + 1) * rows, :].reshape(-1, r_ref.shape[4])
            for h in range(LH)
        ]
        high, low = halves(jnp.concatenate(tiles, axis=1).T)
        made = []
        for i in range(2):
            y = pair * 2 + i
            plane = block[:, y * zl : (y + 1) * zl, :].reshape(-1, block.shape[2]).astype(BF)
            value = dot(high, th_ref[i]) + dot(low, th_ref[i]) + dot(high, tl_ref[i])
            value = value + dot(mix[...], plane) + shift[...]
            made.append(jax.nn.gelu(value).reshape(block.shape[0], zl, block.shape[2]))
        at = slice(pair * 2 * zl, (pair + 1) * 2 * zl)
        o_ref[:, at, :] = jnp.concatenate(made, axis=1).astype(BF)


def whole(shape):
    return pl.BlockSpec(shape, lambda i: (0,) * len(shape))


def per_device(tables, n_y, n_z, features, spectral_weight, bypass_weight, bias_vector):
    xf, xi, yf, yi, zf, zi = tables
    c, yl, zl, nx = features.shape
    _, kl, _, mz, pairs = spectral_weight.shape
    lanes = c * zl
    tile = lanes // LH
    kp = kl // PARTS
    rows = yl * 2 * kp
    part = LH * 2 * kp
    flat = features.reshape(c, yl * zl, nx)
    x_rows = split(xf).reshape(-1, nx)
    y_rows, y_back = split(yf, 1), split(yi, 1)
    z_rows, z_back = thrice(zf), thrice(zi)
    pair_rows = np.einsum("ekx,yw->weykx", xi.reshape(PARTS * n_y, -1, nx), np.eye(2))
    th, tl = split(pair_rows.reshape(2, -1, nx))
    weight = spectral_weight.reshape(2, kl * mz, pairs)
    bias = bias_vector.reshape(1, c)
    my_rows = y_rows.shape[2]
    modes = my_rows // part
    n_ring = n_y // 2
    reach = n_ring // 2
    strips = yl // STRIP
    operands = [flat] + [jnp.asarray(t) for t in (x_rows, y_rows, y_back, z_rows, z_back)] + [weight]
    hops = PARTS * 2 * reach * GROUP
    turns = PARTS * n_ring
    sems = [16] + [turns * 2] * 2 + [hops] * 2 + [PARTS * n_z] * 4 + [hops] * 2 + [turns] * 3
    planes = pl.pallas_call(
        functools.partial(spectrum_kernel, n_y, n_z, zl),
        out_shape=jax.ShapeDtypeStruct((PARTS, n_y, strips, LH, rows // strips, tile), F32),
        in_specs=[pl.BlockSpec(memory_space=pl.ANY)] * len(operands),
        out_specs=pl.BlockSpec(memory_space=pl.ANY),
        scratch_shapes=[
            pltpu.VMEM(flat.shape, BF),
            pltpu.VMEM(x_rows.shape, BF),
            pltpu.VMEM((2, my_rows, 2 * y_rows.shape[3]), BF),
            pltpu.VMEM((2,) + y_back.shape[1:], BF),
            pltpu.VMEM(z_rows.shape, BF),
            pltpu.VMEM(z_back.shape, BF),
            pltpu.VMEM(weight.shape, BF),
            pltpu.VMEM((PARTS, n_y // 2, 2, rows, lanes), F32),
            pltpu.VMEM((PARTS, n_ring, rows, lanes), F32),
            pltpu.VMEM((PARTS, 2, reach, my_rows, tile), F32),
            pltpu.VMEM((PARTS, 2, reach, my_rows, tile), F32),
            pltpu.VMEM((PARTS, modes, part, tile), F32),
            pltpu.VMEM((PARTS, n_z, part, tile), F32),
            pltpu.VMEM((PARTS, n_z, part, tile), F32),
            pltpu.VMEM((PARTS, modes, part, tile), F32),
            pltpu.VMEM((PARTS, 2, reach, modes, part, tile), F32),
            pltpu.VMEM((PARTS, n_ring, strips, LH, rows // strips, tile), F32),
            pltpu.VMEM((PARTS, n_ring, strips, LH, rows // strips, tile), F32),
        ]
        + [pltpu.SemaphoreType.DMA((n,)) for n in sems],
        compiler_params=pltpu.CompilerParams(
            collective_id=0, has_side_effects=True, vmem_limit_bytes=62 * MIB
        ),
        name="spectrum",
    )(*operands)

    block = pl.BlockSpec((c, STRIP * zl, nx), lambda i: (0, i, 0))
    planes = planes.reshape(PARTS * n_y, strips, LH, rows // strips, tile)
    out = pl.pallas_call(
        functools.partial(field_kernel, zl),
        grid=(strips,),
        in_specs=[
            pl.BlockSpec((PARTS * n_y, 1) + planes.shape[2:], lambda i: (0, i, 0, 0, 0)),
            block,
            whole(bypass_weight.shape),
            whole(bias.shape),
            whole(th.shape),
            whole(tl.shape),
        ],
        out_specs=block,
        out_shape=jax.ShapeDtypeStruct(flat.shape, BF),
        scratch_shapes=[pltpu.VMEM((lanes, lanes), BF), pltpu.VMEM((lanes, nx), F32)],
        compiler_params=pltpu.CompilerParams(vmem_limit_bytes=62 * MIB),
        name="field",
    )(planes, flat, bypass_weight, bias, jnp.asarray(th), jnp.asarray(tl))
    return out.reshape(features.shape)


def solution(mesh):
    n_y, n_z = mesh.shape["py"], mesh.shape["pz"]

    def run(features, spectral_weight, bypass_weight, bias_vector):
        _, ny, nz, nx = features.shape
        _, mx, my, mz, _ = spectral_weight.shape
        tables = make_tables(nx, ny, nz, mx, my, mz, n_y, n_z)
        return jax.shard_map(
            functools.partial(per_device, tables, n_y, n_z),
            mesh=mesh,
            in_specs=(P(None, "py", "pz", None), P(None, "py", "pz", None, None), P(), P()),
            out_specs=P(None, "py", "pz", None),
            check_vma=False,
        )(features, spectral_weight, bypass_weight, bias_vector)

    return run
```
